32 devices in a mesh: dp: 32 (over z, y, x, core).
Axes of the slice: x: 2, y: 2, z: 4, core: 2. Of those that a mesh axis runs over, the one named last changes fastest.
Arguments:
- tokens: bfloat16 [32768, 768], P('dp'), may hold values from -6 to 6
- lengths: int32 [64, 5], P('dp'), may hold values from 0 to 509, as said below
- norm_gain: bfloat16 [768], P('dp'), may hold values from 0.5 to 1.5
- w_query: bfloat16 [768, 768], P('dp'), may hold values from -0.109375 to 0.109375
- w_key: bfloat16 [768, 768], P('dp'), may hold values from -0.109375 to 0.109375
- w_value: bfloat16 [768, 768], P('dp'), may hold values from -0.21875 to 0.21875
- w_out: bfloat16 [768, 768], P('dp'), may hold values from -0.625 to 0.625
- bias_table: bfloat16 [32, 12], replicated, may hold values from -4 to 4
- ffn_gain: bfloat16 [768], P('dp'), may hold values from 0.5 to 1.5
- w_in: bfloat16 [768, 3072], P('dp'), may hold values from -0.21875 to 0.21875
- w_ffn_out: bfloat16 [3072, 768], P('dp'), may hold values from -0.15625 to 0.15625
- cotangent: bfloat16 [32768, 768], P('dp'), may hold values from -6 to 6
Outputs:
- output: bfloat16 [32768, 768], P('dp')
- grad_tokens: float32 [32768, 768], P('dp')
- grad_norm_gain: float32 [768], P('dp')
- grad_query: float32 [768, 768], P('dp')
- grad_key: float32 [768, 768], P('dp')
- grad_value: float32 [768, 768], P('dp')
- grad_out: float32 [768, 768], P('dp')
- grad_bias_table: float32 [32, 12], replicated
- grad_ffn_gain: float32 [768], P('dp')
- grad_in: float32 [768, 3072], P('dp')
- grad_ffn_out: float32 [3072, 768], P('dp')
The draws below stay inside these ranges and needn't reach their ends.
Inputs may be any that keep to these rules, and one draw needn't show every extreme that they name: Column 0 of a row is its count of padding positions, which stand at the row's end; columns 1 to 4 are the lengths of its pairs in order, each 1 or more; a row's entries sum to 512. Some row has 24 padding positions and some row none; some row has a pair of 509 positions.
All inputs are finite; a program needn't handle non-finite values.
Results may differ from the reference program's by a relative error of at most 0.013.
The reference program's roundings to bfloat16 on the way count: a program that leaves them out, or rounds other values in their place, can miss the bound.
Values may be sent and summed in bfloat16 or wider, within the bound.
A program may use at most 192 MiB of HBM per device.

```python
import jax
import jax.numpy as jnp
from jax import lax

D = 768
H = 12
DH = 64
FF = 3072
NB = 32
SEQ = 512
NSEG = 4
PADMAX = 24
ROWS = 64
TOKENS = 32768


def draw_lengths(key, part):
    key = jax.random.fold_in(key, 11)
    pad_key, cut_key = jax.random.split(key)
    padding = jax.random.randint(pad_key, (ROWS,), 0, PADMAX + 1)
    padding = padding.at[0].set(PADMAX).at[1].set(0)
    row_keys = jax.random.split(cut_key, ROWS)

    def one_row(row_key, row_pad):
        picks = jax.random.permutation(row_key, SEQ - PADMAX - 1)[:NSEG - 1] + 1
        picks = jnp.sort(picks).astype(jnp.int32)
        bounds = jnp.concatenate([jnp.zeros((1,), jnp.int32), picks, (SEQ - row_pad).reshape(1).astype(jnp.int32)])
        return jnp.concatenate([row_pad.reshape(1).astype(jnp.int32), jnp.diff(bounds)])
    drawn = jax.vmap(one_row)(row_keys, padding).astype(jnp.int32)
    longest = jnp.concatenate([jnp.zeros((1,), jnp.int32), jnp.ones((NSEG - 1,), jnp.int32), jnp.full((1,), SEQ - NSEG + 1, jnp.int32)])
    return drawn.at[1].set(longest).astype(jnp.int32)


def raised(values, rng, source, target, blocks, factor):
    def block_of(dim):
        return (jnp.arange(values.shape[dim]) // (values.shape[dim] // blocks)).reshape((-1,) + (1,) * (values.ndim - 1 - dim))

    near = jax.random.permutation(rng, blocks)[block_of(target)]
    second = (block_of(target) + blocks // 2) % blocks
    return jnp.where((block_of(source) == near) | (block_of(source) == second), factor * values, values)


def block_levels(stream_key, shape, shards, smallest, top_value):
    loudness, own = 1.0, jax.random.fold_in(stream_key, 6)
    for dim, parts in shards:
        steps = jnp.exp(jax.random.uniform(jax.random.fold_in(own, dim), (parts,), jnp.float32, smallest / len(shards), top_value / len(shards)))
        loudness = loudness * jnp.repeat(steps, shape[dim] // parts).reshape([-1 if axis == dim else 1 for axis in range(len(shape))])
    return loudness


def bell_draw(own_key, shape, spread, bound, shards=(), kind=jnp.bfloat16):
    array = spread * jax.random.normal(own_key, shape, jnp.float32)
    if shards:
        array = array * block_levels(own_key, shape, shards, -0.22, 0.18)
    return jnp.clip(array, -bound, bound).astype(kind)


def heavy_noise(stream_key, extent, scale, reach, pieces, heavy, held_as=jnp.bfloat16):
    values = scale * jax.random.normal(stream_key, extent, jnp.float32)
    if pieces:
        values = values * block_levels(stream_key, extent, pieces, -0.22, 0.18)
    return jnp.clip(raised(values, jax.random.fold_in(stream_key, 3), *heavy), -reach, reach).astype(held_as)


def setup_inputs(seed: int = 0) -> dict:
    keys = jax.random.split(jax.random.key(seed), 13)
    tokens = heavy_noise(keys[0], (TOKENS, D), 1.0, 6.0, ((0, 32),), (0, 1, 32, 2.75))
    lengths = draw_lengths(jax.random.fold_in(keys[12], 71), 0)
    norm_gain = jnp.clip(1.0 + 0.1 * jax.random.normal(keys[2], (D,), jnp.float32), 0.5, 1.5).astype(jnp.bfloat16)
    w_query = bell_draw(keys[3], (D, D), (4 * D) ** -0.5, 0.109375, ((0, 32),))
    w_key = bell_draw(keys[4], (D, D), (4 * D) ** -0.5, 0.109375, ((0, 32),))
    w_value = bell_draw(keys[5], (D, D), D ** -0.5, 0.21875, ((0, 32),))
    w_out = bell_draw(keys[6], (D, D), (D // 8) ** -0.5, 0.625, ((0, 32),))
    bias_table = bell_draw(keys[7], (NB, H), 1.0, 4.0)
    ffn_gain = jnp.clip(1.0 + 0.1 * jax.random.normal(keys[8], (D,), jnp.float32), 0.5, 1.5).astype(jnp.bfloat16)
    w_in = bell_draw(keys[9], (D, FF), D ** -0.5, 0.21875, ((0, 32),))
    w_ffn_out = bell_draw(keys[10], (FF, D), (FF // 2) ** -0.5, 0.15625, ((0, 32),))
    cotangent = bell_draw(keys[11], (TOKENS, D), 1.0, 6.0, ((0, 32),))
    return dict(tokens=tokens, lengths=lengths, norm_gain=norm_gain, w_query=w_query, w_key=w_key, w_value=w_value, w_out=w_out, bias_table=bias_table, ffn_gain=ffn_gain, w_in=w_in, w_ffn_out=w_ffn_out, cotangent=cotangent)


EPSILON = 1e-06
CUTOFFS = (12, 16, 23, 32, 46, 64, 91)
PRECISE = lax.Precision.HIGHEST

@jax.custom_vjp
def low(v):
    return lax.optimization_barrier(v.astype(jnp.bfloat16)).astype(jnp.float32)

@jax.custom_vjp
def low_back(v):
    return v

def low_keep(v):
    return (low(v), None)

def low_pass(kept, grad):
    return (grad,)

def back_keep(v):
    return (v, None)

def back_low(kept, grad):
    return (low(grad),)
low.defvjp(low_keep, low_pass)
low_back.defvjp(back_keep, back_low)

def bucket_table(length, bucket_count):
    positions = jnp.arange(length, dtype=jnp.int32)
    offsets = positions[None, :] - positions[:, None]
    distance = jnp.abs(offsets)
    coarse = jnp.full_like(distance, 8)
    for cutoff in CUTOFFS:
        coarse = coarse + (distance >= cutoff).astype(jnp.int32)
    bucket = jnp.where(distance < 8, distance, coarse) + jnp.where(offsets > 0, 16, 0)
    return (bucket[:, :, None] == jnp.arange(bucket_count, dtype=jnp.int32)[None, None, :]).astype(jnp.float32)

def segment_ids(lengths, length):
    seg_ends = jnp.cumsum(lengths[:, 1:], axis=1)
    positions = jnp.arange(length, dtype=jnp.int32)
    return lax.optimization_barrier(jnp.sum((positions[None, :, None] >= seg_ends[:, None, :]).astype(jnp.int32), axis=2))

def rms_norm(values, gains):
    inv_rms = lax.rsqrt(lax.optimization_barrier(jnp.mean(values * values, axis=-1, keepdims=True)) + EPSILON)
    return values * inv_rms * gains

def matmul_hi(left, right):
    return jnp.dot(left, right, precision=PRECISE)

def reference(tokens, lengths, norm_gain, w_query, w_key, w_value, w_out, bias_table, ffn_gain, w_in, w_ffn_out, cotangent):
    seg_all = segment_ids(lengths, SEQ)
    onehot = bucket_table(SEQ, NB)

    def forward(inputs, gain_one, full_query, full_key, full_value, full_out, table, gain_two, full_in, full_ffn):
        normed_one = low(rms_norm(inputs, gain_one))
        query_proj = low_back(low(matmul_hi(normed_one, full_query))).reshape(-1, SEQ, H, DH)
        key_proj = low_back(low(matmul_hi(normed_one, full_key))).reshape(-1, SEQ, H, DH)
        value_proj = low_back(low(matmul_hi(normed_one, full_value))).reshape(-1, SEQ, H, DH)
        rel_bias = jnp.einsum('ijb,bh->hij', onehot, table, precision=PRECISE)

        def attend(row_items):
            query_row, key_row, value_row, seg_row = row_items
            raw_scores = jnp.einsum('ihd,jhd->hij', query_row, key_row, precision=PRECISE) + rel_bias
            raw_scores = low_back(raw_scores)
            same_seg = seg_row[:, None] == seg_row[None, :]
            scores = jnp.where(same_seg[None], raw_scores, -1e+30)
            row_peak = lax.optimization_barrier(jnp.max(scores, axis=2, keepdims=True))
            expo = jnp.exp(scores - row_peak)
            probabilities = expo / lax.optimization_barrier(jnp.sum(expo, axis=2, keepdims=True))
            return jnp.einsum('hij,jhd->ihd', low(probabilities), value_row, precision=PRECISE)
        attn_mix = lax.map(jax.checkpoint(attend), (query_proj, key_proj, value_proj, seg_all))
        attn_mix = low_back(low(attn_mix.reshape(-1, D)))
        residual = inputs + low_back(matmul_hi(attn_mix, full_out))
        normed_two = low(rms_norm(residual, gain_two))
        ffn_inner = low_back(matmul_hi(normed_two, full_in))
        ffn_act = low(jax.nn.gelu(ffn_inner, approximate=False))
        return residual + low_back(matmul_hi(ffn_act, full_ffn))
    primals = (tokens, norm_gain, w_query, w_key, w_value, w_out, bias_table, ffn_gain, w_in, w_ffn_out)
    primals = tuple((item.astype(jnp.float32) for item in primals))
    result, pull = jax.vjp(forward, *primals)
    grads = pull(cotangent.astype(jnp.float32))
    return (result.astype(jnp.bfloat16), grads[0], grads[1], grads[2], grads[3], grads[4], grads[5], grads[6], grads[7], grads[8], grads[9])
```

```python
from functools import partial

import jax
import jax.numpy as jnp
from jax import lax
from jax.sharding import PartitionSpec as P

from jax.experimental import pallas as pl
from jax.experimental.pallas import tpu as pltpu

D = 768
H = 12
DH = 64
NB = 32
SEQ = 512


EPSILON = 1e-06
CUTOFFS = (12, 16, 23, 32, 46, 64, 91)


def bucket_index(length):
    positions = jnp.arange(length, dtype=jnp.int32)
    offsets = positions[None, :] - positions[:, None]
    distance = jnp.abs(offsets)
    coarse = jnp.full_like(distance, 8)
    for cutoff in CUTOFFS:
        coarse = coarse + (distance >= cutoff).astype(jnp.int32)
    return jnp.where(distance < 8, distance, coarse) + jnp.where(offsets > 0, 16, 0)


def segment_ids(lengths, length):
    seg_ends = jnp.cumsum(lengths[:, 1:], axis=1)
    positions = jnp.arange(length, dtype=jnp.int32)
    return jnp.sum((positions[None, :, None] >= seg_ends[:, None, :]).astype(jnp.int32), axis=2)


def rms_norm(values, gains):
    inv_rms = lax.rsqrt(jnp.mean(values * values, axis=-1, keepdims=True) + EPSILON)
    return values * inv_rms * gains


def project(left, right):
    return jnp.dot(left, right, preferred_element_type=jnp.float32)


def project_back(left, right):
    return jnp.einsum("te,de->td", left, right, preferred_element_type=jnp.float32)


def weight_grad(left, right):
    return jnp.einsum("te,td->ed", left, right, preferred_element_type=jnp.float32)


MESH_ID = pl.DeviceIdType.MESH
RANKS = 32


def place():
    me = lax.axis_index("dp")
    group = lax.axis_size("dp") // RANKS
    rank, low = me // group, me % group
    digits = dict(z=rank // 8, y=(rank // 4) % 2, x=(rank // 2) % 2, c=rank % 2)

    def device(**changed):
        d = {**digits, **changed}
        return ((((d["z"] * 2 + d["y"]) * 2 + d["x"]) * 2 + d["c"]) * group + low,)

    return digits, device


def greet(digits, device):
    barrier = pltpu.get_barrier_semaphore()
    others = [device(z=(digits["z"] + step) % 4) for step in (1, 2, 3)]
    others += [device(**{axis: 1 - digits[axis]}) for axis in "yxc"]
    for other in others:
        pl.semaphore_signal(barrier, inc=1, device_id=other, device_id_type=MESH_ID)
    pl.semaphore_wait(barrier, len(others))


def send(source, target, send_sem, recv_sem, device_id):
    return pltpu.make_async_remote_copy(
        src_ref=source,
        dst_ref=target,
        send_sem=send_sem,
        recv_sem=recv_sem,
        device_id=device_id,
        device_id_type=MESH_ID,
    )


class Gather:
    COPIES = 10

    def __init__(self, block, full, own_sem, send_sems, recv_sems, order):
        self.block, self.full, self.own_sem = block, full, own_sem
        self.send_sems, self.recv_sems = send_sems, recv_sems
        self.first, self.second = order
        self.digits, self.device = place()
        self.started = []

    def part(self, **changed):
        d = {**self.digits, **changed}
        return self.full.at[:, d["y"], d["x"], d["c"]]

    def one(self, z, **changed):
        d = {**self.digits, **changed}
        return self.full.at[z, d["y"], d["x"], d["c"]]

    def go(self, slot, source, target, device_id):
        copy = send(source, target, self.send_sems.at[slot], self.recv_sems.at[slot], device_id)
        copy.start()
        self.started.append(copy)

    def arrived(self, slot, landing):
        send(landing, landing, self.send_sems.at[slot], self.recv_sems.at[slot], self.device(c=1 - self.digits["c"])).wait_recv()

    def start(self):
        z = self.digits["z"]
        own = pltpu.make_async_copy(self.block, self.one(z), self.own_sem)
        own.start()
        for step in (1, 2, 3):
            self.go(step - 1, self.block, self.one(z), self.device(z=(z + step) % 4))
        self.own = own

    def spread_line(self):
        z = self.digits["z"]
        self.own.wait()
        for step in (1, 2, 3):
            self.arrived(step - 1, self.one((z - step + 4) % 4))
        line = self.part()
        self.go(3, line, line, self.device(**{self.first: 1 - self.digits[self.first]}))
        self.go(4, line, line, self.device(**{self.second: 1 - self.digits[self.second]}))
        self.go(5, line, line, self.device(c=1 - self.digits["c"]))

    def spread_first(self):
        line = self.part(**{self.first: 1 - self.digits[self.first]})
        self.arrived(3, line)
        self.go(6, line, line, self.device(**{self.second: 1 - self.digits[self.second]}))
        self.go(7, line, line, self.device(c=1 - self.digits["c"]))

    def spread_second(self):
        other = {self.second: 1 - self.digits[self.second]}
        for slot, line in ((4, self.part(**other)), (6, self.part(**other, **{self.first: 1 - self.digits[self.first]}))):
            self.arrived(slot, line)
            self.go(slot + 4 - (slot == 6), line, line, self.device(c=1 - self.digits["c"]))

    def finish(self):
        c = 1 - self.digits["c"]
        a = {self.first: 1 - self.digits[self.first]}
        b = {self.second: 1 - self.digits[self.second]}
        for slot, line in ((5, self.part(c=c)), (7, self.part(c=c, **a)), (8, self.part(c=c, **b)), (9, self.part(c=c, **a, **b))):
            self.arrived(slot, line)
        for copy in self.started:
            copy.wait_send()


class Reduce:
    COPIES = 8

    def __init__(self, parts, from_core, from_first, from_second, from_line, send_sems, recv_sems, order):
        self.parts = parts
        self.from_core, self.from_first, self.from_second, self.from_line = from_core, from_first, from_second, from_line
        self.send_sems, self.recv_sems = send_sems, recv_sems
        self.first, self.second = order
        self.digits, self.device = place()
        self.started = []

    def at(self, z, first, second, c):
        d = {self.first: first, self.second: second}
        return (z, d["y"], d["x"], c)

    def go(self, slot, source, target, device_id):
        copy = send(source, target, self.send_sems.at[slot], self.recv_sems.at[slot], device_id)
        copy.start()
        self.started.append(copy)

    def arrived(self, slot, landing):
        send(landing, landing, self.send_sems.at[slot], self.recv_sems.at[slot], self.device(c=1 - self.digits["c"])).wait_recv()

    def add(self, place_of, received, count):
        def body(i, carry):
            index = place_of(i)
            total = self.parts[index].astype(jnp.float32) + received(i).astype(jnp.float32)
            self.parts[index] = total.astype(jnp.bfloat16)
            return carry

        lax.fori_loop(0, count, body, 0)

    def half(self, first, c):
        if self.first == "y":
            return self.parts.at[:, first, :, c]
        return self.parts.at[:, :, first, c]

    def start(self):
        d = self.digits
        c = 1 - d["c"]
        sibling = self.device(c=c)
        self.go(0, self.half(1 - d[self.first], c), self.from_core.at[0], sibling)
        self.go(1, self.half(d[self.first], c), self.from_core.at[1], sibling)

    def core_far(self):
        d = self.digits
        self.arrived(0, self.from_core.at[0])
        self.add(
            lambda i: self.at(i // 2, 1 - d[self.first], i % 2, d["c"]), lambda i: self.from_core[0, i // 2, i % 2], 8
        )
        self.go(2, self.half(1 - d[self.first], d["c"]), self.from_first, self.device(**{self.first: 1 - d[self.first]}))

    def core_near(self):
        d = self.digits
        self.arrived(1, self.from_core.at[1])
        self.add(lambda i: self.at(i // 2, d[self.first], i % 2, d["c"]), lambda i: self.from_core[1, i // 2, i % 2], 8)

    def first_axis(self):
        d = self.digits
        self.arrived(2, self.from_first)
        far = 1 - d[self.second]
        self.add(lambda i: self.at(i, d[self.first], far, d["c"]), lambda i: self.from_first[i, far], 4)
        q = {self.first: d[self.first], self.second: far}
        self.go(3, self.parts.at[:, q["y"], q["x"], d["c"]], self.from_second, self.device(**{self.second: far}))
        near = d[self.second]
        self.add(lambda i: self.at(i, d[self.first], near, d["c"]), lambda i: self.from_first[i, near], 4)

    def second_axis(self):
        d = self.digits
        self.arrived(3, self.from_second)
        self.add(lambda i: self.at(i, d[self.first], d[self.second], d["c"]), lambda i: self.from_second[i], 4)
        for step in (1, 2, 3):
            z = (d["z"] + step) % 4
            source = self.parts.at[z, d["y"], d["x"], d["c"]]
            self.go(3 + step, source, self.from_line.at[step - 1], self.device(z=z))

    def finish(self, out_ref):
        d = self.digits
        total = self.parts[d["z"], d["y"], d["x"], d["c"]].astype(jnp.float32)
        for step in (1, 2, 3):
            self.arrived(3 + step, self.from_line.at[step - 1])
            total = total + self.from_line[step - 1].astype(jnp.float32)
        out_ref[...] = total
        for copy in self.started:
            copy.wait_send()


ORDERS = ("xy", "yx")
ANY = pl.BlockSpec(memory_space=pl.ANY)
VMEM = pl.BlockSpec(memory_space=pltpu.VMEM)
FULL = (4, 2, 2, 2)


def halves(width):
    return ((0, width // 2), (width // 2, width))


def gather_kernel(count, *refs):
    blocks, fulls = refs[:count], refs[count : 2 * count]
    own_sems, send_sems, recv_sems = refs[2 * count :]
    digits, device = place()
    greet(digits, device)
    pieces = [
        Gather(blocks[i], fulls[i], own_sems.at[i], send_sems.at[i], recv_sems.at[i], ORDERS[i % 2]) for i in range(count)
    ]
    for stage in ("start", "spread_line", "spread_first", "spread_second", "finish"):
        for piece in pieces:
            getattr(piece, stage)()


def inner_groups():
    total = lax.axis_size("dp")
    group = total // RANKS
    return group, [list(range(i * group, (i + 1) * group)) for i in range(RANKS)]


def widen(block):
    group, groups = inner_groups()
    if group == 1:
        return block
    return lax.all_gather(block, "dp", axis=0, tiled=True, axis_index_groups=groups)


def narrow(block):
    group, groups = inner_groups()
    if group == 1:
        return block
    return lax.psum_scatter(block, "dp", scatter_dimension=0, tiled=True, axis_index_groups=groups)


def gather_weights(norm_gain, ffn_gain, attn_weights, w_in, w_ffn_out):
    gains = widen(jnp.stack([norm_gain, ffn_gain], axis=1))
    gain_rows = jnp.zeros((16, 128), jnp.bfloat16).at[: 2, : gains.shape[0]].set(gains.T)
    attn = widen(jnp.concatenate(attn_weights, axis=1))
    wide = widen(w_in)
    ffn = widen(w_ffn_out)
    blocks = [gain_rows, gain_rows]
    for block in (attn, wide, ffn):
        blocks += [block[:, lo:hi] for lo, hi in halves(block.shape[1])]
    blocks = blocks[1:]
    count = len(blocks)
    fulls = pl.pallas_call(
        partial(gather_kernel, count),
        out_shape=[jax.ShapeDtypeStruct(FULL + block.shape, block.dtype) for block in blocks],
        in_specs=[ANY] * count,
        out_specs=[ANY] * count,
        scratch_shapes=[
            pltpu.SemaphoreType.DMA((count,)),
            pltpu.SemaphoreType.DMA((count, Gather.COPIES)),
            pltpu.SemaphoreType.DMA((count, Gather.COPIES)),
        ],
        compiler_params=pltpu.CompilerParams(collective_id=1, has_side_effects=True),
    )(*blocks)
    gain_full = fulls[0].reshape(RANKS, 16, 128)[:, :2, : gains.shape[0]]
    gain_one, gain_two = gain_full[:, 0].reshape(-1), gain_full[:, 1].reshape(-1)
    whole = [jnp.concatenate([a.reshape(-1, a.shape[-1]), b.reshape(-1, b.shape[-1])], axis=1) for a, b in zip(fulls[1::2], fulls[2::2])]
    return gain_one, gain_two, *whole


def reduce_kernel(count, *refs):
    parts, small, outs, small_out = refs[:count], refs[count], refs[count + 1 : 2 * count + 1], refs[2 * count + 1]
    buffers = refs[2 * count + 2 : 6 * count + 2]
    small_buffer, send_sems, recv_sems, small_send, small_recv = refs[6 * count + 2 :]
    digits, device = place()
    greet(digits, device)
    pieces = [
        Reduce(parts[i], *buffers[4 * i : 4 * i + 4], send_sems.at[i], recv_sems.at[i], ORDERS[i % 2]) for i in range(count)
    ]
    for stage in ("start", "core_far", "core_near", "first_axis", "second_axis"):
        for piece in pieces:
            getattr(piece, stage)()
    small_sum(small, small_buffer, small_out, small_send, small_recv, digits, device)
    for piece, out in zip(pieces, outs):
        piece.finish(out)


def small_sum(values, buffer, out, send_sems, recv_sems, digits, device):
    out[...] = values[...]
    copies = []
    for slot, axis in enumerate("cxy"):
        buffer[2 * slot] = out[...]
        copy = send(
            buffer.at[2 * slot],
            buffer.at[2 * slot + 1],
            send_sems.at[slot],
            recv_sems.at[slot],
            device(**{axis: 1 - digits[axis]}),
        )
        copy.start()
        copies.append(copy)
        copy.wait_recv()
        out[...] = out[...] + buffer[2 * slot + 1]
    z = digits["z"]
    buffer[6 + z] = out[...]
    line = []
    for step in (1, 2, 3):
        mine = buffer.at[6 + z]
        copy = send(mine, mine, send_sems.at[2 + step], recv_sems.at[2 + step], device(z=(z + step) % 4))
        copy.start()
        line.append(copy)
    for step in (1, 2, 3):
        theirs = buffer.at[6 + (z - step + 4) % 4]
        send(theirs, theirs, send_sems.at[2 + step], recv_sems.at[2 + step], device(z=(z + step) % 4)).wait_recv()
    out[...] = (buffer[6] + buffer[7]) + (buffer[8] + buffer[9])
    for copy in copies + line:
        copy.wait_send()


def reduce_grads(attn, wide, ffn, gain_one, gain_two, table_sum):
    blocks = []
    for block in (attn, wide, ffn):
        blocks += [
            block[:, lo:hi].astype(jnp.bfloat16).reshape(FULL + (-1, hi - lo)) for lo, hi in halves(block.shape[1])
        ]
    count = len(blocks)
    small = jnp.concatenate([gain_one, gain_two, table_sum.reshape(-1)])
    pad = -small.shape[0] % 1024
    small = jnp.pad(small, (0, pad)).reshape(-1, 128)
    buffers = []
    for block in blocks:
        one = block.shape[4:]
        buffers += [
            pltpu.VMEM((2, 4, 2) + one, jnp.bfloat16),
            pltpu.VMEM((4, 2) + one, jnp.bfloat16),
            pltpu.VMEM((4,) + one, jnp.bfloat16),
            pltpu.VMEM((3,) + one, jnp.bfloat16),
        ]
    outs = pl.pallas_call(
        partial(reduce_kernel, count),
        out_shape=[jax.ShapeDtypeStruct(block.shape[4:], jnp.float32) for block in blocks]
        + [jax.ShapeDtypeStruct(small.shape, jnp.float32)],
        in_specs=[VMEM] * (count + 1),
        out_specs=[VMEM] * (count + 1),
        scratch_shapes=buffers
        + [
            pltpu.VMEM((10,) + small.shape, jnp.float32),
            pltpu.SemaphoreType.DMA((count, Reduce.COPIES)),
            pltpu.SemaphoreType.DMA((count, Reduce.COPIES)),
            pltpu.SemaphoreType.DMA((6,)),
            pltpu.SemaphoreType.DMA((6,)),
        ],
        compiler_params=pltpu.CompilerParams(collective_id=2, has_side_effects=True, vmem_limit_bytes=60 << 20),
    )(*blocks, small)
    sums = [narrow(jnp.concatenate(pair, axis=1)) for pair in zip(outs[0:count:2], outs[1:count:2])]
    flat = outs[count].reshape(-1)
    if inner_groups()[0] > 1:
        flat = lax.psum(flat, "dp", axis_index_groups=inner_groups()[1])
    each = D // lax.axis_size("dp")
    start = lax.axis_index("dp") * each
    gain_one_sum = lax.dynamic_slice(flat, (start,), (each,))
    gain_two_sum = lax.dynamic_slice(flat, (D + start,), (each,))
    table_total = flat[2 * D : 2 * D + NB * H].reshape(NB, H)
    return *sums, gain_one_sum, gain_two_sum, table_total


def per_device(
    tokens,
    lengths,
    norm_gain,
    w_query,
    w_key,
    w_value,
    w_out,
    bias_table,
    ffn_gain,
    w_in,
    w_ffn_out,
    cotangent,
):
    row_count = tokens.shape[0] // SEQ
    gain_one, gain_two, full_attn, full_in, full_ffn = gather_weights(
        norm_gain, ffn_gain, (w_query, w_key, w_value, w_out), w_in, w_ffn_out
    )
    full_query, full_key, full_value, full_out = jnp.split(full_attn, 4, axis=1)
    bucket = bucket_index(SEQ).reshape(1, SEQ * SEQ)
    onehot_flat = (bucket == jnp.arange(NB, dtype=jnp.int32)[:, None]).astype(jnp.bfloat16)
    rel_bias = jnp.dot(
        jnp.transpose(bias_table), onehot_flat, preferred_element_type=jnp.float32
    ).reshape(H, SEQ, SEQ)
    onehot = onehot_flat.reshape(NB, SEQ, SEQ)
    seg_all = segment_ids(lengths, SEQ)
    inputs = tokens.astype(jnp.float32)
    normed_one = rms_norm(inputs, gain_one.astype(jnp.float32)).astype(jnp.bfloat16)
    query_proj = project(normed_one, full_query).astype(jnp.bfloat16).reshape(row_count, SEQ, H, DH)
    key_proj = project(normed_one, full_key).astype(jnp.bfloat16).reshape(row_count, SEQ, H, DH)
    value_proj = project(normed_one, full_value).astype(jnp.bfloat16).reshape(row_count, SEQ, H, DH)

    def scores_of(query_row, key_row, seg_row):
        raw_scores = (
            jnp.einsum("ihd,jhd->hij", query_row, key_row, preferred_element_type=jnp.float32)
            + rel_bias
        )
        same_seg = seg_row[:, None] == seg_row[None, :]
        return jnp.where(same_seg[None], raw_scores, -1e30)

    def attend(row_items):
        query_row, key_row, value_row, seg_row = row_items
        scores = scores_of(query_row, key_row, seg_row)
        row_peak = jnp.max(scores, axis=2, keepdims=True)
        log_total = row_peak + jnp.log(jnp.sum(jnp.exp(scores - row_peak), axis=2, keepdims=True))
        probs_low = jnp.exp(scores - log_total).astype(jnp.bfloat16)
        attn_row = jnp.einsum(
            "hij,jhd->ihd", probs_low, value_row, preferred_element_type=jnp.float32
        )
        return (attn_row.astype(jnp.bfloat16), log_total)

    attn_mix, log_totals = lax.map(attend, (query_proj, key_proj, value_proj, seg_all))
    attn_mix = attn_mix.reshape(-1, D)
    residual = inputs + project(attn_mix, full_out)
    normed_two = rms_norm(residual, gain_two.astype(jnp.float32)).astype(jnp.bfloat16)
    ffn_inner = project(normed_two, full_in)
    ffn_act = jax.nn.gelu(ffn_inner, approximate=False).astype(jnp.bfloat16)
    output = (residual + project(ffn_act, full_ffn)).astype(jnp.bfloat16)
    grad_output = cotangent.astype(jnp.float32)
    grad_ffn = weight_grad(ffn_act, cotangent)
    grad_act = project_back(cotangent, full_ffn)
    gelu_value, gelu_pull = jax.vjp(partial(jax.nn.gelu, approximate=False), ffn_inner)
    grad_inner = gelu_pull(grad_act)[0].astype(jnp.bfloat16)
    grad_wide = weight_grad(normed_two, grad_inner)
    grad_normed_two = project_back(grad_inner, full_in)
    norm_value, norm_pull = jax.vjp(rms_norm, residual, gain_two.astype(jnp.float32))
    grad_res_norm, grad_gain_two = norm_pull(grad_normed_two)
    grad_residual = grad_output + grad_res_norm
    grad_attn = grad_residual.astype(jnp.bfloat16)
    grad_proj_out = weight_grad(attn_mix, grad_attn)
    grad_mix = project_back(grad_attn, full_out).astype(jnp.bfloat16).reshape(row_count, SEQ, H, DH)

    def attend_back(table_sum, row_items):
        query_row, key_row, value_row, seg_row, log_total, grad_row = row_items
        scores = scores_of(query_row, key_row, seg_row)
        probabilities = jnp.exp(scores - log_total)
        grad_values = jnp.einsum(
            "hij,ihd->jhd",
            probabilities.astype(jnp.bfloat16),
            grad_row,
            preferred_element_type=jnp.float32,
        )
        grad_probs = jnp.einsum(
            "ihd,jhd->hij", grad_row, value_row, preferred_element_type=jnp.float32
        )
        inner_sum = jnp.sum(probabilities * grad_probs, axis=2, keepdims=True)
        grad_scores = (probabilities * (grad_probs - inner_sum)).astype(jnp.bfloat16)
        grad_queries = jnp.einsum(
            "hij,jhd->ihd", grad_scores, key_row, preferred_element_type=jnp.float32
        )
        grad_keys = jnp.einsum(
            "hij,ihd->jhd", grad_scores, query_row, preferred_element_type=jnp.float32
        )
        table_sum = table_sum + jnp.einsum(
            "hij,bij->bh", grad_scores, onehot, preferred_element_type=jnp.float32
        )
        return (
            table_sum,
            (
                grad_queries.astype(jnp.bfloat16),
                grad_keys.astype(jnp.bfloat16),
                grad_values.astype(jnp.bfloat16),
            ),
        )

    table_start = jnp.zeros((NB, H), jnp.float32)
    table_sum, grad_heads = lax.scan(
        attend_back, table_start, (query_proj, key_proj, value_proj, seg_all, log_totals, grad_mix)
    )
    grad_queries = grad_heads[0].reshape(-1, D)
    grad_keys = grad_heads[1].reshape(-1, D)
    grad_values = grad_heads[2].reshape(-1, D)
    grad_proj_query = weight_grad(normed_one, grad_queries)
    grad_proj_key = weight_grad(normed_one, grad_keys)
    grad_proj_value = weight_grad(normed_one, grad_values)
    grad_normed_one = (
        project_back(grad_queries, full_query)
        + project_back(grad_keys, full_key)
        + project_back(grad_values, full_value)
    )
    first_value, first_pull = jax.vjp(rms_norm, inputs, gain_one.astype(jnp.float32))
    grad_in_norm, grad_gain_one = first_pull(grad_normed_one)
    grad_tokens = grad_residual + grad_in_norm
    grad_attn_weights = jnp.concatenate([grad_proj_query, grad_proj_key, grad_proj_value, grad_proj_out], axis=1)
    sums = reduce_grads(grad_attn_weights, grad_wide, grad_ffn, grad_gain_one, grad_gain_two, table_sum)
    attn_sum, wide_sum, ffn_sum, gain_one_sum, gain_two_sum, table_total = sums
    return (
        output,
        grad_tokens,
        gain_one_sum,
        *jnp.split(attn_sum, 4, axis=1),
        table_total,
        gain_two_sum,
        wide_sum,
        ffn_sum,
    )


def solution(mesh):
    return jax.shard_map(
        per_device,
        mesh=mesh,
        in_specs=(
            P("dp", None),
            P("dp", None),
            P("dp"),
            P("dp", None),
            P("dp", None),
            P("dp", None),
            P("dp", None),
            P(),
            P("dp"),
            P("dp", None),
            P("dp", None),
            P("dp", None),
        ),
        out_specs=(
            P("dp", None),
            P("dp", None),
            P("dp"),
            P("dp", None),
            P("dp", None),
            P("dp", None),
            P("dp", None),
            P(),
            P("dp"),
            P("dp", None),
            P("dp", None),
        ),
        check_vma=False,
    )
```

```python
from functools import partial
from jax.sharding import PartitionSpec as P
import jax
import jax.numpy as jnp
from jax import lax
from jax.experimental import pallas as pl
from jax.experimental.pallas import tpu as pltpu

D = 768
H = 12
DH = 64
NB = 32
SEQ = 512
FF = 3072
PAIRS = 6
EPSILON = 1e-6
CUTOFFS = (12, 16, 23, 32, 46, 64, 91)
VMEM = pl.BlockSpec(memory_space=pltpu.VMEM)
SMEM = pl.BlockSpec(memory_space=pltpu.SMEM)
f32, bf16 = jnp.float32, jnp.bfloat16

def nt(a, b):
    return lax.dot_general(a, b, (((1,), (1,)), ((), ())), preferred_element_type=f32)

def nn(a, b):
    return jnp.dot(a, b, preferred_element_type=f32)

def bucket_of(offsets):
    distance = jnp.abs(offsets)
    coarse = jnp.full_like(distance, 8)
    for cutoff in CUTOFFS:
        coarse = coarse + (distance >= cutoff).astype(jnp.int32)
    return jnp.where(distance < 8, distance, coarse) + jnp.where(offsets > 0, 16, 0)

def strip_onehot():
    d = jnp.arange(-1, 2, dtype=jnp.int32)[:, None, None] * 128
    jj = jnp.arange(128, dtype=jnp.int32)
    off = d + jj[None, :, None] - jj[None, None, :]
    return (bucket_of(off).reshape(1, -1) == jnp.arange(NB, dtype=jnp.int32)[:, None])

def bias_strips(table):
    oh = strip_onehot().astype(bf16)
    return jnp.dot(table.T, oh, preferred_element_type=f32).reshape(H, 3, 128, 128)

def seg_marks(lengths):
    ends = jnp.cumsum(lengths[:, 1:], axis=1)
    pos = jnp.arange(SEQ, dtype=jnp.int32)
    seg = jnp.sum((pos[None, :, None] >= ends[:, None, :]).astype(jnp.int32), axis=2)
    one = seg.reshape(-1)[:, None] == jnp.arange(128, dtype=jnp.int32)[None, :]
    keep = jnp.arange(128)[None, :] < 5
    return one.astype(bf16), jnp.where(one | ~keep, 0.0, -1e30).astype(bf16)

def lane_mask(h):
    lane = lax.broadcasted_iota(jnp.int32, (1, 128), 1)
    return lane < 64 if h == 0 else lane >= 64

def scores_t(km, qm, strips, far, head, ib):
    s = nt(km, qm)
    lo, hi = far[head, 0], far[head, 1]
    rows = []
    for bj in range(4):
        blocks = []
        for bi in (2 * ib, 2 * ib + 1):
            d = bj - bi
            b = s[128 * bj:128 * (bj + 1), 128 * (bi - 2 * ib):128 * (bi - 2 * ib + 1)]
            if d <= -2: b = b + lo
            elif d >= 2: b = b + hi
            else: b = b + strips[head, d + 1]
            blocks.append(b)
        rows.append(jnp.concatenate(blocks, axis=1))
    return jnp.concatenate(rows, axis=0)

def attn_fwd_pair(q, k, v, km_marks, qm_marks, strips, far, mix, lse, row, hp):
    rows = pl.ds(pl.multiple_of(row * 512, 512), 512)
    cols = pl.ds(pl.multiple_of(hp * 128, 128), 128)
    q2, k2 = q[rows, cols], k[rows, cols]
    v2t = v[rows, cols].T
    kmk, qmk = km_marks[rows, :], qm_marks[rows, :]
    outs = []
    for h in range(2):
        head = hp * 2 + h
        km = jnp.concatenate([jnp.where(lane_mask(h), k2, 0), kmk], axis=1)
        for ib in range(2):
            sl = slice(256 * ib, 256 * ib + 256)
            qm = jnp.concatenate([q2[sl], qmk[sl]], axis=1)
            s = scores_t(km, qm, strips, far, head, ib)
            m = jnp.max(s, axis=0, keepdims=True)
            e = jnp.exp(s - m)
            l = jnp.sum(e, axis=0, keepdims=True)
            p = (e * (1.0 / l)).astype(bf16)
            lse[row, pl.ds(head, 1), sl] = m + jnp.log(l)
            outs.append(nn(v2t[64 * h:64 * h + 64], p))
    o0 = jnp.concatenate(outs[:2], axis=1)
    o1 = jnp.concatenate(outs[2:], axis=1)
    mix[rows, cols] = jnp.concatenate([o0, o1], axis=0).T.astype(bf16)

def inv_rms(x):
    return lax.rsqrt(jnp.mean(x * x, axis=-1, keepdims=True) + EPSILON)

def attn_fwd_kernel(tokens, gain, wqkv, wo, gain2, km_marks, qm_marks, strips, far, n1, q, k, v, mix, lse, resid, n2):
    def proj(c, _):
        rows = pl.ds(pl.multiple_of(c * 256, 256), 256)
        x = tokens[rows, :].astype(f32)
        n = (x * inv_rms(x) * gain[...]).astype(bf16)
        n1[rows, :] = n
        for i, o in enumerate((q, k, v)):
            o[rows, :] = nn(n, wqkv[:, i * D:(i + 1) * D]).astype(bf16)
        return 0
    lax.fori_loop(0, 4, proj, 0)
    def body(i, _):
        attn_fwd_pair(q, k, v, km_marks, qm_marks, strips, far, mix, lse, i // PAIRS, i % PAIRS)
        return 0
    lax.fori_loop(0, 2 * PAIRS, body, 0)
    def out(c, _):
        rows = pl.ds(pl.multiple_of(c * 256, 256), 256)
        r = tokens[rows, :].astype(f32) + nn(mix[rows, :], wo[...])
        resid[rows, :] = r
        n2[rows, :] = (r * inv_rms(r) * gain2[...]).astype(bf16)
        return 0
    lax.fori_loop(0, 4, out, 0)

def sds(*shape, dtype=bf16):
    return jax.ShapeDtypeStruct(shape, dtype)

def attn_fwd(tokens, gain, wqkv, wo, gain2, km_marks, qm_marks, strips, far):
    T = tokens.shape[0]
    return pl.pallas_call(attn_fwd_kernel,
        out_shape=[sds(T, D), sds(T, D), sds(T, D), sds(T, D), sds(T, D), sds(T // SEQ, H, SEQ, dtype=f32), sds(T, D, dtype=f32), sds(T, D)],
        in_specs=[VMEM] * 8 + [SMEM], out_specs=[VMEM] * 8,
        compiler_params=pltpu.CompilerParams(vmem_limit_bytes=60 << 20),
    )(tokens, gain.reshape(1, D).astype(f32), wqkv, wo, gain2.reshape(1, D).astype(f32), km_marks, qm_marks, strips, far)

R2 = 0.7071067811865476
PHI = 0.3989422804014327

def gelu_pair(x):
    cdf = 0.5 + 0.5 * lax.erf(x * R2)
    return x * cdf, cdf + x * (jnp.exp(x * x * -0.5) * PHI)

def gelu_pair_as(x):
    z = jnp.abs(x) * R2
    t = 1.0 / (1.0 + 0.3275911 * z)
    e = jnp.exp(-(z * z))
    poly = t * (0.254829592 + t * (-0.284496736 + t * (1.421413741 + t * (-1.453152027 + t * 1.061405429))))
    tail = 0.5 * poly * e
    cdf = jnp.where(x < 0, tail, 1.0 - tail)
    return x * cdf, cdf + x * (e * PHI)

FT = 512
GELU = gelu_pair
def ffn_kernel(n2, cot, resid, gain2, win, wff, out, gres, gn2sum, gin, gff, n2t, cott, oacc, gacc, act, ginn):
    T = n2.shape[0]
    C = 256
    for c in range(T // C):
        rows = slice(c * C, c * C + C)
        n2t[:, rows] = n2[rows, :].T
        cott[:, rows] = cot[rows, :].T
    def tile(t, _):
        cols = pl.ds(pl.multiple_of(t * FT, FT), FT)
        wi = win.at[:, cols]
        wf = wff.at[cols, :]
        def chunk(c, _):
            rows = pl.ds(pl.multiple_of(c * C, C), C)
            inner = nn(n2[rows, :], wi[...])
            ga = nt(cot[rows, :], wf[...])
            a, dg = GELU(inner)
            a = a.astype(bf16)
            g = (dg * ga).astype(bf16)
            act[rows, :] = a
            ginn[rows, :] = g
            o = nn(a, wf[...])
            gn = nt(g, wi[...])
            @pl.when(t == 0)
            def _():
                oacc[rows, :] = resid[rows, :] + o
                gacc[rows, :] = gn
            @pl.when(t > 0)
            def _():
                oacc[rows, :] += o
                gacc[rows, :] += gn
            return 0
        lax.fori_loop(0, T // C, chunk, 0)
        gin[:, cols] = nn(n2t[...], ginn[...]).astype(bf16)
        gff[cols, :] = nn(cott[...], act[...]).astype(bf16).T
        return 0
    lax.fori_loop(0, FF // FT, tile, 0)
    gn2sum[...] = jnp.zeros((1, D), f32)
    def fin(c, _):
        rows = pl.ds(pl.multiple_of(c * C, C), C)
        out[rows, :] = oacc[rows, :].astype(bf16)
        r = resid[rows, :]
        s = inv_rms(r)
        gn = gacc[rows, :]
        gn2sum[...] += jnp.sum(gn * r * s, axis=0, keepdims=True)
        gg = gn * gain2[...]
        gres[rows, :] = cot[rows, :].astype(f32) + s * gg - r * (s * s * s * jnp.mean(gg * r, axis=-1, keepdims=True))
        return 0
    lax.fori_loop(0, T // C, fin, 0)

def ffn(n2, cot, resid, gain2, win, wff):
    T = n2.shape[0]
    return pl.pallas_call(ffn_kernel,
        out_shape=[sds(T, D), sds(T, D, dtype=f32), sds(1, D, dtype=f32), sds(D, FF), sds(FF, D)],
        in_specs=[VMEM] * 6, out_specs=[VMEM] * 5,
        scratch_shapes=[pltpu.VMEM((D, T), bf16), pltpu.VMEM((D, T), bf16), pltpu.VMEM((T, D), f32), pltpu.VMEM((T, D), f32),
                        pltpu.VMEM((T, FT), bf16), pltpu.VMEM((T, FT), bf16)],
        compiler_params=pltpu.CompilerParams(vmem_limit_bytes=60 << 20),
    )(n2, cot, resid, gain2.reshape(1, D).astype(f32), win, wff)

def attn_bwd_pair(q, k, v, gmix, km_marks, qm_marks, strips, far, lse, dq, dk, dv, tacc, facc, row, hp):
    rows = pl.ds(pl.multiple_of(row * 512, 512), 512)
    cols = pl.ds(pl.multiple_of(hp * 128, 128), 128)
    q2, k2, v2, g2 = q[rows, cols], k[rows, cols], v[rows, cols], gmix[rows, cols]
    k2t = k2.T
    kmk, qmk = km_marks[rows, :], qm_marks[rows, :]
    dvs, dks, dqs = None, None, []
    for h in range(2):
        head = hp * 2 + h
        msk = lane_mask(h)
        km = jnp.concatenate([jnp.where(msk, k2, 0), kmk], axis=1)
        vm = jnp.where(msk, v2, 0)
        qh = jnp.where(msk, q2, 0)
        gh = jnp.where(msk, g2, 0)
        for ib in range(2):
            sl = slice(256 * ib, 256 * ib + 256)
            qm = jnp.concatenate([q2[sl], qmk[sl]], axis=1)
            s = scores_t(km, qm, strips, far, head, ib)
            p = jnp.exp(s - lse[row, pl.ds(head, 1), sl])
            dp = nt(vm, g2[sl])
            dsum = jnp.sum(p * dp, axis=0, keepdims=True)
            ds = p * (dp - dsum)
            dsl = ds.astype(bf16)
            dv1 = nn(p.astype(bf16), gh[sl])
            dk1 = nn(dsl, qh[sl])
            dvs = dv1 if dvs is None else dvs + dv1
            dks = dk1 if dks is None else dks + dk1
            dqs.append(nn(k2t[64 * h:64 * h + 64], dsl))
            for bi in (2 * ib, 2 * ib + 1):
                los, his = [], []
                for bj in range(4):
                    d = bj - bi
                    b = ds[128 * bj:128 * (bj + 1), 128 * (bi - 2 * ib):128 * (bi - 2 * ib + 1)]
                    if abs(d) <= 1: tacc[head, d + 1] += b
                    else: (los if d < 0 else his).append(jnp.sum(b.reshape(16, 8, 128), axis=0))
                for lst, idx in ((los, 0), (his, 1)):
                    if lst: facc[head, idx] += sum(lst[1:], lst[0])
    dv[rows, cols] = dvs.astype(bf16)
    dk[rows, cols] = dks.astype(bf16)
    dqt = jnp.concatenate([jnp.concatenate(dqs[:2], axis=1), jnp.concatenate(dqs[2:], axis=1)], axis=0)
    dq[rows, cols] = dqt.T.astype(bf16)

def attn_bwd_kernel(tokens, gain, n1, wqkv, wo, mix, q, k, v, gres, km_marks, qm_marks, strips, lse, far,
                    gtok, gn1sum, gattn, gout, tacc, facc, n1t, ga, gmix, dq, dk, dv):
    T = tokens.shape[0]
    C = 256
    tacc[...] = jnp.zeros(tacc.shape, f32)
    facc[...] = jnp.zeros(facc.shape, f32)
    def pre(c, _):
        rows = pl.ds(pl.multiple_of(c * C, C), C)
        g = gres[rows, :].astype(bf16)
        ga[rows, :] = g
        gmix[rows, :] = nt(g, wo[...]).astype(bf16)
        n1t[:, rows] = n1[rows, :].T
        return 0
    lax.fori_loop(0, T // C, pre, 0)
    def wout(c, _):
        cols = pl.ds(pl.multiple_of(c * C, C), C)
        gout[cols, :] = nn(mix[:, cols].T, ga[...]).astype(bf16)
        return 0
    lax.fori_loop(0, D // C, wout, 0)
    def body(hp, _):
        for row in range(T // SEQ):
            attn_bwd_pair(q, k, v, gmix, km_marks, qm_marks, strips, far, lse, dq, dk, dv, tacc, facc, row, hp)
        cols = pl.ds(pl.multiple_of(hp * 128, 128), 128)
        for i, dd in enumerate((dq, dk, dv)):
            gattn[i, :, cols] = nn(n1t[...], dd[:, cols]).astype(bf16)
        return 0
    lax.fori_loop(0, PAIRS, body, 0)
    gn1sum[...] = jnp.zeros((1, D), f32)
    def fin(c, _):
        rows = pl.ds(pl.multiple_of(c * C, C), C)
        gn = nt(dq[rows, :], wqkv[:, :D]) + nt(dk[rows, :], wqkv[:, D:2 * D]) + nt(dv[rows, :], wqkv[:, 2 * D:])
        r = tokens[rows, :].astype(f32)
        s = inv_rms(r)
        gn1sum[...] += jnp.sum(gn * r * s, axis=0, keepdims=True)
        gg = gn * gain[...]
        gtok[rows, :] = gres[rows, :] + s * gg - r * (s * s * s * jnp.mean(gg * r, axis=-1, keepdims=True))
        return 0
    lax.fori_loop(0, T // C, fin, 0)

def attn_bwd(tokens, gain, n1, wqkv, wo, mix, q, k, v, gres, km_marks, qm_marks, strips, lse, far):
    T = tokens.shape[0]
    return pl.pallas_call(attn_bwd_kernel,
        out_shape=[sds(T, D, dtype=f32), sds(1, D, dtype=f32), sds(3, D, D), sds(D, D), sds(H, 3, 128, 128, dtype=f32), sds(H, 2, 8, 128, dtype=f32)],
        in_specs=[VMEM] * 14 + [SMEM], out_specs=[VMEM] * 6,
        scratch_shapes=[pltpu.VMEM((D, T), bf16)] + [pltpu.VMEM((T, D), bf16)] * 5,
        compiler_params=pltpu.CompilerParams(vmem_limit_bytes=60 << 20),
    )(tokens, gain.reshape(1, D).astype(f32), n1, wqkv, wo, mix, q, k, v, gres, km_marks, qm_marks, strips, lse, far)

def table_grad(tacc, facc):
    oh = strip_onehot().astype(f32)
    g = jnp.dot(oh, tacc.reshape(H, -1).T, precision=lax.Precision.HIGHEST)
    far = jnp.sum(facc, axis=(2, 3))
    return g.at[15].add(far[:, 0]).at[31].add(far[:, 1])
MESH_ID = pl.DeviceIdType.MESH
RANKS = 32


def place():
    me = lax.axis_index("dp")
    group = lax.axis_size("dp") // RANKS
    rank, low = me // group, me % group
    digits = dict(z=rank // 8, y=(rank // 4) % 2, x=(rank // 2) % 2, c=rank % 2)

    def device(**changed):
        d = {**digits, **changed}
        return ((((d["z"] * 2 + d["y"]) * 2 + d["x"]) * 2 + d["c"]) * group + low,)

    return digits, device


def greet(digits, device):
    barrier = pltpu.get_barrier_semaphore()
    others = [device(z=(digits["z"] + step) % 4) for step in (1, 2, 3)]
    others += [device(**{axis: 1 - digits[axis]}) for axis in "yxc"]
    for other in others:
        pl.semaphore_signal(barrier, inc=1, device_id=other, device_id_type=MESH_ID)
    pl.semaphore_wait(barrier, len(others))


def send(source, target, send_sem, recv_sem, device_id):
    return pltpu.make_async_remote_copy(
        src_ref=source,
        dst_ref=target,
        send_sem=send_sem,
        recv_sem=recv_sem,
        device_id=device_id,
        device_id_type=MESH_ID,
    )


class Gather:
    COPIES = 10

    def __init__(self, block, full, own_sem, send_sems, recv_sems, order):
        self.block, self.full, self.own_sem = block, full, own_sem
        self.send_sems, self.recv_sems = send_sems, recv_sems
        self.first, self.second = order
        self.digits, self.device = place()
        self.started = []

    def part(self, **changed):
        d = {**self.digits, **changed}
        return self.full.at[:, d["y"], d["x"], d["c"]]

    def one(self, z, **changed):
        d = {**self.digits, **changed}
        return self.full.at[z, d["y"], d["x"], d["c"]]

    def go(self, slot, source, target, device_id):
        copy = send(source, target, self.send_sems.at[slot], self.recv_sems.at[slot], device_id)
        copy.start()
        self.started.append(copy)

    def arrived(self, slot, landing):
        send(landing, landing, self.send_sems.at[slot], self.recv_sems.at[slot], self.device(c=1 - self.digits["c"])).wait_recv()

    def start(self):
        z = self.digits["z"]
        own = pltpu.make_async_copy(self.block, self.one(z), self.own_sem)
        own.start()
        for step in (1, 2, 3):
            self.go(step - 1, self.block, self.one(z), self.device(z=(z + step) % 4))
        self.own = own

    def spread_line(self):
        z = self.digits["z"]
        self.own.wait()
        for step in (1, 2, 3):
            self.arrived(step - 1, self.one((z - step + 4) % 4))
        line = self.part()
        self.go(3, line, line, self.device(**{self.first: 1 - self.digits[self.first]}))
        self.go(4, line, line, self.device(**{self.second: 1 - self.digits[self.second]}))
        self.go(5, line, line, self.device(c=1 - self.digits["c"]))

    def spread_first(self):
        line = self.part(**{self.first: 1 - self.digits[self.first]})
        self.arrived(3, line)
        self.go(6, line, line, self.device(**{self.second: 1 - self.digits[self.second]}))
        self.go(7, line, line, self.device(c=1 - self.digits["c"]))

    def spread_second(self):
        other = {self.second: 1 - self.digits[self.second]}
        for slot, line in ((4, self.part(**other)), (6, self.part(**other, **{self.first: 1 - self.digits[self.first]}))):
            self.arrived(slot, line)
            self.go(slot + 4 - (slot == 6), line, line, self.device(c=1 - self.digits["c"]))

    def finish(self):
        c = 1 - self.digits["c"]
        a = {self.first: 1 - self.digits[self.first]}
        b = {self.second: 1 - self.digits[self.second]}
        for slot, line in ((5, self.part(c=c)), (7, self.part(c=c, **a)), (8, self.part(c=c, **b)), (9, self.part(c=c, **a, **b))):
            self.arrived(slot, line)
        for copy in self.started:
            copy.wait_send()


class Reduce:
    COPIES = 8

    def __init__(self, parts, from_core, from_first, from_second, from_line, send_sems, recv_sems, order):
        self.parts = parts
        self.from_core, self.from_first, self.from_second, self.from_line = from_core, from_first, from_second, from_line
        self.send_sems, self.recv_sems = send_sems, recv_sems
        self.first, self.second = order
        self.digits, self.device = place()
        self.started = []

    def at(self, z, first, second, c):
        d = {self.first: first, self.second: second}
        return (z, d["y"], d["x"], c)

    def go(self, slot, source, target, device_id):
        copy = send(source, target, self.send_sems.at[slot], self.recv_sems.at[slot], device_id)
        copy.start()
        self.started.append(copy)

    def arrived(self, slot, landing):
        send(landing, landing, self.send_sems.at[slot], self.recv_sems.at[slot], self.device(c=1 - self.digits["c"])).wait_recv()

    def add(self, place_of, received, count):
        def body(i, carry):
            index = place_of(i)
            total = self.parts[index].astype(jnp.float32) + received(i).astype(jnp.float32)
            self.parts[index] = total.astype(jnp.bfloat16)
            return carry

        lax.fori_loop(0, count, body, 0)

    def half(self, first, c):
        if self.first == "y":
            return self.parts.at[:, first, :, c]
        return self.parts.at[:, :, first, c]

    def start(self):
        d = self.digits
        c = 1 - d["c"]
        sibling = self.device(c=c)
        self.go(0, self.half(1 - d[self.first], c), self.from_core.at[0], sibling)
        self.go(1, self.half(d[self.first], c), self.from_core.at[1], sibling)

    def core_far(self):
        d = self.digits
        self.arrived(0, self.from_core.at[0])
        self.add(
            lambda i: self.at(i // 2, 1 - d[self.first], i % 2, d["c"]), lambda i: self.from_core[0, i // 2, i % 2], 8
        )
        self.go(2, self.half(1 - d[self.first], d["c"]), self.from_first, self.device(**{self.first: 1 - d[self.first]}))

    def core_near(self):
        d = self.digits
        self.arrived(1, self.from_core.at[1])
        self.add(lambda i: self.at(i // 2, d[self.first], i % 2, d["c"]), lambda i: self.from_core[1, i // 2, i % 2], 8)

    def first_axis(self):
        d = self.digits
        self.arrived(2, self.from_first)
        far = 1 - d[self.second]
        self.add(lambda i: self.at(i, d[self.first], far, d["c"]), lambda i: self.from_first[i, far], 4)
        q = {self.first: d[self.first], self.second: far}
        self.go(3, self.parts.at[:, q["y"], q["x"], d["c"]], self.from_second, self.device(**{self.second: far}))
        near = d[self.second]
        self.add(lambda i: self.at(i, d[self.first], near, d["c"]), lambda i: self.from_first[i, near], 4)

    def second_axis(self):
        d = self.digits
        self.arrived(3, self.from_second)
        self.add(lambda i: self.at(i, d[self.first], d[self.second], d["c"]), lambda i: self.from_second[i], 4)
        for step in (1, 2, 3):
            z = (d["z"] + step) % 4
            source = self.parts.at[z, d["y"], d["x"], d["c"]]
            self.go(3 + step, source, self.from_line.at[step - 1], self.device(z=z))

    def finish(self, out_ref):
        d = self.digits
        total = self.parts[d["z"], d["y"], d["x"], d["c"]].astype(jnp.float32)
        for step in (1, 2, 3):
            self.arrived(3 + step, self.from_line.at[step - 1])
            total = total + self.from_line[step - 1].astype(jnp.float32)
        out_ref[...] = total
        for copy in self.started:
            copy.wait_send()


ORDERS = ("xy", "yx")
ANY = pl.BlockSpec(memory_space=pl.ANY)
FULL = (4, 2, 2, 2)


def halves(width):
    return ((0, width // 2), (width // 2, width))


def gather_kernel(count, *refs):
    blocks, fulls = refs[:count], refs[count : 2 * count]
    own_sems, send_sems, recv_sems = refs[2 * count :]
    digits, device = place()
    greet(digits, device)
    pieces = [
        Gather(blocks[i], fulls[i], own_sems.at[i], send_sems.at[i], recv_sems.at[i], ORDERS[i % 2]) for i in range(count)
    ]
    for stage in ("start", "spread_line", "spread_first", "spread_second", "finish"):
        for piece in pieces:
            getattr(piece, stage)()


def inner_groups():
    total = lax.axis_size("dp")
    group = total // RANKS
    return group, [list(range(i * group, (i + 1) * group)) for i in range(RANKS)]


def widen(block):
    group, groups = inner_groups()
    if group == 1:
        return block
    return lax.all_gather(block, "dp", axis=0, tiled=True, axis_index_groups=groups)


def narrow(block):
    group, groups = inner_groups()
    if group == 1:
        return block
    return lax.psum_scatter(block, "dp", scatter_dimension=0, tiled=True, axis_index_groups=groups)


def gather_weights(norm_gain, ffn_gain, attn_weights, w_in, w_ffn_out):
    gains = widen(jnp.stack([norm_gain, ffn_gain], axis=1))
    gain_rows = jnp.zeros((16, 128), jnp.bfloat16).at[: 2, : gains.shape[0]].set(gains.T)
    attn = widen(jnp.concatenate(attn_weights, axis=1))
    wide = widen(w_in)
    ffn = widen(w_ffn_out)
    blocks = [gain_rows, gain_rows]
    for block in (attn, wide, ffn):
        blocks += [block[:, lo:hi] for lo, hi in halves(block.shape[1])]
    blocks = blocks[1:]
    count = len(blocks)
    fulls = pl.pallas_call(
        partial(gather_kernel, count),
        out_shape=[jax.ShapeDtypeStruct(FULL + block.shape, block.dtype) for block in blocks],
        in_specs=[ANY] * count,
        out_specs=[ANY] * count,
        scratch_shapes=[
            pltpu.SemaphoreType.DMA((count,)),
            pltpu.SemaphoreType.DMA((count, Gather.COPIES)),
            pltpu.SemaphoreType.DMA((count, Gather.COPIES)),
        ],
        compiler_params=pltpu.CompilerParams(collective_id=1, has_side_effects=True),
    )(*blocks)
    gain_full = fulls[0].reshape(RANKS, 16, 128)[:, :2, : gains.shape[0]]
    gain_one, gain_two = gain_full[:, 0].reshape(-1), gain_full[:, 1].reshape(-1)
    whole = [jnp.concatenate([a.reshape(-1, a.shape[-1]), b.reshape(-1, b.shape[-1])], axis=1) for a, b in zip(fulls[1::2], fulls[2::2])]
    return gain_one, gain_two, *whole


def reduce_kernel(count, *refs):
    parts, small, outs, small_out = refs[:count], refs[count], refs[count + 1 : 2 * count + 1], refs[2 * count + 1]
    buffers = refs[2 * count + 2 : 6 * count + 2]
    small_buffer, send_sems, recv_sems, small_send, small_recv = refs[6 * count + 2 :]
    digits, device = place()
    greet(digits, device)
    pieces = [
        Reduce(parts[i], *buffers[4 * i : 4 * i + 4], send_sems.at[i], recv_sems.at[i], ORDERS[i % 2]) for i in range(count)
    ]
    for stage in ("start", "core_far", "core_near", "first_axis", "second_axis"):
        for piece in pieces:
            getattr(piece, stage)()
    small_sum(small, small_buffer, small_out, small_send, small_recv, digits, device)
    for piece, out in zip(pieces, outs):
        piece.finish(out)


def small_sum(values, buffer, out, send_sems, recv_sems, digits, device):
    out[...] = values[...]
    copies = []
    for slot, axis in enumerate("cxy"):
        buffer[2 * slot] = out[...]
        copy = send(
            buffer.at[2 * slot],
            buffer.at[2 * slot + 1],
            send_sems.at[slot],
            recv_sems.at[slot],
            device(**{axis: 1 - digits[axis]}),
        )
        copy.start()
        copies.append(copy)
        copy.wait_recv()
        out[...] = out[...] + buffer[2 * slot + 1]
    z = digits["z"]
    buffer[6 + z] = out[...]
    line = []
    for step in (1, 2, 3):
        mine = buffer.at[6 + z]
        copy = send(mine, mine, send_sems.at[2 + step], recv_sems.at[2 + step], device(z=(z + step) % 4))
        copy.start()
        line.append(copy)
    for step in (1, 2, 3):
        theirs = buffer.at[6 + (z - step + 4) % 4]
        send(theirs, theirs, send_sems.at[2 + step], recv_sems.at[2 + step], device(z=(z + step) % 4)).wait_recv()
    out[...] = (buffer[6] + buffer[7]) + (buffer[8] + buffer[9])
    for copy in copies + line:
        copy.wait_send()


def reduce_grads(attn, wide, ffn, gain_one, gain_two, table_sum):
    blocks = []
    for block in (attn, wide, ffn):
        blocks += [
            block[:, lo:hi].astype(jnp.bfloat16).reshape(FULL + (-1, hi - lo)) for lo, hi in halves(block.shape[1])
        ]
    count = len(blocks)
    small = jnp.concatenate([gain_one, gain_two, table_sum.reshape(-1)])
    pad = -small.shape[0] % 1024
    small = jnp.pad(small, (0, pad)).reshape(-1, 128)
    buffers = []
    for block in blocks:
        one = block.shape[4:]
        buffers += [
            pltpu.VMEM((2, 4, 2) + one, jnp.bfloat16),
            pltpu.VMEM((4, 2) + one, jnp.bfloat16),
            pltpu.VMEM((4,) + one, jnp.bfloat16),
            pltpu.VMEM((3,) + one, jnp.bfloat16),
        ]
    outs = pl.pallas_call(
        partial(reduce_kernel, count),
        out_shape=[jax.ShapeDtypeStruct(block.shape[4:], jnp.float32) for block in blocks]
        + [jax.ShapeDtypeStruct(small.shape, jnp.float32)],
        in_specs=[VMEM] * (count + 1),
        out_specs=[VMEM] * (count + 1),
        scratch_shapes=buffers
        + [
            pltpu.VMEM((10,) + small.shape, jnp.float32),
            pltpu.SemaphoreType.DMA((count, Reduce.COPIES)),
            pltpu.SemaphoreType.DMA((count, Reduce.COPIES)),
            pltpu.SemaphoreType.DMA((6,)),
            pltpu.SemaphoreType.DMA((6,)),
        ],
        compiler_params=pltpu.CompilerParams(collective_id=2, has_side_effects=True, vmem_limit_bytes=60 << 20),
    )(*blocks, small)
    sums = [narrow(jnp.concatenate(pair, axis=1)) for pair in zip(outs[0:count:2], outs[1:count:2])]
    flat = outs[count].reshape(-1)
    if inner_groups()[0] > 1:
        flat = lax.psum(flat, "dp", axis_index_groups=inner_groups()[1])
    each = D // lax.axis_size("dp")
    start = lax.axis_index("dp") * each
    gain_one_sum = lax.dynamic_slice(flat, (start,), (each,))
    gain_two_sum = lax.dynamic_slice(flat, (D + start,), (each,))
    table_total = flat[2 * D : 2 * D + NB * H].reshape(NB, H)
    return *sums, gain_one_sum, gain_two_sum, table_total


def per_device(
    tokens,
    lengths,
    norm_gain,
    w_query,
    w_key,
    w_value,
    w_out,
    bias_table,
    ffn_gain,
    w_in,
    w_ffn_out,
    cotangent,
):
    gain_one, gain_two, full_attn, full_in, full_ffn = gather_weights(
        norm_gain, ffn_gain, (w_query, w_key, w_value, w_out), w_in, w_ffn_out
    )
    wqkv, wo = full_attn[:, : 3 * D], full_attn[:, 3 * D :]
    km_marks, qm_marks = seg_marks(lengths)
    strips = bias_strips(bias_table)
    far = jnp.stack([bias_table[15], bias_table[31]], axis=1).astype(f32)
    n1, q, k, v, mix, lse, resid, n2 = attn_fwd(tokens, gain_one, wqkv, wo, gain_two, km_marks, qm_marks, strips, far)
    out, gres, g2, gin, gff = ffn(n2, cotangent, resid, gain_two, full_in, full_ffn)
    gtok, g1, gat, gout, tacc, facc = attn_bwd(
        tokens, gain_one, n1, wqkv, wo, mix, q, k, v, gres, km_marks, qm_marks, strips, lse, far
    )
    table = table_grad(tacc, facc)
    gattn = jnp.concatenate([gat[0], gat[1], gat[2], gout], axis=1)
    attn_sum, wide_sum, ffn_sum, g1s, g2s, table_total = reduce_grads(gattn, gin, gff, g1[0], g2[0], table)
    return (out, gtok, g1s, *jnp.split(attn_sum, 4, axis=1), table_total, g2s, wide_sum, ffn_sum)


def solution(mesh):
    return jax.shard_map(
        per_device,
        mesh=mesh,
        in_specs=(
            P("dp", None),
            P("dp", None),
            P("dp"),
            P("dp", None),
            P("dp", None),
            P("dp", None),
            P("dp", None),
            P(),
            P("dp"),
            P("dp", None),
            P("dp", None),
            P("dp", None),
        ),
        out_specs=(
            P("dp", None),
            P("dp", None),
            P("dp"),
            P("dp", None),
            P("dp", None),
            P("dp", None),
            P("dp", None),
            P(),
            P("dp"),
            P("dp", None),
            P("dp", None),
        ),
        check_vma=False,
    )
```

```python
from functools import partial

import jax
import jax.numpy as jnp
from jax import lax
from jax.experimental import pallas as pl
from jax.experimental.pallas import tpu as pltpu
from jax.sharding import PartitionSpec as P

D = 768
H = 12
NB = 32
SEQ = 512
FF = 3072
EPSILON = 1e-6
CUTOFFS = (12, 16, 23, 32, 46, 64, 91)
RANKS = 32
GROUPS = 3
TILES = 4
TILE = 768
MESH_ID = pl.DeviceIdType.MESH
f32, bf16 = jnp.float32, jnp.bfloat16

GROUP_PIECE, OUT_PIECE, FFN_PIECE, IN_PIECE, PIECES = 0, 3, 4, 8, 12
ROWS, COLS = 48, 384


def nt(a, b):
    return lax.dot_general(a, b, (((1,), (1,)), ((), ())), preferred_element_type=f32)


def nn(a, b):
    return jnp.dot(a, b, preferred_element_type=f32)


def exact(a, b, dims=(((1,), (0,)), ((), ()))):
    return lax.dot_general(a, b, dims, precision=lax.Precision.HIGHEST, preferred_element_type=f32)


def part_of(index, size):
    return pl.ds(pl.multiple_of(index * size, size), size)


def place():
    me = lax.axis_index("dp")
    group = lax.axis_size("dp") // RANKS
    rank, low = me // group, me % group
    digits = dict(z=rank // 8, y=(rank // 4) % 2, x=(rank // 2) % 2, c=rank % 2)

    def device(**changed):
        d = {**digits, **changed}
        return ((((d["z"] * 2 + d["y"]) * 2 + d["x"]) * 2 + d["c"]) * group + low,)

    return digits, device


def partners(digits, device):
    line = [device(z=(digits["z"] + step) % 4) for step in (1, 2, 3)]
    return line + [device(**{axis: 1 - digits[axis]}) for axis in "yxc"]


def greet(digits, device):
    barrier = pltpu.get_barrier_semaphore()
    others = partners(digits, device)
    for other in others:
        pl.semaphore_signal(barrier, inc=1, device_id=other, device_id_type=MESH_ID)
    pl.semaphore_wait(barrier, len(others))


class Transfers:
    def __init__(self, send_sems, recv_sems, digits, device):
        self.send_sems, self.recv_sems, self.digits, self.device = send_sems, recv_sems, digits, device

    def flip(self, *axes):
        return {axis: 1 - self.digits[axis] for axis in axes}

    def copy(self, slot):
        source, target, device_id = self.spec(slot)
        return pltpu.make_async_remote_copy(
            src_ref=source,
            dst_ref=target,
            send_sem=self.send_sems.at[slot],
            recv_sem=self.recv_sems.at[slot],
            device_id=device_id,
            device_id_type=MESH_ID,
        )

    def go(self, *slots):
        for slot in slots:
            self.copy(slot).start()

    def arrived(self, *slots):
        for slot in slots:
            landing = self.landing(slot)
            pltpu.make_async_remote_copy(
                src_ref=landing,
                dst_ref=landing,
                send_sem=self.send_sems.at[slot],
                recv_sem=self.recv_sems.at[slot],
                device_id=self.device(c=1 - self.digits["c"]),
                device_id_type=MESH_ID,
            ).wait_recv()

    def sent(self, count):
        for slot in range(count):
            self.copy(slot).wait_send()


class Gather(Transfers):
    SLOTS = 10

    def __init__(self, full, send_sems, recv_sems, order, digits, device):
        super().__init__(send_sems, recv_sems, digits, device)
        self.full = full
        self.first, self.second = order

    def line_of(self, *flipped):
        d = {**self.digits, **self.flip(*flipped)}
        return self.full.at[:, d["y"], d["x"], d["c"]]

    def block_of(self, z):
        d = self.digits
        return self.full.at[z, d["y"], d["x"], d["c"]]

    def spec(self, slot):
        z, a, b = self.digits["z"], self.first, self.second
        if slot < 3:
            own = self.block_of(z)
            return own, own, self.device(z=(z + slot + 1) % 4)
        flipped, towards = ((), (), (), (a,), (a,), (b,), (b, a))[slot - 3], (a, b, "c", b, "c", "c", "c")[slot - 3]
        line = self.line_of(*flipped)
        return line, line, self.device(**self.flip(towards))

    def landing(self, slot):
        a, b = self.first, self.second
        if slot < 3:
            return self.block_of((self.digits["z"] + 3 - slot) % 4)
        return self.line_of(*((a,), (b,), ("c",), (b, a), ("c", a), ("c", b), ("c", b, a))[slot - 3])

    def start(self):
        self.go(0, 1, 2)

    def line(self):
        self.arrived(0, 1, 2)
        self.go(3, 4, 5)

    def across(self):
        self.arrived(3)
        self.go(6, 7)

    def along(self):
        self.arrived(4)
        self.go(8)
        self.arrived(6)
        self.go(9)

    def finish(self):
        self.arrived(5, 7, 8, 9)
        self.sent(self.SLOTS)


class Reduce(Transfers):
    SLOTS = 7

    def __init__(self, parts, received, send_sems, recv_sems, order, digits, device, credits=None, grants=None):
        super().__init__(send_sems, recv_sems, digits, device)
        self.parts = parts
        self.from_core, self.from_first, self.from_second, self.from_line = received
        self.first, self.second = order
        self.credits, self.grants = credits, grants

    def half(self, first, c):
        if self.first == "y":
            return self.parts.at[:, first, :, c]
        return self.parts.at[:, :, first, c]

    def at(self, z, first, second):
        d = {self.first: first, self.second: second}
        return (z, d["y"], d["x"], self.digits["c"])

    def spec(self, slot):
        d, a, b = self.digits, self.first, self.second
        if slot < 2:
            side = (1 - d[a], d[a])[slot]
            return self.half(side, 1 - d["c"]), self.from_core.at[slot], self.device(**self.flip("c"))
        if slot == 2:
            return self.half(1 - d[a], d["c"]), self.from_first, self.device(**self.flip(a))
        if slot == 3:
            q = {**d, **self.flip(b)}
            return self.parts.at[:, q["y"], q["x"], d["c"]], self.from_second, self.device(**self.flip(b))
        z = (d["z"] + slot - 3) % 4
        return self.parts.at[z, d["y"], d["x"], d["c"]], self.from_line.at[slot - 4], self.device(z=z)

    def landing(self, slot):
        if slot < 2:
            return self.from_core.at[slot]
        if slot < 4:
            return (self.from_first, self.from_second)[slot - 2]
        return self.from_line.at[slot - 4]

    def spend(self, *kinds):
        if self.credits is not None:
            for kind in kinds:
                pl.semaphore_wait(self.credits.at[kind], 1)

    def grant(self):
        d = self.digits
        if self.grants is not None:
            others = [self.device(**self.flip(axis)) for axis in ("c", self.first, self.second)]
            others += [self.device(z=(d["z"] + 4 - step) % 4) for step in (1, 2, 3)]
            for kind, other in enumerate(others):
                pl.semaphore_signal(self.grants.at[kind], inc=1, device_id=other, device_id_type=MESH_ID)

    def add(self, place_of, received, count):
        def body(i, carry):
            index = place_of(i)
            self.parts[index] = (self.parts[index].astype(f32) + received(i).astype(f32)).astype(bf16)
            return carry

        lax.fori_loop(0, count, body, 0)

    def start(self):
        self.spend(0)
        self.go(0, 1)

    def core(self):
        d, a = self.digits, self.first
        self.arrived(0)
        self.add(lambda i: self.at(i // 2, 1 - d[a], i % 2), lambda i: self.received_core(0, i), 8)
        self.spend(1)
        self.go(2)
        self.arrived(1)
        self.add(lambda i: self.at(i // 2, d[a], i % 2), lambda i: self.received_core(1, i), 8)

    def received_core(self, side, i):
        return self.from_core[side, i // 2, i % 2]

    def across(self):
        d, a, b = self.digits, self.first, self.second
        self.arrived(2)
        self.add(lambda i: self.at(i, d[a], 1 - d[b]), lambda i: self.from_first[i, 1 - d[b]], 4)
        self.spend(2)
        self.go(3)
        self.add(lambda i: self.at(i, d[a], d[b]), lambda i: self.from_first[i, d[b]], 4)

    def along(self):
        d, a, b = self.digits, self.first, self.second
        self.arrived(3)
        self.add(lambda i: self.at(i, d[a], d[b]), lambda i: self.from_second[i], 4)
        self.spend(3, 4, 5)
        self.go(4, 5, 6)

    def finish(self, store):
        d = self.digits
        total = self.parts[d["z"], d["y"], d["x"], d["c"]].astype(f32)
        for slot in (4, 5, 6):
            self.arrived(slot)
            total = total + self.from_line[slot - 4].astype(f32)
        store(total)
        self.sent(self.SLOTS)
        self.grant()


class SmallSum(Transfers):
    SLOTS = 6

    def __init__(self, total, buffer, send_sems, recv_sems, digits, device):
        super().__init__(send_sems, recv_sems, digits, device)
        self.total, self.buffer = total, buffer

    def spec(self, slot):
        z = self.digits["z"]
        if slot < 3:
            return self.buffer.at[2 * slot], self.buffer.at[2 * slot + 1], self.device(**self.flip("cxy"[slot]))
        mine = self.buffer.at[6 + z]
        return mine, mine, self.device(z=(z + slot - 2) % 4)

    def landing(self, slot):
        if slot < 3:
            return self.buffer.at[2 * slot + 1]
        return self.buffer.at[6 + (self.digits["z"] + 6 - slot) % 4]

    def start(self, slot):
        if slot < 3:
            self.buffer[2 * slot] = self.total[...]
            self.go(slot)
        else:
            self.buffer[6 + self.digits["z"]] = self.total[...]
            self.go(3, 4, 5)

    def finish(self, slot):
        if slot < 3:
            self.arrived(slot)
            self.total[...] = self.total[...] + self.buffer[2 * slot + 1]
        else:
            self.arrived(3, 4, 5)
            self.total[...] = (self.buffer[6] + self.buffer[7]) + (self.buffer[8] + self.buffer[9])
            self.sent(self.SLOTS)


def pack(block):
    rows = block.reshape(-1, 8, 2 * COLS)
    return jnp.concatenate([rows[:, :, :COLS], rows[:, :, COLS:]], axis=1).reshape(-1, COLS)


def unpack(block):
    rows = block.reshape(-1, 2, 8, COLS)
    return jnp.concatenate([rows[:, 0].reshape(-1, COLS), rows[:, 1].reshape(-1, COLS)], axis=1)


def unpack_piece(piece, target):
    def plane(z, carry):
        target[part_of(z, 192), :] = unpack(piece[z].astype(f32).reshape(8 * ROWS, COLS)).astype(bf16)
        return carry

    lax.fori_loop(0, 4, plane, 0)


def pack_piece(piece, z, grad):
    piece[z] = pack(grad).astype(bf16).reshape(2, 2, 2, ROWS, COLS)


def bucket_of(offsets):
    distance = jnp.abs(offsets)
    coarse = jnp.full_like(distance, 8)
    for cutoff in CUTOFFS:
        coarse = coarse + (distance >= cutoff).astype(jnp.int32)
    return jnp.where(distance < 8, distance, coarse) + jnp.where(offsets > 0, 16, 0)


def strip_onehot(shift):
    column = lax.broadcasted_iota(jnp.int32, (128, 512), 1)
    column = jnp.where(column >= shift, column - shift, column - shift + 512)
    offset = jnp.where(column < 384, 128 - column, 640 - column)
    return bucket_of(offset) == lax.broadcasted_iota(jnp.int32, (128, 512), 0)


def make_strips(table_t, strips):
    line = nn(table_t[...], strip_onehot(0).astype(bf16))
    for head in range(H):
        rows = jnp.broadcast_to(line[head : head + 1], (128, 512))
        strips[head] = pltpu.roll(rows, 0, 1, stride=1, stride_axis=0)[:, :384].astype(strips.dtype)


def strip_sums(strip):
    wide = jnp.concatenate([strip, jnp.zeros((128, 128), f32)], axis=1)
    total = wide[:8]
    for r in range(1, 16):
        total = total + pltpu.roll(wide[8 * r : 8 * r + 8], 512 - 8 * r, 1)
    return total


def table_sums(sums, far_sums):
    row = lax.broadcasted_iota(jnp.int32, (8 * H, 8 * H), 0)
    column = lax.broadcasted_iota(jnp.int32, (8 * H, 8 * H), 1)
    turned = exact((column == (row // 8) * 8 + 7 - row % 8).astype(f32), sums)
    lines = [
        jnp.sum(pltpu.roll(turned[8 * h : 8 * h + 8], 0, 1, stride=1, stride_axis=0), axis=0, keepdims=True)
        for h in range(H)
    ]
    lines.append(jnp.zeros((128 - H, 512), f32))
    table = exact(strip_onehot(7).astype(f32)[:NB], jnp.concatenate(lines, axis=0), (((1,), (1,)), ((), ())))
    bucket = lax.broadcasted_iota(jnp.int32, (NB, 128), 0)
    head = lax.broadcasted_iota(jnp.int32, (NB, 128), 1)
    for h in range(H):
        for side, index in ((0, 15), (1, 31)):
            total = jnp.sum(jnp.sum(far_sums[h, side], axis=0, keepdims=True), axis=1, keepdims=True)
            table = table + jnp.where((bucket == index) & (head == h), total, 0.0)
    return table


def make_marks(lengths, key_marks, query_marks):
    position = lax.broadcasted_iota(jnp.int32, (SEQ, 128), 0)
    lane = lax.broadcasted_iota(jnp.int32, (SEQ, 128), 1)
    for row in range(key_marks.shape[0] // SEQ):
        segment = jnp.zeros((SEQ, 128), jnp.int32)
        end = 0
        for k in range(1, 5):
            end = end + lengths[row, k]
            segment = segment + (position >= end).astype(jnp.int32)
        own = segment == lane
        rows = slice(row * SEQ, (row + 1) * SEQ)
        key_marks[rows, :] = jnp.where(own, 1.0, 0.0).astype(bf16)
        query_marks[rows, :] = jnp.where(own | (lane >= 5), 0.0, -1e30).astype(bf16)


def lane_mask(h):
    lane = lax.broadcasted_iota(jnp.int32, (1, 128), 1)
    return lane < 64 if h == 0 else lane >= 64


def scores_t(keys, queries, strip, low, high, half):
    raw = nt(keys, queries)
    rows = []
    for bj in range(4):
        blocks = []
        for bi in (0, 1):
            d = bj - bi - 2 * half
            block = raw[128 * bj : 128 * (bj + 1), 128 * bi : 128 * (bi + 1)]
            if d <= -2:
                block = block + low
            elif d >= 2:
                block = block + high
            else:
                block = block + strip[:, 128 * (1 - d) : 128 * (2 - d)].astype(f32)
            blocks.append(block)
        rows.append(jnp.concatenate(blocks, axis=1))
    return jnp.concatenate(rows, axis=0)


def heads_of(ref, rows, which, pair):
    return ref[rows, pl.ds(pl.multiple_of(which * 256 + pair * 128, 128), 128)]


def attend(qkv, key_marks, query_marks, strips, table, mix, lse, row, group, pair):
    rows = part_of(row, SEQ)
    q2, k2, v2 = (heads_of(qkv, rows, which, pair) for which in range(3))
    v2t = v2.T
    kmk, qmk = key_marks[rows, :], query_marks[rows, :]
    outs = []
    for h in range(2):
        head = (group * 2 + pair) * 2 + h
        keys = jnp.concatenate([jnp.where(lane_mask(h), k2, 0), kmk], axis=1)
        for half in range(2):
            span = slice(256 * half, 256 * half + 256)
            queries = jnp.concatenate([q2[span], qmk[span]], axis=1)
            scores = scores_t(keys, queries, strips[head], table[15, head], table[31, head], half)
            peak = jnp.max(scores, axis=0, keepdims=True)
            expo = jnp.exp(scores - peak)
            total = jnp.sum(expo, axis=0, keepdims=True)
            probs = (expo * (1.0 / total)).astype(bf16)
            lse[row, pl.ds(head, 1), span] = peak + jnp.log(total)
            outs.append(nn(v2t[64 * h : 64 * h + 64], probs))
    both = jnp.concatenate([jnp.concatenate(outs[:2], axis=1), jnp.concatenate(outs[2:], axis=1)], axis=0)
    mix[rows, part_of(group * 2 + pair, 128)] = both.T.astype(bf16)


def attend_back(qkv, gmix, key_marks, query_marks, strips, table, lse, strip_grads, far_sums, row, group, pair):
    rows = part_of(row, SEQ)
    q2, k2, v2 = (heads_of(qkv, rows, which, pair) for which in range(3))
    g2 = gmix[rows, part_of(group * 2 + pair, 128)]
    k2t = k2.T
    kmk, qmk = key_marks[rows, :], query_marks[rows, :]
    grad_v, grad_k, grad_q = 0.0, 0.0, []
    for h in range(2):
        head = (group * 2 + pair) * 2 + h
        mask = lane_mask(h)
        keys = jnp.concatenate([jnp.where(mask, k2, 0), kmk], axis=1)
        vm, qh, gh = jnp.where(mask, v2, 0), jnp.where(mask, q2, 0), jnp.where(mask, g2, 0)
        for half in range(2):
            span = slice(256 * half, 256 * half + 256)
            queries = jnp.concatenate([q2[span], qmk[span]], axis=1)
            scores = scores_t(keys, queries, strips[head], table[15, head], table[31, head], half)
            probs = jnp.exp(scores - lse[row, pl.ds(head, 1), span])
            grad_probs = nt(vm, g2[span])
            inner = jnp.sum(probs * grad_probs, axis=0, keepdims=True)
            grad = probs * (grad_probs - inner)
            low = grad.astype(bf16)
            grad_v = grad_v + nn(probs.astype(bf16), gh[span])
            grad_k = grad_k + nn(low, qh[span])
            grad_q.append(nn(k2t[64 * h : 64 * h + 64], low))
            strip_rows, strip_base = part_of(group * 2 + pair, 128), 384 * h
            for bi in (0, 1):
                far = [[], []]
                for bj in range(4):
                    d = bj - bi - 2 * half
                    block = grad[128 * bj : 128 * (bj + 1), 128 * bi : 128 * (bi + 1)]
                    if abs(d) <= 1:
                        span_d = slice(strip_base + 128 * (1 - d), strip_base + 128 * (2 - d))
                        strip_grads[strip_rows, span_d] += block
                    else:
                        far[d > 0].append(jnp.sum(block.reshape(16, 8, 128), axis=0))
                for side in (0, 1):
                    if far[side]:
                        far_sums[head, side] += sum(far[side][1:], far[side][0])
    qt = jnp.concatenate([jnp.concatenate(grad_q[:2], axis=1), jnp.concatenate(grad_q[2:], axis=1)], axis=0)
    for which, value in enumerate((qt.T, grad_k, grad_v)):
        qkv[rows, pl.ds(pl.multiple_of(which * 256 + pair * 128, 128), 128)] = value.astype(bf16)


def inv_rms(x):
    return lax.rsqrt(jnp.mean(x * x, axis=-1, keepdims=True) + EPSILON)


def norm_back(grad, x, gain):
    s = inv_rms(x)
    gg = grad * gain
    return s * gg - x * (s * s * s * jnp.mean(gg * x, axis=-1, keepdims=True)), jnp.sum(grad * x * s, axis=0, keepdims=True)


def gelu_both(x):
    cdf = 0.5 + 0.5 * lax.erf(x * 0.7071067811865476)
    return x * cdf, cdf + x * (jnp.exp(x * x * -0.5) * 0.3989422804014327)


def gain_line(gains, which):
    blocks = gains[...].reshape(8 * RANKS, 128).astype(bf16)
    lane = lax.broadcasted_iota(jnp.int32, (128, D), 1)
    spread = nn(blocks, (lane % 24 == lax.broadcasted_iota(jnp.int32, (128, D), 0)).astype(bf16))
    row = lax.broadcasted_iota(jnp.int32, (8 * RANKS, D), 0)
    column = lax.broadcasted_iota(jnp.int32, (8 * RANKS, D), 1)
    return jnp.sum(jnp.where(row == (column // 24) * 8 + which, spread, 0.0), axis=0, keepdims=True)


def run_at(step, plan):
    for when, stages in plan.items():

        @pl.when(step == when)
        def _(stages=stages):
            for stage in stages:
                stage()


def layer_kernel(
    tokens, cot_hbm, lengths, norm_gain, ffn_gain, w_query, w_key, w_value, w_out, w_in, w_ffn, table, table_t,
    out_hbm, gtok_hbm, grad_q, grad_k, grad_v, grad_o, grad_in, grad_ffn, small,
    pieces, gains, weights, win, wff, qkv, mix, normed, turned, cot, cot_t, resid, out_sum, grad_sum, act, grad_inner,
    strips, key_marks, query_marks, lse, far_sums, diagonals, from_core, from_first, from_second, from_line, small_buffer,
    gather_send, gather_recv, gain_send, gain_recv, reduce_send, reduce_recv, small_send, small_recv, credits, local_sems,
):
    count = tokens.shape[0]
    halves = count // SEQ
    digits, device = place()
    me = (digits["z"], digits["y"], digits["x"], digits["c"])

    load_cot = pltpu.make_async_copy(cot_hbm, cot, local_sems.at[0])
    load_cot.start()

    gains[me] = jnp.zeros((8, 128), f32)
    gains[(*me, slice(0, 1), slice(0, 24))] = norm_gain[...].astype(f32)
    gains[(*me, slice(1, 2), slice(0, 24))] = ffn_gain[...].astype(f32)
    for g in range(GROUPS):
        span = slice(256 * g, 256 * g + 256)
        block = jnp.concatenate([w[:, span] for w in (w_query, w_key, w_value)], axis=1)
        pieces[(GROUP_PIECE + g, *me)] = pack(block.astype(f32)).astype(bf16)
    pieces[(OUT_PIECE, *me)] = pack(w_out[...].astype(f32)).astype(bf16)
    for i in range(4):
        pieces[(FFN_PIECE + i, *me)] = w_ffn[ROWS * (i // 2) : ROWS * (i // 2 + 1), COLS * (i % 2) : COLS * (i % 2 + 1)]
        pieces[(IN_PIECE + i, *me)] = pack(w_in[:, TILE * i : TILE * (i + 1)].astype(f32)).astype(bf16)

    greet(digits, device)
    orders = ("xy", "yx")
    gain_gather = Gather(gains, gain_send, gain_recv, "xy", digits, device)
    gathers = [
        Gather(pieces.at[i], gather_send.at[i], gather_recv.at[i], orders[i % 2], digits, device) for i in range(PIECES)
    ]
    order = [IN_PIECE + t for t in range(4)] + [FFN_PIECE + i for i in range(4)] + [OUT_PIECE] + [0, 1, 2]
    reduces = []
    for n, i in enumerate(order):
        slot = n if n < 8 else n - 8
        received = (from_core.at[slot], from_first.at[slot], from_second.at[slot], from_line.at[slot])
        reduces.append(
            Reduce(
                pieces.at[i],
                received,
                reduce_send.at[n],
                reduce_recv.at[n],
                orders[n % 2],
                digits,
                device,
                credits=credits.at[slot] if n >= 8 else None,
                grants=credits.at[slot] if n < 4 else None,
            )
        )

    def store_in(t):
        def store(total):
            grad_in[:, TILE * t : TILE * (t + 1)] = unpack(total)

        return store

    def store_ffn(i):
        def store(total):
            grad_ffn[ROWS * (i // 2) : ROWS * (i // 2 + 1), COLS * (i % 2) : COLS * (i % 2 + 1)] = total

        return store

    def store_out(total):
        grad_o[...] = unpack(total)

    def store_group(g):
        def store(total):
            block = unpack(total)
            for which, target in enumerate((grad_q, grad_k, grad_v)):
                target[:, 256 * g : 256 * (g + 1)] = block[:, 256 * which : 256 * (which + 1)]

        return store

    stores = [store_in(t) for t in range(4)] + [store_ffn(i) for i in range(4)] + [store_out]
    stores += [store_group(g) for g in range(3)]

    def gather_wave(k):
        stages = []
        if k < PIECES:
            stages.append(gathers[k].line)
        if 0 <= k - 1 < PIECES:
            stages.append(gathers[k - 1].across)
        if 0 <= k - 2 < PIECES:
            stages.append(gathers[k - 2].along)
        if 0 <= k - 3 < PIECES:
            stages.append(gathers[k - 3].finish)
            if k - 3 < FFN_PIECE:
                stages.append(partial(unpack_piece, pieces.at[k - 3], weights.at[k - 3]))
        return stages

    def reduce_wave(k):
        stages = []
        if k < PIECES:
            stages.append(reduces[k].core)
        if 0 <= k - 1 < PIECES:
            stages.append(reduces[k - 1].across)
        if 0 <= k - 2 < PIECES:
            stages.append(reduces[k - 2].along)
        if 0 <= k - 3 < PIECES:
            stages.append(partial(reduces[k - 3].finish, stores[k - 3]))
        return stages

    def run(stages):
        for stage in stages:
            stage()

    gain_gather.start()
    for gather in gathers:
        gather.start()
    make_marks(lengths, key_marks, query_marks)
    make_strips(table_t, strips)
    gain_gather.line()
    gain_gather.across()
    gain_gather.along()
    run(gather_wave(0))
    gain_gather.finish()
    gain_one, gain_two = gain_line(gains, 0), gain_line(gains, 1)

    def norm_one(i, carry):
        rows = part_of(i, 256)
        x = tokens[rows, :].astype(f32)
        normed[rows, :] = (x * inv_rms(x) * gain_one).astype(bf16)
        return carry

    lax.fori_loop(0, count // 256, norm_one, 0)
    for k in (1, 2, 3):
        run(gather_wave(k))

    steps = 2 * halves
    forward_plan = {0: gather_wave(4), 2: gather_wave(5), 4: gather_wave(6), 6: gather_wave(7), 8: gather_wave(8), 10: gather_wave(9)}

    def forward_group(g, carry):
        def project(i, carry):
            rows = part_of(i, 256)
            qkv[g, rows, :] = nn(normed[rows, :], weights[GROUP_PIECE + g]).astype(bf16)
            return carry

        lax.fori_loop(0, count // 256, project, 0)

        def forward(s, carry):
            attend(qkv.at[g], key_marks, query_marks, strips, table, mix, lse, s % halves, g, s // halves)
            run_at(g * steps + s, forward_plan)
            return carry

        lax.fori_loop(0, steps, forward, 0)
        return carry

    lax.fori_loop(0, GROUPS, forward_group, 0)

    load_cot.wait()

    def after_attention(i, carry):
        rows = part_of(i, 256)
        r = tokens[rows, :].astype(f32) + nn(mix[rows, :], weights[OUT_PIECE])
        resid[rows, :] = r
        n = (r * inv_rms(r) * gain_two).astype(bf16)
        turned[:, rows] = n.T
        normed[rows, :] = n
        cot_t[:, rows] = cot[rows, :].T
        return carry

    lax.fori_loop(0, count // 256, after_attention, 0)
    run(gather_wave(10))
    run(gather_wave(11))

    ffn_plan = {
        1: gather_wave(12),
        3: gather_wave(13),
        5: gather_wave(14),
        6: [reduces[0].core],
        7: [reduces[0].across],
        8: [reduces[0].along],
        9: [partial(reduces[0].finish, stores[0])],
        11: [reduces[1].core],
        12: [reduces[1].across],
        13: [reduces[1].along],
        14: [partial(reduces[1].finish, stores[1])],
        16: [reduces[2].core],
        17: [reduces[2].across],
        18: [reduces[2].along],
        19: [partial(reduces[2].finish, stores[2])],
    }
    width = 256

    def ffn_tile(t, carry):
        unpack_piece(pieces.at[IN_PIECE + t], win)
        for i in range(4):
            blocks = pieces[FFN_PIECE + i, t].reshape(8, ROWS, COLS)
            for b in range(8):
                rows = slice(96 * b + ROWS * (i // 2), 96 * b + ROWS * (i // 2 + 1))
                wff[rows, COLS * (i % 2) : COLS * (i % 2 + 1)] = blocks[b]

        def columns(w, carry):
            span = part_of(w, width)

            def chunk(i, carry):
                rows = part_of(i, 512)
                inner = nn(normed[rows, :], win[:, span])
                grad_act = nt(cot[rows, :], wff[span, :])
                value, slope = gelu_both(inner)
                act[rows, span] = value.astype(bf16)
                grad_inner[rows, span] = (slope * grad_act).astype(bf16)
                return carry

            lax.fori_loop(0, count // 512, chunk, 0)
            run_at(5 * t + w, ffn_plan)
            return carry

        lax.fori_loop(0, TILE // width, columns, 0)

        def sums(i, carry):
            rows = part_of(i, 512)
            o = nn(act[rows, :], wff[...])
            gn = nt(grad_inner[rows, :], win[...])

            @pl.when(t == 0)
            def _():
                out_sum[rows, :] = resid[rows, :] + o
                grad_sum[rows, :] = gn

            @pl.when(t > 0)
            def _():
                out_sum[rows, :] += o
                grad_sum[rows, :] += gn

            return carry

        lax.fori_loop(0, count // 512, sums, 0)
        run_at(5 * t + 3, ffn_plan)

        def grads_in(z, carry):
            pack_piece(pieces.at[IN_PIECE + t], z, nn(turned[part_of(z, 192), :], grad_inner[...]))
            return carry

        lax.fori_loop(0, 4, grads_in, 0)
        run_at(t, {k: [reduces[k].start] for k in range(TILES)})

        for ch in range(2):
            grad = nn(cot_t[COLS * ch : COLS * (ch + 1), :], act[...]).astype(bf16).T
            for b in range(8):
                for rh in range(2):
                    pieces[FFN_PIECE + 2 * rh + ch, t, b // 4, (b // 2) % 2, b % 2] = grad[
                        96 * b + ROWS * rh : 96 * b + ROWS * (rh + 1)
                    ]
        run_at(5 * t + 4, ffn_plan)
        return carry

    lax.fori_loop(0, TILES, ffn_tile, 0)
    for n in range(4, 8):
        reduces[n].start()

    small[...] = jnp.zeros(small.shape, f32)

    def spread_line(row, line):
        for j in range(D // 128):
            small[row + j : row + j + 1, :] += line[:, 128 * j : 128 * (j + 1)]

    def before_back(i, carry):
        rows = part_of(i, 256)
        act[rows, :] = out_sum[rows, :].astype(bf16)
        r = resid[rows, :]
        into, gain_sum = norm_back(grad_sum[rows, :], r, gain_two)
        spread_line(6, gain_sum)
        grad = cot[rows, :].astype(f32) + into
        grad_sum[rows, :] = grad
        low = grad.astype(bf16)
        cot[rows, :] = low
        normed[rows, :] = nt(low, weights[OUT_PIECE]).astype(bf16)
        x = tokens[rows, :].astype(f32)
        turned[:, rows] = (x * inv_rms(x) * gain_one).astype(bf16).T
        return carry

    lax.fori_loop(0, count // 256, before_back, 0)
    store_output = pltpu.make_async_copy(act, out_hbm, local_sems.at[1])
    store_output.start()
    out_sum[...] = jnp.zeros(out_sum.shape, f32)
    far_sums[...] = jnp.zeros(far_sums.shape, f32)
    run(reduce_wave(3)[:1])

    for z in range(4):
        pack_piece(pieces.at[OUT_PIECE], z, nn(mix[:, 192 * z : 192 * (z + 1)].T, cot[...]))

    def wave(core=None, across=None, along=None, finish=None, start=None):
        stages = []
        if start is not None:
            stages.append(reduces[start].start)
        if core is not None:
            stages.append(reduces[core].core)
        if across is not None:
            stages.append(reduces[across].across)
        if along is not None:
            stages.append(reduces[along].along)
        if finish is not None:
            stages.append(partial(reduces[finish].finish, stores[finish]))
        return stages

    back_plan = {
        0: wave(core=4, across=3),
        1: wave(core=5, across=4, along=3),
        2: wave(core=6, across=5, along=4, finish=3, start=8),
        3: wave(core=7, across=6, along=5, finish=4),
        4: wave(core=8, across=7, along=6, finish=5),
        5: wave(across=8, along=7, finish=6, core=9),
        6: wave(along=8, finish=7, across=9),
        7: wave(finish=8, along=9),
        8: wave(finish=9),
        9: wave(core=10),
        10: wave(across=10),
        11: wave(along=10),
    }

    def back_group(g, carry):
        def back(s, carry):
            attend_back(
                qkv.at[g], normed, key_marks, query_marks, strips, table, lse, out_sum, far_sums, s % halves, g, s // halves
            )
            run_at(g * steps + s, back_plan)
            return carry

        lax.fori_loop(0, steps, back, 0)

        def grads(z, carry):
            pack_piece(pieces.at[GROUP_PIECE + g], z, nn(turned[part_of(z, 192), :], qkv[g]))
            return carry

        lax.fori_loop(0, 4, grads, 0)
        run_at(g, {k: [reduces[9 + k].start] for k in range(GROUPS)})
        return carry

    lax.fori_loop(0, GROUPS, back_group, 0)

    last_plan = {0: wave(core=11, finish=10), 2: wave(across=11)}

    def last(i, carry):
        rows = part_of(i, 256)
        grad = nt(qkv[0, rows, :], weights[0]) + nt(qkv[1, rows, :], weights[1]) + nt(qkv[2, rows, :], weights[2])
        into, gain_sum = norm_back(grad, tokens[rows, :].astype(f32), gain_one)
        spread_line(0, gain_sum)
        grad_sum[rows, :] = grad_sum[rows, :] + into
        run_at(i, last_plan)
        return carry

    lax.fori_loop(0, count // 256, last, 0)
    store_gtok = pltpu.make_async_copy(grad_sum, gtok_hbm, local_sems.at[2])
    store_gtok.start()
    for pair in range(H // 2):
        for h in range(2):
            head = 2 * pair + h
            diagonals[8 * head : 8 * head + 8, :] = strip_sums(out_sum[128 * pair : 128 * pair + 128, 384 * h : 384 * h + 384])
    small[16:48, :] = table_sums(diagonals[...], far_sums)
    sums = SmallSum(small, small_buffer, small_send, small_recv, digits, device)
    sums.start(0)
    reduces[11].along()
    sums.finish(0)
    sums.start(1)
    sums.finish(1)
    sums.start(2)
    reduces[11].finish(stores[11])
    sums.finish(2)
    sums.start(3)
    sums.finish(3)
    store_output.wait()
    store_gtok.wait()


def inner_groups():
    total = lax.axis_size("dp")
    group = total // RANKS
    return group, [list(range(i * group, (i + 1) * group)) for i in range(RANKS)]


def widen(block):
    group, groups = inner_groups()
    if group == 1:
        return block
    return lax.all_gather(block, "dp", axis=0, tiled=True, axis_index_groups=groups)


def narrow(block):
    group, groups = inner_groups()
    if group == 1:
        return block
    return lax.psum_scatter(block, "dp", scatter_dimension=0, tiled=True, axis_index_groups=groups)


def per_device(
    tokens, lengths, norm_gain, w_query, w_key, w_value, w_out, bias_table, ffn_gain, w_in, w_ffn_out, cotangent
):
    count = tokens.shape[0]
    norm_gain, ffn_gain, w_query, w_key, w_value, w_out, w_in, w_ffn_out = (
        widen(w) for w in (norm_gain, ffn_gain, w_query, w_key, w_value, w_out, w_in, w_ffn_out)
    )
    table_t = jnp.pad(bias_table.T, ((0, 4), (0, 128 - NB)))
    any_space = pl.BlockSpec(memory_space=pl.ANY)
    vmem = pl.BlockSpec(memory_space=pltpu.VMEM)
    smem = pl.BlockSpec(memory_space=pltpu.SMEM)
    full = (4, 2, 2, 2)
    out = jax.ShapeDtypeStruct
    outs = pl.pallas_call(
        layer_kernel,
        out_shape=[out((count, D), bf16), out((count, D), f32)]
        + [out((24, D), f32)] * 4
        + [out((24, FF), f32), out((96, D), f32), out((48, 128), f32)],
        in_specs=[vmem, any_space, smem] + [vmem] * 8 + [smem, vmem],
        out_specs=[any_space] * 2 + [vmem] * 7,
        scratch_shapes=[
            pltpu.VMEM((PIECES,) + full + (ROWS, COLS), bf16),
            pltpu.VMEM(full + (8, 128), f32),
            pltpu.VMEM((4, D, D), bf16),
            pltpu.VMEM((D, TILE), bf16),
            pltpu.VMEM((TILE, D), bf16),
            pltpu.VMEM((GROUPS, count, D), bf16),
            pltpu.VMEM((count, D), bf16),
            pltpu.VMEM((count, D), bf16),
            pltpu.VMEM((D, count), bf16),
            pltpu.VMEM((count, D), bf16),
            pltpu.VMEM((D, count), bf16),
            pltpu.VMEM((count, D), f32),
            pltpu.VMEM((count, D), f32),
            pltpu.VMEM((count, D), f32),
            pltpu.VMEM((count, TILE), bf16),
            pltpu.VMEM((count, TILE), bf16),
            pltpu.VMEM((H, 128, 384), bf16),
            pltpu.VMEM((count, 128), bf16),
            pltpu.VMEM((count, 128), bf16),
            pltpu.VMEM((count // SEQ, H, SEQ), f32),
            pltpu.VMEM((H, 2, 8, 128), f32),
            pltpu.VMEM((8 * H, 512), f32),
            pltpu.VMEM((8, 2, 4, 2, ROWS, COLS), bf16),
            pltpu.VMEM((8, 4, 2, ROWS, COLS), bf16),
            pltpu.VMEM((8, 4, ROWS, COLS), bf16),
            pltpu.VMEM((8, 3, ROWS, COLS), bf16),
            pltpu.VMEM((10, 48, 128), f32),
            pltpu.SemaphoreType.DMA((PIECES, Gather.SLOTS)),
            pltpu.SemaphoreType.DMA((PIECES, Gather.SLOTS)),
            pltpu.SemaphoreType.DMA((Gather.SLOTS,)),
            pltpu.SemaphoreType.DMA((Gather.SLOTS,)),
            pltpu.SemaphoreType.DMA((PIECES, Reduce.SLOTS)),
            pltpu.SemaphoreType.DMA((PIECES, Reduce.SLOTS)),
            pltpu.SemaphoreType.DMA((SmallSum.SLOTS,)),
            pltpu.SemaphoreType.DMA((SmallSum.SLOTS,)),
            pltpu.SemaphoreType.REGULAR((4, 6)),
            pltpu.SemaphoreType.DMA((3,)),
        ],
        compiler_params=pltpu.CompilerParams(collective_id=1, has_side_effects=True, vmem_limit_bytes=63 << 20),
    )(
        tokens,
        cotangent,
        lengths,
        norm_gain.reshape(1, -1),
        ffn_gain.reshape(1, -1),
        w_query,
        w_key,
        w_value,
        w_out,
        w_in,
        w_ffn_out,
        bias_table.astype(f32),
        table_t,
    )
    output, grad_tokens, grad_q, grad_k, grad_v, grad_o, grad_in, grad_ffn, small = outs
    group, groups = inner_groups()
    if group > 1:
        small = lax.psum(small, "dp", axis_index_groups=groups)
    each = D // lax.axis_size("dp")
    start = lax.axis_index("dp") * each
    grad_norm_gain = lax.dynamic_slice(small[:6].reshape(-1), (start,), (each,))
    grad_ffn_gain = lax.dynamic_slice(small[6:12].reshape(-1), (start,), (each,))
    return (
        output,
        grad_tokens,
        grad_norm_gain,
        narrow(grad_q),
        narrow(grad_k),
        narrow(grad_v),
        narrow(grad_o),
        small[16:48, :H],
        grad_ffn_gain,
        narrow(grad_in),
        narrow(grad_ffn),
    )


def solution(mesh):
    rows, whole = P("dp", None), P("dp")
    return jax.shard_map(
        per_device,
        mesh=mesh,
        in_specs=(rows, rows, whole, rows, rows, rows, rows, P(), whole, rows, rows, rows),
        out_specs=(rows, rows, whole, rows, rows, rows, rows, P(), whole, rows, rows),
        check_vma=False,
    )
```

```python
from functools import partial

import jax
import jax.numpy as jnp
from jax import lax
from jax.experimental import pallas as pl
from jax.experimental.pallas import tpu as pltpu
from jax.sharding import PartitionSpec as P

D = 768
H = 12
NB = 32
SEQ = 512
FF = 3072
EPSILON = 1e-6
CUTOFFS = (12, 16, 23, 32, 46, 64, 91)
RANKS = 32
GROUPS = 3
TILES = 4
TILE = 768
MESH_ID = pl.DeviceIdType.MESH
f32, bf16 = jnp.float32, jnp.bfloat16

GROUP_PIECE, OUT_PIECE, PIECES = 0, 3, 12
FFN_PIECES, IN_PIECES = (4, 6, 8, 10), (5, 7, 9, 11)
ROWS, COLS = 48, 384
LANDINGS = 6


PLAN = {
    "S": [("g", 1, "line"), ("g", 0, "across"), ("g", 2, "line"), ("g", 1, "across"), ("g", 3, "line"), ("g", 0, "along"), ("g", 2, "across"), ("g", 0, "finish")],
    "F0": [("g", 1, "along"), ("g", 3, "across"), ("g", 4, "line"), ("g", 5, "line")],
    "F1": [("g", 1, "finish")],
    "F2": [("g", 2, "along")],
    "F3": [("g", 3, "along"), ("g", 2, "finish")],
    "F4": [("g", 3, "finish"), ("g", 4, "across"), ("g", 5, "across"), ("g", 6, "line"), ("g", 7, "line")],
    "A": [("g", 4, "along"), ("g", 5, "along"), ("g", 4, "finish"), ("g", 6, "across"), ("g", 8, "line"), ("g", 5, "finish")],
    "T1": [("g", 7, "across"), ("g", 9, "line")],
    "T4": [("g", 6, "along"), ("g", 8, "across"), ("g", 10, "line")],
    "T5": [("g", 7, "along"), ("g", 6, "finish")],
    "T6": [("g", 9, "across"), ("g", 11, "line"), ("r", 0, "core"), ("g", 7, "finish")],
    "T7": [("r", 1, "core"), ("g", 8, "along"), ("g", 10, "across")],
    "T9": [("g", 8, "finish"), ("g", 9, "along")],
    "T11": [("g", 9, "finish"), ("g", 11, "across")],
    "T16": [("r", 0, "across"), ("r", 1, "across"), ("r", 2, "core"), ("r", 3, "core"), ("g", 10, "along"), ("g", 11, "along")],
    "T18": [("g", 10, "finish"), ("g", 11, "finish")],
    "T19": [("r", 0, "along"), ("r", 1, "along")],
    "T23": [("r", 2, "across"), ("r", 3, "across"), ("r", 4, "core"), ("r", 5, "core"), ("r", 0, "finish")],
    "T26": [("r", 2, "along"), ("r", 1, "finish")],
    "T27": [("r", 3, "along")],
    "B2": [("r", 2, "finish"), ("r", 4, "across"), ("r", 5, "across"), ("r", 6, "core"), ("r", 7, "core")],
    "B4": [("r", 8, "start")],
    "K0": [("r", 4, "along")],
    "K1": [("r", 3, "finish"), ("r", 5, "along")],
    "K2": [("r", 4, "finish"), ("r", 6, "across"), ("r", 7, "across"), ("r", 8, "core"), ("r", 9, "core")],
    "K4": [("r", 5, "finish"), ("r", 6, "along"), ("r", 7, "along")],
    "K5": [("r", 8, "across"), ("r", 9, "across"), ("r", 10, "core")],
    "L0": [("r", 6, "finish")],
    "L1": [("r", 8, "along"), ("r", 11, "core")],
    "E": [("r", 7, "finish"), ("r", 9, "along"), ("r", 10, "across"), ("r", 8, "finish"), ("r", 11, "across"), ("r", 9, "finish"), ("r", 10, "along"), ("r", 11, "along"), ("r", 10, "finish"), ("r", 11, "finish")],
}


def nt(a, b):
    return lax.dot_general(a, b, (((1,), (1,)), ((), ())), preferred_element_type=f32)


def nn(a, b):
    return jnp.dot(a, b, preferred_element_type=f32)


def tn(a, b):
    return lax.dot_general(a, b, (((0,), (0,)), ((), ())), preferred_element_type=f32)


def exact(a, b, dims=(((1,), (0,)), ((), ()))):
    return lax.dot_general(a, b, dims, precision=lax.Precision.HIGHEST, preferred_element_type=f32)


def part_of(index, size):
    return pl.ds(pl.multiple_of(index * size, size), size)


def place():
    me = lax.axis_index("dp")
    group = lax.axis_size("dp") // RANKS
    rank, low = me // group, me % group
    digits = dict(z=rank // 8, y=(rank // 4) % 2, x=(rank // 2) % 2, c=rank % 2)

    def device(**changed):
        d = {**digits, **changed}
        return ((((d["z"] * 2 + d["y"]) * 2 + d["x"]) * 2 + d["c"]) * group + low,)

    return digits, device


def partners(digits, device):
    line = [device(z=(digits["z"] + step) % 4) for step in (1, 2, 3)]
    return line + [device(**{axis: 1 - digits[axis]}) for axis in "yxc"]


def greet(digits, device):
    barrier = pltpu.get_barrier_semaphore()
    others = partners(digits, device)
    for other in others:
        pl.semaphore_signal(barrier, inc=1, device_id=other, device_id_type=MESH_ID)
    return lambda: pl.semaphore_wait(barrier, len(others))


class Transfers:
    def __init__(self, send_sems, recv_sems, digits, device):
        self.send_sems, self.recv_sems, self.digits, self.device = send_sems, recv_sems, digits, device

    def flip(self, *axes):
        return {axis: 1 - self.digits[axis] for axis in axes}

    def copy(self, slot):
        source, target, device_id = self.spec(slot)
        return pltpu.make_async_remote_copy(
            src_ref=source,
            dst_ref=target,
            send_sem=self.send_sems.at[slot],
            recv_sem=self.recv_sems.at[slot],
            device_id=device_id,
            device_id_type=MESH_ID,
        )

    def go(self, *slots):
        for slot in slots:
            self.copy(slot).start()

    def arrived_at(self, slot, landing):
        pltpu.make_async_remote_copy(
            src_ref=landing,
            dst_ref=landing,
            send_sem=self.send_sems.at[slot],
            recv_sem=self.recv_sems.at[slot],
            device_id=self.device(c=1 - self.digits["c"]),
            device_id_type=MESH_ID,
        ).wait_recv()

    def arrived(self, *slots):
        for slot in slots:
            self.arrived_at(slot, self.landing(slot))

    def sent(self, count):
        for slot in range(count):
            self.copy(slot).wait_send()


class Gather(Transfers):
    SLOTS = 10

    def __init__(self, full, send_sems, recv_sems, order, digits, device):
        super().__init__(send_sems, recv_sems, digits, device)
        self.full = full
        self.first, self.second = order

    def line_of(self, *flipped):
        d = {**self.digits, **self.flip(*flipped)}
        return self.full.at[:, d["y"], d["x"], d["c"]]

    def block_of(self, z):
        d = self.digits
        return self.full.at[z, d["y"], d["x"], d["c"]]

    def spec(self, slot):
        z, a, b = self.digits["z"], self.first, self.second
        if slot < 3:
            own = self.block_of(z)
            return own, own, self.device(z=(z + slot + 1) % 4)
        flipped, towards = ((), (), (), (a,), (a,), (b,), (b, a))[slot - 3], (a, b, "c", b, "c", "c", "c")[slot - 3]
        line = self.line_of(*flipped)
        return line, line, self.device(**self.flip(towards))

    def landing(self, slot):
        a, b = self.first, self.second
        if slot < 3:
            return self.block_of((self.digits["z"] + 3 - slot) % 4)
        return self.line_of(*((a,), (b,), ("c",), (b, a), ("c", a), ("c", b), ("c", b, a))[slot - 3])

    def start(self):
        self.go(0, 1, 2)

    def line(self):
        self.arrived(0, 1, 2)
        self.go(3, 4, 5)

    def across(self):
        self.arrived(3)
        self.go(6, 7)

    def along(self):
        self.arrived(4)
        self.go(8)
        self.arrived(6)
        self.go(9)

    def finish(self):
        self.arrived(5, 7, 8, 9)
        self.sent(self.SLOTS)


class PlaneGather(Gather):
    def __init__(self, full, send_sems, recv_sems, order, digits, device, plane):
        super().__init__(full, send_sems, recv_sems, order, digits, device)
        self.plane = plane

    def spec(self, slot):
        if slot < 3:
            line = self.line_of()
            return line, line, self.device(z=(self.digits["z"] + slot + 1) % 4)
        return super().spec(slot)

    def start(self):
        @pl.when(self.digits["z"] == self.plane)
        def _():
            self.go(0, 1, 2)

    def line(self):
        z = self.digits["z"]
        for slot in range(3):

            @pl.when(z == (self.plane + slot + 1) % 4)
            def _(slot=slot):
                line = self.line_of()
                self.arrived_at(slot, line)

        self.go(3, 4, 5)

    def sent(self, count):
        for slot in range(3, count):
            self.copy(slot).wait_send()

        @pl.when(self.digits["z"] == self.plane)
        def _():
            for slot in range(3):
                self.copy(slot).wait_send()


class Reduce(Transfers):
    SLOTS = 7

    def __init__(self, parts, received, send_sems, recv_sems, order, digits, device, credits=None, grants=None):
        super().__init__(send_sems, recv_sems, digits, device)
        self.parts = parts
        self.from_core, self.from_first, self.from_second, self.from_line = received
        self.first, self.second = order
        self.credits, self.grants = credits, grants

    def half(self, first, c):
        if self.first == "y":
            return self.parts.at[:, first, :, c]
        return self.parts.at[:, :, first, c]

    def at(self, z, first, second):
        d = {self.first: first, self.second: second}
        return (z, d["y"], d["x"], self.digits["c"])

    def spec(self, slot):
        d, a, b = self.digits, self.first, self.second
        if slot < 2:
            side = (1 - d[a], d[a])[slot]
            return self.half(side, 1 - d["c"]), self.from_core.at[slot], self.device(**self.flip("c"))
        if slot == 2:
            return self.half(1 - d[a], d["c"]), self.from_first, self.device(**self.flip(a))
        if slot == 3:
            q = {**d, **self.flip(b)}
            return self.parts.at[:, q["y"], q["x"], d["c"]], self.from_second, self.device(**self.flip(b))
        z = (d["z"] + slot - 3) % 4
        return self.parts.at[z, d["y"], d["x"], d["c"]], self.from_line.at[slot - 4], self.device(z=z)

    def landing(self, slot):
        if slot < 2:
            return self.from_core.at[slot]
        if slot < 4:
            return (self.from_first, self.from_second)[slot - 2]
        return self.from_line.at[slot - 4]

    def spend(self, *kinds):
        if self.credits is not None:
            for kind in kinds:
                pl.semaphore_wait(self.credits.at[kind], 1)

    def grant(self):
        d = self.digits
        if self.grants is not None:
            others = [self.device(**self.flip(axis)) for axis in ("c", self.first, self.second)]
            others += [self.device(z=(d["z"] + 4 - step) % 4) for step in (1, 2, 3)]
            for kind, other in enumerate(others):
                pl.semaphore_signal(self.grants.at[kind], inc=1, device_id=other, device_id_type=MESH_ID)

    def add(self, first, second, received):
        d = {self.first: first, self.second: slice(None) if second is None else second}
        index = (slice(None), d["y"], d["x"], self.digits["c"])
        self.parts[index] = (self.parts[index].astype(f32) + received.astype(f32)).astype(bf16)

    def start(self):
        self.spend(0)
        self.go(0, 1)

    def core(self):
        d, a = self.digits, self.first
        self.arrived(0)
        self.add(1 - d[a], None, self.from_core[0])
        self.spend(1)
        self.go(2)
        self.arrived(1)
        self.add(d[a], None, self.from_core[1])

    def across(self):
        d, a, b = self.digits, self.first, self.second
        self.arrived(2)
        self.add(d[a], 1 - d[b], self.from_first[:, 1 - d[b]])
        self.spend(2)
        self.go(3)
        self.add(d[a], d[b], self.from_first[:, d[b]])

    def along(self):
        d, a, b = self.digits, self.first, self.second
        self.arrived(3)
        self.add(d[a], d[b], self.from_second[...])
        self.spend(3, 4, 5)
        self.go(4, 5, 6)

    def finish(self, store):
        d = self.digits
        total = self.parts[d["z"], d["y"], d["x"], d["c"]].astype(f32)
        for slot in (4, 5, 6):
            self.arrived(slot)
            total = total + self.from_line[slot - 4].astype(f32)
        store(total)
        self.sent(self.SLOTS)
        self.grant()


class PlaneReduce(Reduce):
    def __init__(self, parts, received, plane_in, send_sems, recv_sems, order, digits, device, credits, grants, plane):
        super().__init__(parts, received, send_sems, recv_sems, order, digits, device, credits, grants)
        self.plane_in, self.plane = plane_in, plane

    def along(self):
        d, a, b = self.digits, self.first, self.second
        self.arrived(3)
        self.add(d[a], d[b], self.from_second[...])
        self.spend(3, 4, 5)
        for step in (1, 2, 3):

            @pl.when(d["z"] == (self.plane + step) % 4)
            def _(step=step):
                self.to_plane(step).start()

    def to_plane(self, step):
        d = self.digits
        return pltpu.make_async_remote_copy(
            src_ref=self.parts.at[:, d["y"], d["x"], d["c"]],
            dst_ref=self.plane_in.at[step - 1],
            send_sem=self.send_sems.at[3 + step],
            recv_sem=self.recv_sems.at[3 + step],
            device_id=self.device(z=self.plane),
            device_id_type=MESH_ID,
        )

    def finish(self, store):
        d = self.digits

        @pl.when(d["z"] == self.plane)
        def _():
            total = self.parts[:, d["y"], d["x"], d["c"]].astype(f32)
            for step in (1, 2, 3):
                self.arrived_at(3 + step, self.plane_in.at[step - 1])
                total = total + self.plane_in[step - 1].astype(f32)
            store(total)

        for step in (1, 2, 3):

            @pl.when(d["z"] == (self.plane + step) % 4)
            def _(step=step):
                self.to_plane(step).wait_send()

        for slot in range(4):
            self.copy(slot).wait_send()
        self.grant()


class SmallSum(Transfers):
    SLOTS = 6

    def __init__(self, total, buffer, send_sems, recv_sems, digits, device):
        super().__init__(send_sems, recv_sems, digits, device)
        self.total, self.buffer = total, buffer

    def spec(self, slot):
        z = self.digits["z"]
        if slot < 3:
            return self.buffer.at[2 * slot], self.buffer.at[2 * slot + 1], self.device(**self.flip("cxy"[slot]))
        mine = self.buffer.at[6 + z]
        return mine, mine, self.device(z=(z + slot - 2) % 4)

    def landing(self, slot):
        if slot < 3:
            return self.buffer.at[2 * slot + 1]
        return self.buffer.at[6 + (self.digits["z"] + 6 - slot) % 4]

    def start(self, slot):
        if slot < 3:
            self.buffer[2 * slot] = self.total[...]
            self.go(slot)
        else:
            self.buffer[6 + self.digits["z"]] = self.total[...]
            self.go(3, 4, 5)

    def finish(self, slot):
        if slot < 3:
            self.arrived(slot)
            self.total[...] = self.total[...] + self.buffer[2 * slot + 1]
        else:
            self.arrived(3, 4, 5)
            self.total[...] = (self.buffer[6] + self.buffer[7]) + (self.buffer[8] + self.buffer[9])
            self.sent(self.SLOTS)


def pack(block):
    rows = block.reshape(-1, 8, 2 * COLS)
    return jnp.concatenate([rows[:, :, :COLS], rows[:, :, COLS:]], axis=1).reshape(-1, COLS)


def unpack(block):
    rows = block.reshape(-1, 2, 8, COLS)
    return jnp.concatenate([rows[:, 0].reshape(-1, COLS), rows[:, 1].reshape(-1, COLS)], axis=1)


def unpack_piece(piece, target):
    def plane(z, carry):
        target[part_of(z, 192), :] = unpack(piece[z].astype(f32).reshape(8 * ROWS, COLS)).astype(bf16)
        return carry

    lax.fori_loop(0, 4, plane, 0)


def pack_piece(piece, z, grad):
    piece[z] = pack(grad).astype(bf16).reshape(2, 2, 2, ROWS, COLS)


def bucket_of(offsets):
    distance = jnp.abs(offsets)
    coarse = jnp.full_like(distance, 8)
    for cutoff in CUTOFFS:
        coarse = coarse + (distance >= cutoff).astype(jnp.int32)
    return jnp.where(distance < 8, distance, coarse) + jnp.where(offsets > 0, 16, 0)


def strip_onehot(shift):
    column = lax.broadcasted_iota(jnp.int32, (128, 512), 1)
    column = jnp.where(column >= shift, column - shift, column - shift + 512)
    offset = jnp.where(column < 384, 128 - column, 640 - column)
    return bucket_of(offset) == lax.broadcasted_iota(jnp.int32, (128, 512), 0)


def make_strips(table_t, strips):
    line = nn(table_t[...], strip_onehot(0).astype(bf16)[:NB])
    for head in range(H):
        rows = jnp.broadcast_to(line[head : head + 1], (128, 512))
        strips[head] = pltpu.roll(rows, 0, 1, stride=1, stride_axis=0)[:, :384].astype(strips.dtype)


def strip_sums(strip):
    wide = jnp.concatenate([strip, jnp.zeros((128, 128), f32)], axis=1)
    total = wide[:8]
    for r in range(1, 16):
        total = total + pltpu.roll(wide[8 * r : 8 * r + 8], 512 - 8 * r, 1)
    return total


def table_sums(sums, far_sums):
    row = lax.broadcasted_iota(jnp.int32, (8 * H, 8 * H), 0)
    column = lax.broadcasted_iota(jnp.int32, (8 * H, 8 * H), 1)
    turned = exact((column == (row // 8) * 8 + 7 - row % 8).astype(f32), sums)
    lines = [
        jnp.sum(pltpu.roll(turned[8 * h : 8 * h + 8], 0, 1, stride=1, stride_axis=0), axis=0, keepdims=True)
        for h in range(H)
    ]
    lines.append(jnp.zeros((16 - H, 512), f32))
    table = exact(jnp.concatenate(lines, axis=0), strip_onehot(7).astype(f32), (((1,), (1,)), ((), ())))
    head = lax.broadcasted_iota(jnp.int32, (16, 128), 0)
    bucket = lax.broadcasted_iota(jnp.int32, (16, 128), 1)
    for side, index in ((0, 15), (1, 31)):
        rows = [jnp.sum(far_sums[h, side], axis=0, keepdims=True) for h in range(H)] + [jnp.zeros((16 - H, 128), f32)]
        total = jnp.sum(jnp.concatenate(rows, axis=0), axis=1, keepdims=True)
        table = table + jnp.where((bucket == index) & (head < H), total, 0.0)
    return table


def make_marks(lengths, key_marks, query_marks):
    position = lax.broadcasted_iota(jnp.int32, (SEQ, 128), 0)
    lane = lax.broadcasted_iota(jnp.int32, (SEQ, 128), 1)
    for row in range(key_marks.shape[0] // SEQ):
        segment = jnp.zeros((SEQ, 128), jnp.int32)
        end = 0
        for k in range(1, 5):
            end = end + lengths[row, k]
            segment = segment + (position >= end).astype(jnp.int32)
        own = segment == lane
        rows = slice(row * SEQ, (row + 1) * SEQ)
        key_marks[rows, :] = jnp.where(own, 1.0, 0.0).astype(bf16)
        query_marks[rows, :] = jnp.where(own | (lane >= 5), 0.0, -1e30).astype(bf16)


def lane_mask(h):
    lane = lax.broadcasted_iota(jnp.int32, (1, 128), 1)
    return lane < 64 if h == 0 else lane >= 64


def biased(raw, strip, half):
    low, high = strip[0:1, 383:384].astype(f32), strip[127:128, 0:1].astype(f32)
    rows = []
    for bj in range(4):
        blocks = []
        for bi in (0, 1):
            d = bj - bi - 2 * half
            block = raw[128 * bj : 128 * (bj + 1), 128 * bi : 128 * (bi + 1)]
            if d <= -2:
                block = block + low
            elif d >= 2:
                block = block + high
            else:
                block = block + strip[:, 128 * (1 - d) : 128 * (2 - d)].astype(f32)
            blocks.append(block)
        rows.append(jnp.concatenate(blocks, axis=1))
    return jnp.concatenate(rows, axis=0)


def heads_of(ref, rows, which, pair):
    return ref[rows, pl.ds(pl.multiple_of(which * 256 + pair * 128, 128), 128)]


def raw_scores(q2, k2, key_marks, query_marks):
    queries = jnp.concatenate([q2, query_marks], axis=1)
    return [nt(jnp.concatenate([jnp.where(lane_mask(h), k2, 0), key_marks], axis=1), queries) for h in range(2)]


def attend(qkv, key_marks, query_marks, strips, mix, lse, group, pair):
    count = mix.shape[0] // SEQ
    raws, values = [], []
    for row in range(count):
        rows = slice(row * SEQ, (row + 1) * SEQ)
        q2, k2, v2 = (heads_of(qkv, rows, which, pair) for which in range(3))
        raws.append(raw_scores(q2, k2, key_marks[rows, :], query_marks[rows, :]))
        values.append(v2.T)
    for row in range(count):
        outs = []
        for h in range(2):
            head = (group * 2 + pair) * 2 + h
            halves = []
            for half in range(2):
                span = slice(256 * half, 256 * half + 256)
                scores = biased(raws[row][h][:, span], strips[head], half)
                peak = jnp.max(scores, axis=0, keepdims=True)
                expo = jnp.exp(scores - peak)
                total = jnp.sum(expo, axis=0, keepdims=True)
                lse[row, pl.ds(head, 1), span] = peak + jnp.log(total)
                halves.append(nn(values[row][64 * h : 64 * h + 64], expo.astype(bf16)) * (1.0 / total))
            outs.append(jnp.concatenate(halves, axis=1))
        mix[row * SEQ : (row + 1) * SEQ, part_of(group * 2 + pair, 128)] = jnp.concatenate(outs, axis=0).T.astype(bf16)


def attend_back(qkv, gmix, key_marks, query_marks, strips, lse, inner, strip_grads, far_sums, group, pair):
    count = gmix.shape[0] // SEQ
    lanes = part_of(group * 2 + pair, 128)
    held = []
    for row in range(count):
        rows = slice(row * SEQ, (row + 1) * SEQ)
        q2, k2, v2 = (heads_of(qkv, rows, which, pair) for which in range(3))
        g2 = gmix[rows, lanes]
        raws = raw_scores(q2, k2, key_marks[rows, :], query_marks[rows, :])
        held.append((q2, k2.T, v2, g2, raws))
    for row in range(count):
        rows = slice(row * SEQ, (row + 1) * SEQ)
        q2, k2t, v2, g2, raws = held[row]
        grads = [nt(jnp.where(lane_mask(h), v2, 0), g2) for h in range(2)]
        grad_v, grad_k, grad_q = 0.0, 0.0, []
        for h in range(2):
            head = (group * 2 + pair) * 2 + h
            mask = lane_mask(h)
            near, far = {}, ([], [])
            probs_low, scores_low = [], []
            for half in range(2):
                span = slice(256 * half, 256 * half + 256)
                probs = jnp.exp(biased(raws[h][:, span], strips[head], half) - lse[row, pl.ds(head, 1), span])
                grad = probs * (grads[h][:, span] - inner[row, pl.ds(head, 1), span])
                probs_low.append(probs.astype(bf16))
                scores_low.append(grad.astype(bf16))
                for bi in (0, 1):
                    for bj in range(4):
                        d = bj - bi - 2 * half
                        block = grad[128 * bj : 128 * (bj + 1), 128 * bi : 128 * (bi + 1)]
                        if abs(d) <= 1:
                            near[d] = near[d] + block if d in near else block
                        else:
                            far[d > 0].append(jnp.sum(block.reshape(16, 8, 128), axis=0))
            strip_rows = part_of(group * 2 + pair, 128)
            for d, block in near.items():
                strip_grads[strip_rows, 384 * h + 128 * (1 - d) : 384 * h + 128 * (2 - d)] += block
            for side in (0, 1):
                far_sums[head, side] += sum(far[side][1:], far[side][0])
            grad_v = grad_v + nn(jnp.concatenate(probs_low, axis=1), jnp.where(mask, g2, 0))
            low = jnp.concatenate(scores_low, axis=1)
            grad_k = grad_k + nn(low, jnp.where(mask, q2, 0))
            grad_q.append(nn(k2t[64 * h : 64 * h + 64], low))
        for which, value in enumerate((jnp.concatenate(grad_q, axis=0).T, grad_k, grad_v)):
            qkv[rows, pl.ds(pl.multiple_of(which * 256 + pair * 128, 128), 128)] = value.astype(bf16)


def inner_sums(gmix, mix):
    product = gmix.astype(f32) * mix.astype(f32)
    high = product.astype(bf16)
    low = (product - high.astype(f32)).astype(bf16)
    feature = lax.broadcasted_iota(jnp.int32, (16, D), 1)
    first = lax.broadcasted_iota(jnp.int32, (16, D), 0) * 64
    own = jnp.where((feature >= first) & (feature < first + 64), 1.0, 0.0).astype(bf16)
    return nt(own, high) + nt(own, low)


def inv_rms(x):
    return lax.rsqrt(jnp.mean(x * x, axis=-1, keepdims=True) + EPSILON)


def norm_back(grad, x, gain):
    s = inv_rms(x)
    gg = grad * gain
    return s * gg - x * (s * s * s * jnp.mean(gg * x, axis=-1, keepdims=True)), jnp.sum(grad * x * s, axis=0, keepdims=True)


def gelu_both(x):
    cdf = 0.5 + 0.5 * lax.erf(x * 0.7071067811865476)
    return x * cdf, cdf + x * (jnp.exp(x * x * -0.5) * 0.3989422804014327)


def gain_line(gains, which):
    blocks = gains[...].reshape(8 * RANKS, 128).astype(bf16)
    lane = lax.broadcasted_iota(jnp.int32, (128, D), 1)
    spread = nn(blocks, (lane % 24 == lax.broadcasted_iota(jnp.int32, (128, D), 0)).astype(bf16))
    row = lax.broadcasted_iota(jnp.int32, (8 * RANKS, D), 0)
    column = lax.broadcasted_iota(jnp.int32, (8 * RANKS, D), 1)
    return jnp.sum(jnp.where(row == (column // 24) * 8 + which, spread, 0.0), axis=0, keepdims=True)


def run_at(step, plan):
    for when, stages in plan.items():

        @pl.when(step == when)
        def _(stages=stages):
            for stage in stages:
                stage()


def layer_kernel(
    tokens_hbm, cot_hbm, lengths, norm_gain, ffn_gain, w_query, w_key, w_value, w_out, w_in, w_ffn, table_t,
    out_hbm, gtok_hbm, grad_one, grad_two, grad_table, grad_q, grad_k, grad_v, grad_o, grad_in, grad_ffn,
    pieces, gains, weights, win, wff, qkv, mix, normed, tokens, cot, resid, out_sum, grad_sum, act, grad_inner,
    strips, key_marks, query_marks, lse, inner, far_sums, small, from_core, from_first, from_second, from_line,
    plane_in, small_buffer,
    gather_send, gather_recv, gain_send, gain_recv, reduce_send, reduce_recv, small_send, small_recv, credits, local_sems,
):
    count = tokens.shape[0]
    digits, device = place()
    me = (digits["z"], digits["y"], digits["x"], digits["c"])
    all_here = greet(digits, device)

    load_tokens = pltpu.make_async_copy(tokens_hbm, tokens, local_sems.at[0])
    load_tokens.start()
    load_cot = pltpu.make_async_copy(cot_hbm, cot, local_sems.at[1])
    load_cot.start()

    orders = ("xy", "yx")
    gain_gather = Gather(gains, gain_send, gain_recv, "xy", digits, device)
    gathers = []
    for i in range(PIECES):
        common = (pieces.at[i], gather_send.at[i], gather_recv.at[i], orders[i % 2], digits, device)
        gathers.append(PlaneGather(*common, FFN_PIECES.index(i)) if i in FFN_PIECES else Gather(*common))
    order = [i for t in range(TILES) for i in (IN_PIECES[t], FFN_PIECES[t])] + [OUT_PIECE, 0, 1, 2]
    reduces = []
    for n, i in enumerate(order):
        slot = n % LANDINGS
        received = (from_core.at[slot], from_first.at[slot], from_second.at[slot], from_line.at[slot])
        sems = (reduce_send.at[n], reduce_recv.at[n], orders[n % 2], digits, device)
        limits = (credits.at[slot] if n >= LANDINGS else None, credits.at[slot] if n + LANDINGS < PIECES else None)
        if i in FFN_PIECES:
            reduces.append(PlaneReduce(pieces.at[i], received, plane_in, *sems, *limits, FFN_PIECES.index(i)))
        else:
            reduces.append(Reduce(pieces.at[i], received, *sems, *limits))

    def store_in(t):
        def store(total):
            grad_in[:, TILE * t : TILE * (t + 1)] = unpack(total)

        return store

    def store_ffn(total):
        for i in range(4):
            grad_ffn[ROWS * (i // 2) : ROWS * (i // 2 + 1), COLS * (i % 2) : COLS * (i % 2 + 1)] = total[i]

    def store_out(total):
        grad_o[...] = unpack(total)

    def store_group(g):
        def store(total):
            block = unpack(total)
            for which, target in enumerate((grad_q, grad_k, grad_v)):
                target[:, 256 * g : 256 * (g + 1)] = block[:, 256 * which : 256 * (which + 1)]

        return store

    stores = [store for t in range(TILES) for store in (store_in(t), store_ffn)] + [store_out]
    stores += [store_group(g) for g in range(GROUPS)]

    def stage(kind, n, name):
        if kind == "r":
            return partial(reduces[n].finish, stores[n]) if name == "finish" else getattr(reduces[n], name)
        if name == "finish" and n <= OUT_PIECE:
            return partial(arrive, n)
        return getattr(gathers[n], name)

    def arrive(n):
        gathers[n].finish()
        unpack_piece(pieces.at[n], weights.at[n])

    def plan(letter):
        return {int(key[1:]): [stage(*entry) for entry in PLAN[key]] for key in PLAN if key[0] == letter}

    def run(stages):
        for each in stages:
            each()

    for g in range(GROUPS):
        span = slice(256 * g, 256 * g + 256)
        block = jnp.concatenate([w[:, span] for w in (w_query, w_key, w_value)], axis=1)
        pieces[(GROUP_PIECE + g, *me)] = pack(block.astype(f32)).astype(bf16)
    gains[me] = jnp.zeros((8, 128), f32)
    gains[(*me, slice(0, 1), slice(0, 24))] = norm_gain[...].astype(f32)
    gains[(*me, slice(1, 2), slice(0, 24))] = ffn_gain[...].astype(f32)
    all_here()
    gathers[0].start()
    gain_gather.start()
    gathers[1].start()
    gathers[2].start()
    pieces[(OUT_PIECE, *me)] = pack(w_out[...].astype(f32)).astype(bf16)
    gathers[3].start()
    for t in range(TILES):

        @pl.when(digits["z"] == t)
        def _(t=t):
            for i in range(4):
                block = w_ffn[ROWS * (i // 2) : ROWS * (i // 2 + 1), COLS * (i % 2) : COLS * (i % 2 + 1)]
                pieces[FFN_PIECES[t], i, digits["y"], digits["x"], digits["c"]] = block

        gathers[FFN_PIECES[t]].start()
        pieces[(IN_PIECES[t], *me)] = pack(w_in[:, TILE * t : TILE * (t + 1)].astype(f32)).astype(bf16)
        gathers[IN_PIECES[t]].start()

    make_marks(lengths, key_marks, query_marks)
    make_strips(table_t, strips)
    gain_gather.line()
    gathers[0].line()
    gain_gather.across()
    gain_gather.along()
    gain_gather.finish()
    gain_one, gain_two = gain_line(gains, 0), gain_line(gains, 1)
    load_tokens.wait()

    def norm_one(i, carry):
        rows = part_of(i, 256)
        x = tokens[rows, :].astype(f32)
        normed[rows, :] = (x * inv_rms(x) * gain_one).astype(bf16)
        return carry

    lax.fori_loop(0, count // 256, norm_one, 0)
    run([stage(*entry) for entry in PLAN["S"]])

    forward_plan = plan("F")

    def forward_group(g, carry):
        qkv[g] = nn(normed[...], weights[GROUP_PIECE + g]).astype(bf16)

        def forward(pair, carry):
            attend(qkv.at[g], key_marks, query_marks, strips, mix, lse, g, pair)
            run_at(2 * g + pair, forward_plan)
            return carry

        lax.fori_loop(0, 2, forward, 0)
        return carry

    lax.fori_loop(0, GROUPS, forward_group, 0)

    def after_attention(i, carry):
        rows = part_of(i, 512)
        r = tokens[rows, :].astype(f32) + nn(mix[rows, :], weights[OUT_PIECE])
        resid[rows, :] = r
        normed[rows, :] = (r * inv_rms(r) * gain_two).astype(bf16)
        return carry

    lax.fori_loop(0, count // 512, after_attention, 0)
    load_cot.wait()
    run([stage(*entry) for entry in PLAN["A"]])

    ffn_plan = plan("T")
    width = 256

    def tile_piece(t, which):
        return pieces.at[4 + 2 * t + which]

    def ffn_tile(t, carry):
        unpack_piece(tile_piece(t, 1), win)
        for b in range(8):
            for i in range(4):
                rows = slice(96 * b + ROWS * (i // 2), 96 * b + ROWS * (i // 2 + 1))
                block = pieces[4 + 2 * t, i, b // 4, (b // 2) % 2, b % 2]
                wff[rows, COLS * (i % 2) : COLS * (i % 2 + 1)] = block

        def columns(w, carry):
            span = part_of(w, width)
            ffn_in = nn(normed[...], win[:, span])
            grad_act = nt(cot[...], wff[span, :])
            value, slope = gelu_both(ffn_in)
            act[:, span] = value.astype(bf16)
            grad_inner[:, span] = (slope * grad_act).astype(bf16)
            run_at(7 * t + w, ffn_plan)
            return carry

        lax.fori_loop(0, TILE // width, columns, 0)

        for i in range(2):
            rows = slice(i * count // 2, (i + 1) * count // 2)
            value = nn(act[rows, :], wff[...])
            out_sum[rows, :] = jnp.where(t == 0, resid[rows, :], out_sum[rows, :]) + value

        run_at(7 * t + 3, ffn_plan)

        for i in range(2):
            rows = slice(i * count // 2, (i + 1) * count // 2)
            value = nt(grad_inner[rows, :], win[...])
            grad_sum[rows, :] = jnp.where(t == 0, 0.0, grad_sum[rows, :]) + value

        run_at(7 * t + 4, ffn_plan)
        grad = tn(normed[...], grad_inner[...])
        for z in range(4):
            pack_piece(tile_piece(t, 1), z, grad[192 * z : 192 * (z + 1)])
        run_at(t, {k: [reduces[2 * k].start] for k in range(TILES)})
        run_at(7 * t + 5, ffn_plan)
        grad = tn(act[...], cot[...]).astype(bf16)
        for b in range(8):
            for i in range(4):
                block = grad[96 * b + ROWS * (i // 2) : 96 * b + ROWS * (i // 2 + 1), COLS * (i % 2) : COLS * (i % 2 + 1)]
                pieces[4 + 2 * t, i, b // 4, (b // 2) % 2, b % 2] = block
        run_at(t, {k: [reduces[2 * k + 1].start] for k in range(TILES)})
        run_at(7 * t + 6, ffn_plan)
        return carry

    lax.fori_loop(0, TILES, ffn_tile, 0)

    before_plan = plan("B")
    small[...] = jnp.zeros(small.shape, f32)

    def spread_line(row, line):
        for j in range(D // 128):
            small[row + j : row + j + 1, :] += line[:, 128 * j : 128 * (j + 1)]

    def before_back(i, carry):
        rows = part_of(i, 256)
        act[rows, :] = out_sum[rows, :].astype(bf16)
        into, gain_sum = norm_back(grad_sum[rows, :], resid[rows, :], gain_two)
        spread_line(6, gain_sum)
        grad = cot[rows, :].astype(f32) + into
        grad_sum[rows, :] = grad
        low = grad.astype(bf16)
        cot[rows, :] = low
        gmix = nt(low, weights[OUT_PIECE]).astype(bf16)
        inner[i // 2, :, part_of(i % 2, 256)] = inner_sums(gmix, mix[rows, :])
        x = tokens[rows, :].astype(f32)
        grad_inner[rows, :] = (x * inv_rms(x) * gain_one).astype(bf16)
        normed[rows, :] = gmix
        run_at(i, before_plan)
        return carry

    lax.fori_loop(0, count // 256, before_back, 0)
    store_output = pltpu.make_async_copy(act, out_hbm, local_sems.at[2])
    store_output.start()
    out_sum[...] = jnp.zeros(out_sum.shape, f32)
    far_sums[...] = jnp.zeros(far_sums.shape, f32)
    grad = tn(mix[...], cot[...])
    for z in range(4):
        pack_piece(pieces.at[OUT_PIECE], z, grad[192 * z : 192 * (z + 1)])
    run(before_plan.get(4, []))
    back_plan = plan("K")

    def back_group(g, carry):
        def back(pair, carry):
            attend_back(qkv.at[g], normed, key_marks, query_marks, strips, lse, inner, out_sum, far_sums, g, pair)
            run_at(2 * g + pair, back_plan)
            return carry

        lax.fori_loop(0, 2, back, 0)
        grad = tn(grad_inner[...], qkv[g])
        for z in range(4):
            pack_piece(pieces.at[GROUP_PIECE + g], z, grad[192 * z : 192 * (z + 1)])
        run_at(g, {k: [reduces[9 + k].start] for k in range(GROUPS)})
        return carry

    lax.fori_loop(0, GROUPS, back_group, 0)
    last_plan = plan("L")

    def last(i, carry):
        rows = part_of(i, 512)
        grad = nt(qkv[0, rows, :], weights[0]) + nt(qkv[1, rows, :], weights[1]) + nt(qkv[2, rows, :], weights[2])
        into, gain_sum = norm_back(grad, tokens[rows, :].astype(f32), gain_one)
        spread_line(0, gain_sum)
        grad_sum[rows, :] = grad_sum[rows, :] + into
        run_at(i, last_plan)
        return carry

    lax.fori_loop(0, count // 512, last, 0)
    store_gtok = pltpu.make_async_copy(grad_sum, gtok_hbm, local_sems.at[3])
    store_gtok.start()
    for pair in range(H // 2):
        for h in range(2):
            head = 2 * pair + h
            strip = out_sum[128 * pair : 128 * pair + 128, 384 * h : 384 * h + 384]
            resid[8 * head : 8 * head + 8, :512] = strip_sums(strip)
    small[16:32, :] = table_sums(resid[: 8 * H, :512], far_sums)
    sums = SmallSum(small, small_buffer, small_send, small_recv, digits, device)
    tail = [stage(*entry) for entry in PLAN["E"]]
    for slot in range(4):
        sums.start(slot)
        if tail:
            tail.pop(0)()
        sums.finish(slot)
    for target, row in ((grad_one, 0), (grad_two, 6)):
        line = jnp.concatenate([small[row + j : row + j + 1, :] for j in range(D // 128)], axis=1)
        rank = (lax.axis_index("dp") // (lax.axis_size("dp") // RANKS)).astype(jnp.int32)
        own = pltpu.roll(jnp.broadcast_to(line, (8, D)), (D - 24 * rank) % D, 1)
        target[...] = own[0:1, :24]
    grad_table[...] = small[16 : 16 + H, :NB]
    run(tail)
    store_output.wait()
    store_gtok.wait()


def deliver_kernel(*refs):
    count = (len(refs) - 1) // 3
    sources, targets, held, sems = refs[:count], refs[count : 2 * count], refs[2 * count : 3 * count], refs[-1]
    loads = [pltpu.make_async_copy(sources[i], held[i], sems.at[0, i]) for i in range(count)]
    stores = [pltpu.make_async_copy(held[i], targets[i], sems.at[1, i]) for i in range(count)]
    for load in loads:
        load.start()
    for load, store in zip(loads, stores):
        load.wait()
        store.start()
    for store in stores:
        store.wait()


def inner_groups():
    total = lax.axis_size("dp")
    group = total // RANKS
    return group, [list(range(i * group, (i + 1) * group)) for i in range(RANKS)]


def widen(block):
    group, groups = inner_groups()
    if group == 1:
        return block
    return lax.all_gather(block, "dp", axis=0, tiled=True, axis_index_groups=groups)


def narrow(block):
    group, groups = inner_groups()
    if group == 1:
        return block
    return lax.psum_scatter(block, "dp", scatter_dimension=0, tiled=True, axis_index_groups=groups)


def per_device(
    tokens, lengths, norm_gain, w_query, w_key, w_value, w_out, bias_table, ffn_gain, w_in, w_ffn_out, cotangent
):
    count = tokens.shape[0]
    norm_gain, ffn_gain, w_query, w_key, w_value, w_out, w_in, w_ffn_out = (
        widen(w) for w in (norm_gain, ffn_gain, w_query, w_key, w_value, w_out, w_in, w_ffn_out)
    )
    any_space = pl.BlockSpec(memory_space=pl.ANY)
    vmem = pl.BlockSpec(memory_space=pltpu.VMEM)
    smem = pl.BlockSpec(memory_space=pltpu.SMEM)
    full = (4, 2, 2, 2)
    out = jax.ShapeDtypeStruct
    shapes = [out((count, D), bf16), out((count, D), f32), out((1, 24), f32), out((1, 24), f32), out((H, NB), f32)]
    shapes += [out((24, D), f32)] * 4 + [out((24, FF), f32), out((96, D), f32)]
    results = pl.pallas_call(
        layer_kernel,
        out_shape=shapes,
        in_specs=[any_space] * 2 + [smem] + [vmem] * 9,
        out_specs=[any_space] * 2 + [vmem] * 9,
        scratch_shapes=[
            pltpu.VMEM((PIECES,) + full + (ROWS, COLS), bf16),
            pltpu.VMEM(full + (8, 128), f32),
            pltpu.VMEM((4, D, D), bf16),
            pltpu.VMEM((D, TILE), bf16),
            pltpu.VMEM((TILE, D), bf16),
            pltpu.VMEM((GROUPS, count, D), bf16),
            pltpu.VMEM((count, D), bf16),
            pltpu.VMEM((count, D), bf16),
            pltpu.VMEM((count, D), bf16),
            pltpu.VMEM((count, D), bf16),
            pltpu.VMEM((count, D), f32),
            pltpu.VMEM((count, D), f32),
            pltpu.VMEM((count, D), f32),
            pltpu.VMEM((count, TILE), bf16),
            pltpu.VMEM((count, TILE), bf16),
            pltpu.VMEM((H, 128, 384), bf16),
            pltpu.VMEM((count, 128), bf16),
            pltpu.VMEM((count, 128), bf16),
            pltpu.VMEM((count // SEQ, H, SEQ), f32),
            pltpu.VMEM((count // SEQ, 16, SEQ), f32),
            pltpu.VMEM((H, 2, 8, 128), f32),
            pltpu.VMEM((32, 128), f32),
            pltpu.VMEM((LANDINGS, 2, 4, 2, ROWS, COLS), bf16),
            pltpu.VMEM((LANDINGS, 4, 2, ROWS, COLS), bf16),
            pltpu.VMEM((LANDINGS, 4, ROWS, COLS), bf16),
            pltpu.VMEM((LANDINGS, 3, ROWS, COLS), bf16),
            pltpu.VMEM((3, 4, ROWS, COLS), bf16),
            pltpu.VMEM((10, 32, 128), f32),
            pltpu.SemaphoreType.DMA((PIECES, Gather.SLOTS)),
            pltpu.SemaphoreType.DMA((PIECES, Gather.SLOTS)),
            pltpu.SemaphoreType.DMA((Gather.SLOTS,)),
            pltpu.SemaphoreType.DMA((Gather.SLOTS,)),
            pltpu.SemaphoreType.DMA((PIECES, Reduce.SLOTS)),
            pltpu.SemaphoreType.DMA((PIECES, Reduce.SLOTS)),
            pltpu.SemaphoreType.DMA((SmallSum.SLOTS,)),
            pltpu.SemaphoreType.DMA((SmallSum.SLOTS,)),
            pltpu.SemaphoreType.REGULAR((LANDINGS, 6)),
            pltpu.SemaphoreType.DMA((4,)),
        ],
        compiler_params=pltpu.CompilerParams(collective_id=1, has_side_effects=True, vmem_limit_bytes=63 << 20),
    )(
        tokens,
        cotangent,
        lengths,
        norm_gain.reshape(1, -1),
        ffn_gain.reshape(1, -1),
        w_query,
        w_key,
        w_value,
        w_out,
        w_in,
        w_ffn_out,
        bias_table.T,
    )
    results = pl.pallas_call(
        deliver_kernel,
        out_shape=shapes,
        in_specs=[any_space] * len(shapes),
        out_specs=[any_space] * len(shapes),
        scratch_shapes=[pltpu.VMEM(shape.shape, shape.dtype) for shape in shapes]
        + [pltpu.SemaphoreType.DMA((2, len(shapes)))],
        compiler_params=pltpu.CompilerParams(vmem_limit_bytes=32 << 20),
    )(*results)
    output, grad_tokens, grad_one, grad_two, grad_table, *weight_grads = results
    group, groups = inner_groups()
    if group > 1:
        grad_table = lax.psum(grad_table, "dp", axis_index_groups=groups)
    grad_q, grad_k, grad_v, grad_o, grad_in, grad_ffn = (narrow(grad) for grad in weight_grads)
    return (
        output,
        grad_tokens,
        narrow(grad_one[0]),
        grad_q,
        grad_k,
        grad_v,
        grad_o,
        grad_table.T,
        narrow(grad_two[0]),
        grad_in,
        grad_ffn,
    )


def solution(mesh):
    rows, whole = P("dp", None), P("dp")
    return jax.shard_map(
        per_device,
        mesh=mesh,
        in_specs=(rows, rows, whole, rows, rows, rows, rows, P(), whole, rows, rows, rows),
        out_specs=(rows, rows, whole, rows, rows, rows, rows, P(), whole, rows, rows),
        check_vma=False,
    )
```

```python
from functools import partial

import jax
import jax.numpy as jnp
from jax import lax
from jax.experimental import pallas as pl
from jax.experimental.pallas import tpu as pltpu
from jax.sharding import PartitionSpec as P

D = 768
H = 12
NB = 32
SEQ = 512
FF = 3072
EPSILON = 1e-6
CUTOFFS = (12, 16, 23, 32, 46, 64, 91)
RANKS = 32
GROUPS = 3
TILES = 4
TILE = 768
MESH_ID = pl.DeviceIdType.MESH
f32, bf16 = jnp.float32, jnp.bfloat16

GROUP_PIECE, OUT_PIECE, PIECES = 0, 3, 12
FFN_PIECES, IN_PIECES = (4, 6, 8, 10), (5, 7, 9, 11)
ROWS, COLS = 48, 384
LANDINGS = 6


PLAN = {
    "S0": [("g", 0, "line")],
    "S1": [("g", 1, "line"), ("g", 0, "across")],
    "S2": [("g", 2, "line"), ("g", 1, "across"), ("g", 3, "line"), ("g", 0, "along")],
    "S3": [("g", 2, "across")],
    "S": [("g", 0, "finish")],
    "F0": [("g", 1, "along"), ("g", 3, "across"), ("g", 4, "line"), ("g", 5, "line")],
    "F1": [("g", 1, "finish")],
    "F2": [("g", 2, "along")],
    "F3": [("g", 3, "along"), ("g", 2, "finish")],
    "F4": [("g", 3, "finish"), ("g", 4, "across"), ("g", 5, "across"), ("g", 6, "line"), ("g", 7, "line")],
    "A": [("g", 4, "along"), ("g", 5, "along"), ("g", 4, "finish"), ("g", 6, "across"), ("g", 8, "line"), ("g", 5, "finish")],
    "T1": [("g", 7, "across"), ("g", 9, "line")],
    "T4": [("g", 6, "along"), ("g", 8, "across"), ("g", 10, "line")],
    "T5": [("g", 7, "along"), ("g", 6, "finish")],
    "T6": [("g", 9, "across"), ("g", 11, "line"), ("r", 0, "core"), ("g", 7, "finish")],
    "T7": [("r", 1, "core"), ("g", 8, "along"), ("g", 10, "across")],
    "T9": [("g", 8, "finish"), ("g", 9, "along")],
    "T11": [("g", 9, "finish"), ("g", 11, "across")],
    "T16": [("r", 0, "across"), ("r", 1, "across"), ("r", 2, "core"), ("r", 3, "core"), ("g", 10, "along"), ("g", 11, "along")],
    "T18": [("g", 10, "finish"), ("g", 11, "finish")],
    "T19": [("r", 0, "along"), ("r", 1, "along")],
    "T23": [("r", 2, "across"), ("r", 3, "across"), ("r", 4, "core"), ("r", 5, "core"), ("r", 0, "finish")],
    "T26": [("r", 2, "along"), ("r", 1, "finish")],
    "T27": [("r", 3, "along")],
    "B2": [("r", 2, "finish"), ("r", 4, "across"), ("r", 5, "across"), ("r", 6, "core"), ("r", 7, "core")],
    "B4": [("r", 8, "start")],
    "K0": [("r", 4, "along")],
    "K1": [("r", 3, "finish"), ("r", 5, "along")],
    "K2": [("r", 4, "finish"), ("r", 6, "across"), ("r", 7, "across"), ("r", 8, "core"), ("r", 9, "core")],
    "K4": [("r", 5, "finish"), ("r", 6, "along"), ("r", 7, "along")],
    "K5": [("r", 8, "across"), ("r", 9, "across"), ("r", 10, "core")],
    "L0": [("r", 6, "finish")],
    "L1": [("r", 8, "along"), ("r", 11, "core")],
    "E": [("r", 7, "finish"), ("r", 9, "along"), ("r", 10, "across"), ("r", 8, "finish"), ("r", 11, "across"), ("r", 9, "finish"), ("r", 10, "along"), ("r", 11, "along"), ("r", 10, "finish"), ("r", 11, "finish")],
}


def nt(a, b):
    return lax.dot_general(a, b, (((1,), (1,)), ((), ())), preferred_element_type=f32)


def nn(a, b):
    return jnp.dot(a, b, preferred_element_type=f32)


def tn(a, b):
    return lax.dot_general(a, b, (((0,), (0,)), ((), ())), preferred_element_type=f32)


def exact(a, b, dims=(((1,), (0,)), ((), ()))):
    return lax.dot_general(a, b, dims, precision=lax.Precision.HIGHEST, preferred_element_type=f32)


def part_of(index, size):
    return pl.ds(pl.multiple_of(index * size, size), size)


def place():
    me = lax.axis_index("dp")
    group = lax.axis_size("dp") // RANKS
    rank, low = me // group, me % group
    digits = dict(z=rank // 8, y=(rank // 4) % 2, x=(rank // 2) % 2, c=rank % 2)

    def device(**changed):
        d = {**digits, **changed}
        return ((((d["z"] * 2 + d["y"]) * 2 + d["x"]) * 2 + d["c"]) * group + low,)

    return digits, device


def partners(digits, device):
    line = [device(z=(digits["z"] + step) % 4) for step in (1, 2, 3)]
    return line + [device(**{axis: 1 - digits[axis]}) for axis in "yxc"]


def greet(digits, device):
    barrier = pltpu.get_barrier_semaphore()
    others = partners(digits, device)
    for other in others:
        pl.semaphore_signal(barrier, inc=1, device_id=other, device_id_type=MESH_ID)
    return lambda: pl.semaphore_wait(barrier, len(others))


class Transfers:
    def __init__(self, send_sems, recv_sems, digits, device):
        self.send_sems, self.recv_sems, self.digits, self.device = send_sems, recv_sems, digits, device

    def flip(self, *axes):
        return {axis: 1 - self.digits[axis] for axis in axes}

    def copy(self, slot):
        source, target, device_id = self.spec(slot)
        return pltpu.make_async_remote_copy(
            src_ref=source,
            dst_ref=target,
            send_sem=self.send_sems.at[slot],
            recv_sem=self.recv_sems.at[slot],
            device_id=device_id,
            device_id_type=MESH_ID,
        )

    def go(self, *slots):
        for slot in slots:
            self.copy(slot).start()

    def arrived_at(self, slot, landing):
        pltpu.make_async_remote_copy(
            src_ref=landing,
            dst_ref=landing,
            send_sem=self.send_sems.at[slot],
            recv_sem=self.recv_sems.at[slot],
            device_id=self.device(c=1 - self.digits["c"]),
            device_id_type=MESH_ID,
        ).wait_recv()

    def arrived(self, *slots):
        for slot in slots:
            self.arrived_at(slot, self.landing(slot))

    def sent(self, count):
        for slot in range(count):
            self.copy(slot).wait_send()


class Gather(Transfers):
    SLOTS = 10

    def __init__(self, full, send_sems, recv_sems, order, digits, device):
        super().__init__(send_sems, recv_sems, digits, device)
        self.full = full
        self.first, self.second = order

    def line_of(self, *flipped):
        d = {**self.digits, **self.flip(*flipped)}
        return self.full.at[:, d["y"], d["x"], d["c"]]

    def block_of(self, z):
        d = self.digits
        return self.full.at[z, d["y"], d["x"], d["c"]]

    def spec(self, slot):
        z, a, b = self.digits["z"], self.first, self.second
        if slot < 3:
            own = self.block_of(z)
            return own, own, self.device(z=(z + slot + 1) % 4)
        flipped, towards = ((), (), (), (a,), (a,), (b,), (b, a))[slot - 3], (a, b, "c", b, "c", "c", "c")[slot - 3]
        line = self.line_of(*flipped)
        return line, line, self.device(**self.flip(towards))

    def landing(self, slot):
        a, b = self.first, self.second
        if slot < 3:
            return self.block_of((self.digits["z"] + 3 - slot) % 4)
        return self.line_of(*((a,), (b,), ("c",), (b, a), ("c", a), ("c", b), ("c", b, a))[slot - 3])

    def start(self):
        self.go(0, 1, 2)

    def line(self):
        self.arrived(0, 1, 2)
        self.go(3, 4, 5)

    def across(self):
        self.arrived(3)
        self.go(6, 7)

    def along(self):
        self.arrived(4)
        self.go(8)
        self.arrived(6)
        self.go(9)

    def finish(self):
        self.arrived(5, 7, 8, 9)
        self.sent(self.SLOTS)


class PlaneGather(Gather):
    def __init__(self, full, send_sems, recv_sems, order, digits, device, plane):
        super().__init__(full, send_sems, recv_sems, order, digits, device)
        self.plane = plane

    def spec(self, slot):
        if slot < 3:
            line = self.line_of()
            return line, line, self.device(z=(self.digits["z"] + slot + 1) % 4)
        return super().spec(slot)

    def start(self):
        @pl.when(self.digits["z"] == self.plane)
        def _():
            self.go(0, 1, 2)

    def line(self):
        z = self.digits["z"]
        for slot in range(3):

            @pl.when(z == (self.plane + slot + 1) % 4)
            def _(slot=slot):
                line = self.line_of()
                self.arrived_at(slot, line)

        self.go(3, 4, 5)

    def sent(self, count):
        for slot in range(3, count):
            self.copy(slot).wait_send()

        @pl.when(self.digits["z"] == self.plane)
        def _():
            for slot in range(3):
                self.copy(slot).wait_send()


class Reduce(Transfers):
    SLOTS = 7

    def __init__(self, parts, received, send_sems, recv_sems, order, digits, device, credits=None, grants=None):
        super().__init__(send_sems, recv_sems, digits, device)
        self.parts = parts
        self.from_core, self.from_first, self.from_second, self.from_line = received
        self.first, self.second = order
        self.credits, self.grants = credits, grants

    def half(self, first, c):
        if self.first == "y":
            return self.parts.at[:, first, :, c]
        return self.parts.at[:, :, first, c]

    def at(self, z, first, second):
        d = {self.first: first, self.second: second}
        return (z, d["y"], d["x"], self.digits["c"])

    def spec(self, slot):
        d, a, b = self.digits, self.first, self.second
        if slot < 2:
            side = (1 - d[a], d[a])[slot]
            return self.half(side, 1 - d["c"]), self.from_core.at[slot], self.device(**self.flip("c"))
        if slot == 2:
            return self.half(1 - d[a], d["c"]), self.from_first, self.device(**self.flip(a))
        if slot == 3:
            q = {**d, **self.flip(b)}
            return self.parts.at[:, q["y"], q["x"], d["c"]], self.from_second, self.device(**self.flip(b))
        z = (d["z"] + slot - 3) % 4
        return self.parts.at[z, d["y"], d["x"], d["c"]], self.from_line.at[slot - 4], self.device(z=z)

    def landing(self, slot):
        if slot < 2:
            return self.from_core.at[slot]
        if slot < 4:
            return (self.from_first, self.from_second)[slot - 2]
        return self.from_line.at[slot - 4]

    def spend(self, *kinds):
        if self.credits is not None:
            for kind in kinds:
                pl.semaphore_wait(self.credits.at[kind], 1)

    def grant(self):
        d = self.digits
        if self.grants is not None:
            others = [self.device(**self.flip(axis)) for axis in ("c", self.first, self.second)]
            others += [self.device(z=(d["z"] + 4 - step) % 4) for step in (1, 2, 3)]
            for kind, other in enumerate(others):
                pl.semaphore_signal(self.grants.at[kind], inc=1, device_id=other, device_id_type=MESH_ID)

    def add(self, first, second, received):
        d = {self.first: first, self.second: slice(None) if second is None else second}
        index = (slice(None), d["y"], d["x"], self.digits["c"])
        self.parts[index] = self.parts[index] + received

    def start(self):
        self.spend(0)
        self.go(0, 1)

    def core(self):
        d, a = self.digits, self.first
        self.arrived(0)
        self.add(1 - d[a], None, self.from_core[0])
        self.spend(1)
        self.go(2)
        self.arrived(1)
        self.add(d[a], None, self.from_core[1])

    def across(self):
        d, a, b = self.digits, self.first, self.second
        self.arrived(2)
        self.add(d[a], 1 - d[b], self.from_first[:, 1 - d[b]])
        self.spend(2)
        self.go(3)
        self.add(d[a], d[b], self.from_first[:, d[b]])

    def along(self):
        d, a, b = self.digits, self.first, self.second
        self.arrived(3)
        self.add(d[a], d[b], self.from_second[...])
        self.spend(3, 4, 5)
        self.go(4, 5, 6)

    def finish(self, store):
        d = self.digits
        total = self.parts[d["z"], d["y"], d["x"], d["c"]].astype(f32)
        for slot in (4, 5, 6):
            self.arrived(slot)
            total = total + self.from_line[slot - 4].astype(f32)
        store(total)
        self.sent(self.SLOTS)
        self.grant()


class PlaneReduce(Reduce):
    def __init__(self, parts, received, plane_in, send_sems, recv_sems, order, digits, device, credits, grants, plane):
        super().__init__(parts, received, send_sems, recv_sems, order, digits, device, credits, grants)
        self.plane_in, self.plane = plane_in, plane

    def along(self):
        d, a, b = self.digits, self.first, self.second
        self.arrived(3)
        self.add(d[a], d[b], self.from_second[...])
        self.spend(3, 4, 5)
        for step in (1, 2, 3):

            @pl.when(d["z"] == (self.plane + step) % 4)
            def _(step=step):
                self.to_plane(step).start()

    def to_plane(self, step):
        d = self.digits
        return pltpu.make_async_remote_copy(
            src_ref=self.parts.at[:, d["y"], d["x"], d["c"]],
            dst_ref=self.plane_in.at[step - 1],
            send_sem=self.send_sems.at[3 + step],
            recv_sem=self.recv_sems.at[3 + step],
            device_id=self.device(z=self.plane),
            device_id_type=MESH_ID,
        )

    def finish(self, store):
        d = self.digits

        @pl.when(d["z"] == self.plane)
        def _():
            total = self.parts[:, d["y"], d["x"], d["c"]].astype(f32)
            for step in (1, 2, 3):
                self.arrived_at(3 + step, self.plane_in.at[step - 1])
                total = total + self.plane_in[step - 1].astype(f32)
            store(total)

        for step in (1, 2, 3):

            @pl.when(d["z"] == (self.plane + step) % 4)
            def _(step=step):
                self.to_plane(step).wait_send()

        for slot in range(4):
            self.copy(slot).wait_send()
        self.grant()


class SmallSum(Transfers):
    SLOTS = 6

    def __init__(self, total, buffer, send_sems, recv_sems, digits, device):
        super().__init__(send_sems, recv_sems, digits, device)
        self.total, self.buffer = total, buffer

    def spec(self, slot):
        z = self.digits["z"]
        if slot < 3:
            return self.buffer.at[2 * slot], self.buffer.at[2 * slot + 1], self.device(**self.flip("cxy"[slot]))
        mine = self.buffer.at[6 + z]
        return mine, mine, self.device(z=(z + slot - 2) % 4)

    def landing(self, slot):
        if slot < 3:
            return self.buffer.at[2 * slot + 1]
        return self.buffer.at[6 + (self.digits["z"] + 6 - slot) % 4]

    def start(self, slot):
        if slot < 3:
            self.buffer[2 * slot] = self.total[...]
            self.go(slot)
        else:
            self.buffer[6 + self.digits["z"]] = self.total[...]
            self.go(3, 4, 5)

    def finish(self, slot):
        if slot < 3:
            self.arrived(slot)
            self.total[...] = self.total[...] + self.buffer[2 * slot + 1]
        else:
            self.arrived(3, 4, 5)
            self.total[...] = (self.buffer[6] + self.buffer[7]) + (self.buffer[8] + self.buffer[9])
            self.sent(self.SLOTS)


def pack(block):
    rows = block.reshape(-1, 8, 2 * COLS)
    return jnp.concatenate([rows[:, :, :COLS], rows[:, :, COLS:]], axis=1).reshape(-1, COLS)


def unpack(block):
    rows = block.reshape(-1, 2, 8, COLS)
    return jnp.concatenate([rows[:, 0].reshape(-1, COLS), rows[:, 1].reshape(-1, COLS)], axis=1)


def unpack_piece(piece, target):
    def plane(z, carry):
        target[part_of(z, 192), :] = unpack(piece[z].astype(f32).reshape(8 * ROWS, COLS)).astype(bf16)
        return carry

    lax.fori_loop(0, 4, plane, 0)


def pack_piece(piece, z, grad):
    piece[z] = pack(grad).astype(bf16).reshape(2, 2, 2, ROWS, COLS)


def bucket_of(offsets):
    distance = jnp.abs(offsets)
    coarse = jnp.full_like(distance, 8)
    for cutoff in CUTOFFS:
        coarse = coarse + (distance >= cutoff).astype(jnp.int32)
    return jnp.where(distance < 8, distance, coarse) + jnp.where(offsets > 0, 16, 0)


def strip_onehot(shift):
    column = lax.broadcasted_iota(jnp.int32, (128, 512), 1)
    column = jnp.where(column >= shift, column - shift, column - shift + 512)
    offset = jnp.where(column < 384, 128 - column, 640 - column)
    return bucket_of(offset) == lax.broadcasted_iota(jnp.int32, (128, 512), 0)


def make_strips(table_t, strips):
    line = nn(table_t[...], strip_onehot(0).astype(bf16)[:NB])
    for head in range(H):
        rows = jnp.broadcast_to(line[head : head + 1], (128, 512))
        strips[head] = pltpu.roll(rows, 0, 1, stride=1, stride_axis=0)[:, :384].astype(strips.dtype)


def strip_sums(strip):
    wide = jnp.concatenate([strip, jnp.zeros((128, 128), f32)], axis=1)
    total = wide[:8]
    for r in range(1, 16):
        total = total + pltpu.roll(wide[8 * r : 8 * r + 8], 512 - 8 * r, 1)
    return total


def table_sums(sums, far_sums):
    row = lax.broadcasted_iota(jnp.int32, (8 * H, 8 * H), 0)
    column = lax.broadcasted_iota(jnp.int32, (8 * H, 8 * H), 1)
    turned = exact((column == (row // 8) * 8 + 7 - row % 8).astype(f32), sums)
    lines = [
        jnp.sum(pltpu.roll(turned[8 * h : 8 * h + 8], 0, 1, stride=1, stride_axis=0), axis=0, keepdims=True)
        for h in range(H)
    ]
    lines.append(jnp.zeros((16 - H, 512), f32))
    table = exact(jnp.concatenate(lines, axis=0), strip_onehot(7).astype(f32), (((1,), (1,)), ((), ())))
    head = lax.broadcasted_iota(jnp.int32, (16, 128), 0)
    bucket = lax.broadcasted_iota(jnp.int32, (16, 128), 1)
    for side, index in ((0, 15), (1, 31)):
        rows = [jnp.sum(far_sums[h, side], axis=0, keepdims=True) for h in range(H)] + [jnp.zeros((16 - H, 128), f32)]
        total = jnp.sum(jnp.concatenate(rows, axis=0), axis=1, keepdims=True)
        table = table + jnp.where((bucket == index) & (head < H), total, 0.0)
    return table


def make_marks(lengths, key_marks, query_marks):
    position = lax.broadcasted_iota(jnp.int32, (SEQ, 128), 0)
    lane = lax.broadcasted_iota(jnp.int32, (SEQ, 128), 1)
    for row in range(key_marks.shape[0] // SEQ):
        segment = jnp.zeros((SEQ, 128), jnp.int32)
        end = 0
        for k in range(1, 5):
            end = end + lengths[row, k]
            segment = segment + (position >= end).astype(jnp.int32)
        own = segment == lane
        rows = slice(row * SEQ, (row + 1) * SEQ)
        key_marks[rows, :] = jnp.where(own, 1.0, 0.0).astype(bf16)
        query_marks[rows, :] = jnp.where(own | (lane >= 5), 0.0, -1e30).astype(bf16)


def lane_mask(h):
    lane = lax.broadcasted_iota(jnp.int32, (1, 128), 1)
    return lane < 64 if h == 0 else lane >= 64


def biased(raw, strip, half):
    low, high = strip[0:1, 383:384].astype(f32), strip[127:128, 0:1].astype(f32)
    rows = []
    for bj in range(4):
        blocks = []
        for bi in (0, 1):
            d = bj - bi - 2 * half
            block = raw[128 * bj : 128 * (bj + 1), 128 * bi : 128 * (bi + 1)]
            if d <= -2:
                block = block + low
            elif d >= 2:
                block = block + high
            else:
                block = block + strip[:, 128 * (1 - d) : 128 * (2 - d)].astype(f32)
            blocks.append(block)
        rows.append(jnp.concatenate(blocks, axis=1))
    return jnp.concatenate(rows, axis=0)


def heads_of(ref, rows, which, pair):
    return ref[rows, pl.ds(pl.multiple_of(which * 256 + pair * 128, 128), 128)]


def raw_scores(q2, k2, key_marks, query_marks):
    queries = jnp.concatenate([q2, query_marks], axis=1)
    return [nt(jnp.concatenate([jnp.where(lane_mask(h), k2, 0), key_marks], axis=1), queries) for h in range(2)]


def attend(qkv, key_marks, query_marks, strips, mix, lse, group, pair):
    count = mix.shape[0] // SEQ
    raws, values = [], []
    for row in range(count):
        rows = slice(row * SEQ, (row + 1) * SEQ)
        q2, k2, v2 = (heads_of(qkv, rows, which, pair) for which in range(3))
        raws.append(raw_scores(q2, k2, key_marks[rows, :], query_marks[rows, :]))
        values.append(v2.T)
    for row in range(count):
        outs = []
        for h in range(2):
            head = (group * 2 + pair) * 2 + h
            halves = []
            for half in range(2):
                span = slice(256 * half, 256 * half + 256)
                scores = biased(raws[row][h][:, span], strips[head], half)
                peak = jnp.max(scores, axis=0, keepdims=True)
                expo = jnp.exp(scores - peak)
                total = jnp.sum(expo, axis=0, keepdims=True)
                lse[row, pl.ds(head, 1), span] = peak + jnp.log(total)
                halves.append(nn(values[row][64 * h : 64 * h + 64], expo.astype(bf16)) * (1.0 / total))
            outs.append(jnp.concatenate(halves, axis=1))
        mix[row * SEQ : (row + 1) * SEQ, part_of(group * 2 + pair, 128)] = jnp.concatenate(outs, axis=0).T.astype(bf16)


def attend_back(qkv, gmix, key_marks, query_marks, strips, lse, inner, strip_grads, far_sums, group, pair):
    count = gmix.shape[0] // SEQ
    lanes = part_of(group * 2 + pair, 128)
    held = []
    for row in range(count):
        rows = slice(row * SEQ, (row + 1) * SEQ)
        q2, k2, v2 = (heads_of(qkv, rows, which, pair) for which in range(3))
        g2 = gmix[rows, lanes]
        raws = raw_scores(q2, k2, key_marks[rows, :], query_marks[rows, :])
        held.append((q2, k2.T, v2, g2, raws))
    for row in range(count):
        rows = slice(row * SEQ, (row + 1) * SEQ)
        q2, k2t, v2, g2, raws = held[row]
        grads = [nt(jnp.where(lane_mask(h), v2, 0), g2) for h in range(2)]
        grad_v, grad_k, grad_q = 0.0, 0.0, []
        for h in range(2):
            head = (group * 2 + pair) * 2 + h
            mask = lane_mask(h)
            near, far = {}, ([], [])
            probs_low, scores_low = [], []
            for half in range(2):
                span = slice(256 * half, 256 * half + 256)
                probs = jnp.exp(biased(raws[h][:, span], strips[head], half) - lse[row, pl.ds(head, 1), span])
                grad = probs * (grads[h][:, span] - inner[row, pl.ds(head, 1), span])
                probs_low.append(probs.astype(bf16))
                scores_low.append(grad.astype(bf16))
                for bi in (0, 1):
                    for bj in range(4):
                        d = bj - bi - 2 * half
                        block = grad[128 * bj : 128 * (bj + 1), 128 * bi : 128 * (bi + 1)]
                        if abs(d) <= 1:
                            near[d] = near[d] + block if d in near else block
                        else:
                            far[d > 0].append(jnp.sum(block.reshape(16, 8, 128), axis=0))
            strip_rows = part_of(group * 2 + pair, 128)
            for d, block in near.items():
                strip_grads[strip_rows, 384 * h + 128 * (1 - d) : 384 * h + 128 * (2 - d)] += block
            for side in (0, 1):
                far_sums[head, side] += sum(far[side][1:], far[side][0])
            grad_v = grad_v + nn(jnp.concatenate(probs_low, axis=1), jnp.where(mask, g2, 0))
            low = jnp.concatenate(scores_low, axis=1)
            grad_k = grad_k + nn(low, jnp.where(mask, q2, 0))
            grad_q.append(nn(k2t[64 * h : 64 * h + 64], low))
        for which, value in enumerate((jnp.concatenate(grad_q, axis=0).T, grad_k, grad_v)):
            qkv[rows, pl.ds(pl.multiple_of(which * 256 + pair * 128, 128), 128)] = value.astype(bf16)


def inner_sums(gmix, mix):
    product = gmix.astype(f32) * mix.astype(f32)
    high = product.astype(bf16)
    low = (product - high.astype(f32)).astype(bf16)
    feature = lax.broadcasted_iota(jnp.int32, (16, D), 1)
    first = lax.broadcasted_iota(jnp.int32, (16, D), 0) * 64
    own = jnp.where((feature >= first) & (feature < first + 64), 1.0, 0.0).astype(bf16)
    return nt(own, high) + nt(own, low)


def inv_rms(x):
    return lax.rsqrt(jnp.mean(x * x, axis=-1, keepdims=True) + EPSILON)


def norm_back(grad, x, gain):
    s = inv_rms(x)
    gg = grad * gain
    return s * gg - x * (s * s * s * jnp.mean(gg * x, axis=-1, keepdims=True)), jnp.sum(grad * x * s, axis=0, keepdims=True)


def gelu_both(x):
    cdf = 0.5 + 0.5 * lax.erf(x * 0.7071067811865476)
    return x * cdf, cdf + x * (jnp.exp(x * x * -0.5) * 0.3989422804014327)


def gain_line(gains, which):
    blocks = gains[...].reshape(8 * RANKS, 128).astype(bf16)
    lane = lax.broadcasted_iota(jnp.int32, (128, D), 1)
    spread = nn(blocks, (lane % 24 == lax.broadcasted_iota(jnp.int32, (128, D), 0)).astype(bf16))
    row = lax.broadcasted_iota(jnp.int32, (8 * RANKS, D), 0)
    column = lax.broadcasted_iota(jnp.int32, (8 * RANKS, D), 1)
    return jnp.sum(jnp.where(row == (column // 24) * 8 + which, spread, 0.0), axis=0, keepdims=True)


def run_at(step, plan):
    for when, stages in plan.items():

        @pl.when(step == when)
        def _(stages=stages):
            for stage in stages:
                stage()


def layer_kernel(
    tokens_hbm, cot_hbm, lengths, norm_gain, ffn_gain, w_query, w_key, w_value, w_out, w_in, w_ffn, table_t,
    out_hbm, gtok_hbm, grad_one, grad_two, grad_table, grad_q, grad_k, grad_v, grad_o, grad_in, grad_ffn,
    pieces, gains, weights, win, wff, qkv, mix, normed, tokens, cot, resid, out_sum, grad_sum, act, grad_inner,
    strips, key_marks, query_marks, lse, inner, far_sums, small, from_core, from_first, from_second, from_line,
    plane_in, small_buffer,
    gather_send, gather_recv, gain_send, gain_recv, reduce_send, reduce_recv, small_send, small_recv, credits, local_sems,
):
    count = tokens.shape[0]
    digits, device = place()
    me = (digits["z"], digits["y"], digits["x"], digits["c"])
    all_here = greet(digits, device)

    load_tokens = pltpu.make_async_copy(tokens_hbm, tokens, local_sems.at[0])
    load_tokens.start()
    load_cot = pltpu.make_async_copy(cot_hbm, cot, local_sems.at[1])
    load_cot.start()

    orders = ("xy", "yx")
    gain_gather = Gather(gains, gain_send, gain_recv, "xy", digits, device)
    gathers = []
    for i in range(PIECES):
        common = (pieces.at[i], gather_send.at[i], gather_recv.at[i], orders[i % 2], digits, device)
        gathers.append(PlaneGather(*common, FFN_PIECES.index(i)) if i in FFN_PIECES else Gather(*common))
    order = [i for t in range(TILES) for i in (IN_PIECES[t], FFN_PIECES[t])] + [OUT_PIECE, 0, 1, 2]
    reduces = []
    for n, i in enumerate(order):
        slot = n % LANDINGS
        received = (from_core.at[slot], from_first.at[slot], from_second.at[slot], from_line.at[slot])
        sems = (reduce_send.at[n], reduce_recv.at[n], orders[n % 2], digits, device)
        limits = (credits.at[slot] if n >= LANDINGS else None, credits.at[slot] if n + LANDINGS < PIECES else None)
        if i in FFN_PIECES:
            reduces.append(PlaneReduce(pieces.at[i], received, plane_in, *sems, *limits, FFN_PIECES.index(i)))
        else:
            reduces.append(Reduce(pieces.at[i], received, *sems, *limits))

    def store_in(t):
        def store(total):
            grad_in[:, TILE * t : TILE * (t + 1)] = unpack(total)

        return store

    def store_ffn(total):
        for i in range(4):
            grad_ffn[ROWS * (i // 2) : ROWS * (i // 2 + 1), COLS * (i % 2) : COLS * (i % 2 + 1)] = total[i]

    def store_out(total):
        grad_o[...] = unpack(total)

    def store_group(g):
        def store(total):
            block = unpack(total)
            for which, target in enumerate((grad_q, grad_k, grad_v)):
                target[:, 256 * g : 256 * (g + 1)] = block[:, 256 * which : 256 * (which + 1)]

        return store

    stores = [store for t in range(TILES) for store in (store_in(t), store_ffn)] + [store_out]
    stores += [store_group(g) for g in range(GROUPS)]

    def stage(kind, n, name):
        if kind == "r":
            return partial(reduces[n].finish, stores[n]) if name == "finish" else getattr(reduces[n], name)
        if name == "finish" and n <= OUT_PIECE:
            return partial(arrive, n)
        return getattr(gathers[n], name)

    def arrive(n):
        gathers[n].finish()
        unpack_piece(pieces.at[n], weights.at[n])

    def plan(letter):
        return {int(key[1:]): [stage(*entry) for entry in PLAN[key]] for key in PLAN if key[0] == letter}

    def run(stages):
        for each in stages:
            each()

    for g in range(GROUPS):
        span = slice(256 * g, 256 * g + 256)
        block = jnp.concatenate([w[:, span] for w in (w_query, w_key, w_value)], axis=1)
        pieces[(GROUP_PIECE + g, *me)] = pack(block.astype(f32)).astype(bf16)
    gains[me] = jnp.zeros((8, 128), f32)
    gains[(*me, slice(0, 1), slice(0, 24))] = norm_gain[...].astype(f32)
    gains[(*me, slice(1, 2), slice(0, 24))] = ffn_gain[...].astype(f32)
    all_here()
    gathers[0].start()
    gain_gather.start()
    gathers[1].start()
    gathers[2].start()
    pieces[(OUT_PIECE, *me)] = pack(w_out[...].astype(f32)).astype(bf16)
    gathers[3].start()
    for t in range(TILES):

        @pl.when(digits["z"] == t)
        def _(t=t):
            for i in range(4):
                block = w_ffn[ROWS * (i // 2) : ROWS * (i // 2 + 1), COLS * (i % 2) : COLS * (i % 2 + 1)]
                pieces[FFN_PIECES[t], i, digits["y"], digits["x"], digits["c"]] = block

        gathers[FFN_PIECES[t]].start()
        pieces[(IN_PIECES[t], *me)] = pack(w_in[:, TILE * t : TILE * (t + 1)].astype(f32)).astype(bf16)
        gathers[IN_PIECES[t]].start()

    make_marks(lengths, key_marks, query_marks)
    make_strips(table_t, strips)
    for i, gain_stage in enumerate((gain_gather.line, gain_gather.across, gain_gather.along, gain_gather.finish)):
        run([stage(*entry) for entry in PLAN[f"S{i}"]])
        gain_stage()
    gain_one, gain_two = gain_line(gains, 0), gain_line(gains, 1)
    load_tokens.wait()

    def norm_one(i, carry):
        rows = part_of(i, 256)
        x = tokens[rows, :].astype(f32)
        normed[rows, :] = (x * inv_rms(x) * gain_one).astype(bf16)
        return carry

    lax.fori_loop(0, count // 256, norm_one, 0)
    run([stage(*entry) for entry in PLAN["S"]])

    forward_plan = plan("F")

    def forward_group(g, carry):
        qkv[g] = nn(normed[...], weights[GROUP_PIECE + g]).astype(bf16)

        def forward(pair, carry):
            attend(qkv.at[g], key_marks, query_marks, strips, mix, lse, g, pair)
            run_at(2 * g + pair, forward_plan)
            return carry

        lax.fori_loop(0, 2, forward, 0)
        return carry

    lax.fori_loop(0, GROUPS, forward_group, 0)

    def after_attention(i, carry):
        rows = part_of(i, 512)
        r = tokens[rows, :].astype(f32) + nn(mix[rows, :], weights[OUT_PIECE])
        resid[rows, :] = r
        normed[rows, :] = (r * inv_rms(r) * gain_two).astype(bf16)
        return carry

    lax.fori_loop(0, count // 512, after_attention, 0)
    load_cot.wait()
    run([stage(*entry) for entry in PLAN["A"]])

    ffn_plan = plan("T")
    width = 256

    def tile_piece(t, which):
        return pieces.at[4 + 2 * t + which]

    def ffn_tile(t, carry):
        unpack_piece(tile_piece(t, 1), win)
        for b in range(8):
            for i in range(4):
                rows = slice(96 * b + ROWS * (i // 2), 96 * b + ROWS * (i // 2 + 1))
                block = pieces[4 + 2 * t, i, b // 4, (b // 2) % 2, b % 2]
                wff[rows, COLS * (i % 2) : COLS * (i % 2 + 1)] = block

        def columns(w, carry):
            span = part_of(w, width)
            ffn_in = nn(normed[...], win[:, span])
            grad_act = nt(cot[...], wff[span, :])
            value, slope = gelu_both(ffn_in)
            act[:, span] = value.astype(bf16)
            grad_inner[:, span] = (slope * grad_act).astype(bf16)
            run_at(7 * t + w, ffn_plan)
            return carry

        lax.fori_loop(0, TILE // width, columns, 0)

        for i in range(2):
            rows = slice(i * count // 2, (i + 1) * count // 2)
            value = nn(act[rows, :], wff[...])
            out_sum[rows, :] = jnp.where(t == 0, resid[rows, :], out_sum[rows, :]) + value

        run_at(7 * t + 3, ffn_plan)

        for i in range(2):
            rows = slice(i * count // 2, (i + 1) * count // 2)
            value = nt(grad_inner[rows, :], win[...])
            grad_sum[rows, :] = jnp.where(t == 0, 0.0, grad_sum[rows, :]) + value

        run_at(7 * t + 4, ffn_plan)
        grad = tn(normed[...], grad_inner[...])
        for z in range(4):
            pack_piece(tile_piece(t, 1), z, grad[192 * z : 192 * (z + 1)])
        run_at(t, {k: [reduces[2 * k].start] for k in range(TILES)})
        run_at(7 * t + 5, ffn_plan)
        grad = tn(act[...], cot[...]).astype(bf16)
        for b in range(8):
            for i in range(4):
                block = grad[96 * b + ROWS * (i // 2) : 96 * b + ROWS * (i // 2 + 1), COLS * (i % 2) : COLS * (i % 2 + 1)]
                pieces[4 + 2 * t, i, b // 4, (b // 2) % 2, b % 2] = block
        run_at(t, {k: [reduces[2 * k + 1].start] for k in range(TILES)})
        run_at(7 * t + 6, ffn_plan)
        return carry

    lax.fori_loop(0, TILES, ffn_tile, 0)

    before_plan = plan("B")
    small[...] = jnp.zeros(small.shape, f32)

    def spread_line(row, line):
        for j in range(D // 128):
            small[row + j : row + j + 1, :] += line[:, 128 * j : 128 * (j + 1)]

    def before_back(i, carry):
        rows = part_of(i, 256)
        act[rows, :] = out_sum[rows, :].astype(bf16)
        into, gain_sum = norm_back(grad_sum[rows, :], resid[rows, :], gain_two)
        spread_line(6, gain_sum)
        grad = cot[rows, :].astype(f32) + into
        grad_sum[rows, :] = grad
        low = grad.astype(bf16)
        cot[rows, :] = low
        gmix = nt(low, weights[OUT_PIECE]).astype(bf16)
        inner[i // 2, :, part_of(i % 2, 256)] = inner_sums(gmix, mix[rows, :])
        x = tokens[rows, :].astype(f32)
        grad_inner[rows, :] = (x * inv_rms(x) * gain_one).astype(bf16)
        normed[rows, :] = gmix
        run_at(i, before_plan)
        return carry

    lax.fori_loop(0, count // 256, before_back, 0)
    store_output = pltpu.make_async_copy(act, out_hbm, local_sems.at[2])
    store_output.start()
    out_sum[...] = jnp.zeros(out_sum.shape, f32)
    far_sums[...] = jnp.zeros(far_sums.shape, f32)
    grad = tn(mix[...], cot[...])
    for z in range(4):
        pack_piece(pieces.at[OUT_PIECE], z, grad[192 * z : 192 * (z + 1)])
    run(before_plan.get(4, []))
    back_plan = plan("K")

    def back_group(g, carry):
        def back(pair, carry):
            attend_back(qkv.at[g], normed, key_marks, query_marks, strips, lse, inner, out_sum, far_sums, g, pair)
            run_at(2 * g + pair, back_plan)
            return carry

        lax.fori_loop(0, 2, back, 0)
        grad = tn(grad_inner[...], qkv[g])
        for z in range(4):
            pack_piece(pieces.at[GROUP_PIECE + g], z, grad[192 * z : 192 * (z + 1)])
        run_at(g, {k: [reduces[9 + k].start] for k in range(GROUPS)})
        return carry

    lax.fori_loop(0, GROUPS, back_group, 0)
    last_plan = plan("L")

    def last(i, carry):
        rows = part_of(i, 512)
        grad = nt(qkv[0, rows, :], weights[0]) + nt(qkv[1, rows, :], weights[1]) + nt(qkv[2, rows, :], weights[2])
        into, gain_sum = norm_back(grad, tokens[rows, :].astype(f32), gain_one)
        spread_line(0, gain_sum)
        grad_sum[rows, :] = grad_sum[rows, :] + into
        run_at(i, last_plan)
        return carry

    lax.fori_loop(0, count // 512, last, 0)
    store_gtok = pltpu.make_async_copy(grad_sum, gtok_hbm, local_sems.at[3])
    store_gtok.start()
    for pair in range(H // 2):
        for h in range(2):
            head = 2 * pair + h
            strip = out_sum[128 * pair : 128 * pair + 128, 384 * h : 384 * h + 384]
            resid[8 * head : 8 * head + 8, :512] = strip_sums(strip)
    small[16:32, :] = table_sums(resid[: 8 * H, :512], far_sums)
    sums = SmallSum(small, small_buffer, small_send, small_recv, digits, device)
    tail = [stage(*entry) for entry in PLAN["E"]]
    for slot in range(4):
        sums.start(slot)
        if tail:
            tail.pop(0)()
        sums.finish(slot)
    for target, row in ((grad_one, 0), (grad_two, 6)):
        line = jnp.concatenate([small[row + j : row + j + 1, :] for j in range(D // 128)], axis=1)
        rank = (lax.axis_index("dp") // (lax.axis_size("dp") // RANKS)).astype(jnp.int32)
        own = pltpu.roll(jnp.broadcast_to(line, (8, D)), (D - 24 * rank) % D, 1)
        target[...] = own[0:1, :24]
    grad_table[...] = small[16 : 16 + H, :NB]
    run(tail)
    store_output.wait()
    store_gtok.wait()


def deliver_kernel(*refs):
    count = (len(refs) - 1) // 3
    sources, targets, held, sems = refs[:count], refs[count : 2 * count], refs[2 * count : 3 * count], refs[-1]
    loads = [pltpu.make_async_copy(sources[i], held[i], sems.at[0, i]) for i in range(count)]
    stores = [pltpu.make_async_copy(held[i], targets[i], sems.at[1, i]) for i in range(count)]
    for load in loads:
        load.start()
    for load, store in zip(loads, stores):
        load.wait()
        store.start()
    for store in stores:
        store.wait()


def inner_groups():
    total = lax.axis_size("dp")
    group = total // RANKS
    return group, [list(range(i * group, (i + 1) * group)) for i in range(RANKS)]


def widen(block):
    group, groups = inner_groups()
    if group == 1:
        return block
    return lax.all_gather(block, "dp", axis=0, tiled=True, axis_index_groups=groups)


def narrow(block):
    group, groups = inner_groups()
    if group == 1:
        return block
    return lax.psum_scatter(block, "dp", scatter_dimension=0, tiled=True, axis_index_groups=groups)


def per_device(
    tokens, lengths, norm_gain, w_query, w_key, w_value, w_out, bias_table, ffn_gain, w_in, w_ffn_out, cotangent
):
    count = tokens.shape[0]
    norm_gain, ffn_gain, w_query, w_key, w_value, w_out, w_in, w_ffn_out = (
        widen(w) for w in (norm_gain, ffn_gain, w_query, w_key, w_value, w_out, w_in, w_ffn_out)
    )
    any_space = pl.BlockSpec(memory_space=pl.ANY)
    vmem = pl.BlockSpec(memory_space=pltpu.VMEM)
    smem = pl.BlockSpec(memory_space=pltpu.SMEM)
    full = (4, 2, 2, 2)
    out = jax.ShapeDtypeStruct
    shapes = [out((count, D), bf16), out((count, D), f32), out((1, 24), f32), out((1, 24), f32), out((H, NB), f32)]
    shapes += [out((24, D), f32)] * 4 + [out((24, FF), f32), out((96, D), f32)]
    results = pl.pallas_call(
        layer_kernel,
        out_shape=shapes,
        in_specs=[any_space] * 2 + [smem] + [vmem] * 9,
        out_specs=[any_space] * 2 + [vmem] * 9,
        scratch_shapes=[
            pltpu.VMEM((PIECES,) + full + (ROWS, COLS), bf16),
            pltpu.VMEM(full + (8, 128), f32),
            pltpu.VMEM((4, D, D), bf16),
            pltpu.VMEM((D, TILE), bf16),
            pltpu.VMEM((TILE, D), bf16),
            pltpu.VMEM((GROUPS, count, D), bf16),
            pltpu.VMEM((count, D), bf16),
            pltpu.VMEM((count, D), bf16),
            pltpu.VMEM((count, D), bf16),
            pltpu.VMEM((count, D), bf16),
            pltpu.VMEM((count, D), f32),
            pltpu.VMEM((count, D), f32),
            pltpu.VMEM((count, D), f32),
            pltpu.VMEM((count, TILE), bf16),
            pltpu.VMEM((count, TILE), bf16),
            pltpu.VMEM((H, 128, 384), bf16),
            pltpu.VMEM((count, 128), bf16),
            pltpu.VMEM((count, 128), bf16),
            pltpu.VMEM((count // SEQ, H, SEQ), f32),
            pltpu.VMEM((count // SEQ, 16, SEQ), f32),
            pltpu.VMEM((H, 2, 8, 128), f32),
            pltpu.VMEM((32, 128), f32),
            pltpu.VMEM((LANDINGS, 2, 4, 2, ROWS, COLS), bf16),
            pltpu.VMEM((LANDINGS, 4, 2, ROWS, COLS), bf16),
            pltpu.VMEM((LANDINGS, 4, ROWS, COLS), bf16),
            pltpu.VMEM((LANDINGS, 3, ROWS, COLS), bf16),
            pltpu.VMEM((3, 4, ROWS, COLS), bf16),
            pltpu.VMEM((10, 32, 128), f32),
            pltpu.SemaphoreType.DMA((PIECES, Gather.SLOTS)),
            pltpu.SemaphoreType.DMA((PIECES, Gather.SLOTS)),
            pltpu.SemaphoreType.DMA((Gather.SLOTS,)),
            pltpu.SemaphoreType.DMA((Gather.SLOTS,)),
            pltpu.SemaphoreType.DMA((PIECES, Reduce.SLOTS)),
            pltpu.SemaphoreType.DMA((PIECES, Reduce.SLOTS)),
            pltpu.SemaphoreType.DMA((SmallSum.SLOTS,)),
            pltpu.SemaphoreType.DMA((SmallSum.SLOTS,)),
            pltpu.SemaphoreType.REGULAR((LANDINGS, 6)),
            pltpu.SemaphoreType.DMA((4,)),
        ],
        compiler_params=pltpu.CompilerParams(collective_id=1, has_side_effects=True, vmem_limit_bytes=63 << 20),
    )(
        tokens,
        cotangent,
        lengths,
        norm_gain.reshape(1, -1),
        ffn_gain.reshape(1, -1),
        w_query,
        w_key,
        w_value,
        w_out,
        w_in,
        w_ffn_out,
        bias_table.T,
    )
    results = pl.pallas_call(
        deliver_kernel,
        out_shape=shapes,
        in_specs=[any_space] * len(shapes),
        out_specs=[any_space] * len(shapes),
        scratch_shapes=[pltpu.VMEM(shape.shape, shape.dtype) for shape in shapes]
        + [pltpu.SemaphoreType.DMA((2, len(shapes)))],
        compiler_params=pltpu.CompilerParams(vmem_limit_bytes=63 << 20),
    )(*results)
    output, grad_tokens, grad_one, grad_two, grad_table, *weight_grads = results
    group, groups = inner_groups()
    if group > 1:
        grad_table = lax.psum(grad_table, "dp", axis_index_groups=groups)
    grad_q, grad_k, grad_v, grad_o, grad_in, grad_ffn = (narrow(grad) for grad in weight_grads)
    return (
        output,
        grad_tokens,
        narrow(grad_one[0]),
        grad_q,
        grad_k,
        grad_v,
        grad_o,
        grad_table.T,
        narrow(grad_two[0]),
        grad_in,
        grad_ffn,
    )


def solution(mesh):
    rows, whole = P("dp", None), P("dp")
    return jax.shard_map(
        per_device,
        mesh=mesh,
        in_specs=(rows, rows, whole, rows, rows, rows, rows, P(), whole, rows, rows, rows),
        out_specs=(rows, rows, whole, rows, rows, rows, rows, P(), whole, rows, rows),
        check_vma=False,
    )
```

```python
from functools import partial

import jax
import jax.numpy as jnp
from jax import lax
from jax.experimental import pallas as pl
from jax.experimental.pallas import tpu as pltpu
from jax.sharding import PartitionSpec as P

D = 768
H = 12
NB = 32
SEQ = 512
FF = 3072
EPSILON = 1e-6
CUTOFFS = (12, 16, 23, 32, 46, 64, 91)
RANKS = 32
GROUPS = 3
TILES = 4
TILE = 768
MESH_ID = pl.DeviceIdType.MESH
f32, bf16 = jnp.float32, jnp.bfloat16

GROUP_PIECE, OUT_PIECE, PIECES = 0, 3, 12
FFN_PIECES, IN_PIECES = (4, 6, 8, 10), (5, 7, 9, 11)
ROWS, COLS = 48, 384
LANDINGS = 6
LOW, HIGH = slice(0, 2), slice(2, 4)


PLAN = {
    "S": [("g", 0, "finish")],
    "P0": [("g", 3, "across"), ("g", 4, "line")],
    "F0": [("g", 1, "along"), ("g", 2, "along")],
    "F1": [("g", 1, "finish")],
    "P1": [("g", 2, "finish"), ("g", 5, "across")],
    "F2": [("g", 3, "along"), ("g", 6, "line")],
    "P2": [("g", 3, "finish"), ("g", 4, "across"), ("g", 7, "line")],
    "F4": [("g", 5, "along"), ("g", 8, "line")],
    "F5": [("g", 6, "across"), ("g", 9, "line")],
    "A": [("g", 4, "along"), ("g", 5, "finish"), ("g", 7, "across"), ("g", 10, "line"), ("g", 4, "finish")],
    "T1": [("g", 8, "across"), ("g", 11, "line")],
    "T2": [("g", 6, "along")],
    "T4": [("g", 6, "finish"), ("g", 9, "across")],
    "T5": [("g", 7, "along")],
    "T6": [("g", 10, "across"), ("r", 0, "core"), ("g", 7, "finish")],
    "T7": [("g", 8, "along"), ("r", 1, "core")],
    "T9": [("g", 8, "finish"), ("g", 11, "across")],
    "T10": [("g", 9, "along")],
    "T11": [("g", 10, "along")],
    "T12": [("g", 9, "finish")],
    "T13": [("g", 10, "finish"), ("r", 0, "across")],
    "T14": [("r", 2, "core")],
    "T15": [("r", 1, "across"), ("r", 3, "core")],
    "T16": [("g", 11, "along")],
    "T17": [("r", 0, "along")],
    "T18": [("g", 11, "finish")],
    "T19": [("r", 2, "across")],
    "T20": [("r", 1, "along")],
    "T21": [("r", 0, "finish"), ("r", 4, "core")],
    "T22": [("r", 3, "across"), ("r", 5, "core")],
    "T23": [("r", 2, "along")],
    "T26": [("r", 4, "across"), ("r", 3, "along"), ("r", 2, "finish"), ("r", 1, "finish")],
    "T27": [("r", 5, "across"), ("r", 6, "core")],
    "B0": [("r", 4, "along")],
    "B2": [("r", 7, "core")],
    "B3": [("r", 5, "along")],
    "B4": [("r", 8, "start")],
    "K0": [("r", 3, "finish"), ("r", 4, "finish"), ("r", 6, "across"), ("r", 8, "core")],
    "K1": [("r", 7, "across")],
    "G0": [("r", 6, "along")],
    "K2": [("r", 5, "finish"), ("r", 8, "across"), ("r", 9, "core")],
    "K3": [("r", 6, "finish"), ("r", 7, "along")],
    "G1": [("r", 8, "along")],
    "K4": [("r", 9, "across"), ("r", 10, "core")],
    "G2": [("r", 8, "finish"), ("r", 9, "along")],
    "L0": [("r", 7, "finish"), ("r", 10, "across"), ("r", 11, "core")],
    "E": [("r", 9, "finish"), ("r", 10, "along"), ("r", 11, "across"), ("r", 10, "finish"), ("r", 11, "along"), ("r", 11, "finish")],
    "S0": [("g", 0, "line")],
    "S1": [("g", 1, "line"), ("g", 2, "line"), ("g", 0, "across")],
    "S2": [("g", 3, "line"), ("g", 1, "across"), ("g", 2, "across"), ("g", 0, "along")],
    "S3": [("g", 5, "line")],
}


def nt(a, b):
    return lax.dot_general(a, b, (((1,), (1,)), ((), ())), preferred_element_type=f32)


def nn(a, b):
    return jnp.dot(a, b, preferred_element_type=f32)


def tn(a, b):
    return lax.dot_general(a, b, (((0,), (0,)), ((), ())), preferred_element_type=f32)


def exact(a, b, dims=(((1,), (0,)), ((), ()))):
    return lax.dot_general(a, b, dims, precision=lax.Precision.HIGHEST, preferred_element_type=f32)


def part_of(index, size):
    return pl.ds(pl.multiple_of(index * size, size), size)


def place():
    me = lax.axis_index("dp")
    group = lax.axis_size("dp") // RANKS
    rank, low = me // group, me % group
    digits = dict(z=rank // 8, y=(rank // 4) % 2, x=(rank // 2) % 2, c=rank % 2)

    def device(**changed):
        d = {**digits, **changed}
        return ((((d["z"] * 2 + d["y"]) * 2 + d["x"]) * 2 + d["c"]) * group + low,)

    return digits, device


def partners(digits, device):
    line = [device(z=(digits["z"] + step) % 4) for step in (1, 2, 3)]
    return line + [device(**{axis: 1 - digits[axis]}) for axis in "yxc"]


def greet(digits, device):
    barrier = pltpu.get_barrier_semaphore()
    others = partners(digits, device)
    for other in others:
        pl.semaphore_signal(barrier, inc=1, device_id=other, device_id_type=MESH_ID)
    return lambda: pl.semaphore_wait(barrier, len(others))


class Transfers:
    def __init__(self, send_sems, recv_sems, digits, device):
        self.send_sems, self.recv_sems, self.digits, self.device = send_sems, recv_sems, digits, device

    def flip(self, *axes):
        return {axis: 1 - self.digits[axis] for axis in axes}

    def copy(self, slot):
        source, target, device_id = self.spec(slot)
        return pltpu.make_async_remote_copy(
            src_ref=source,
            dst_ref=target,
            send_sem=self.send_sems.at[slot],
            recv_sem=self.recv_sems.at[slot],
            device_id=device_id,
            device_id_type=MESH_ID,
        )

    def go(self, *slots):
        for slot in slots:
            self.copy(slot).start()

    def arrived_at(self, slot, landing):
        pltpu.make_async_remote_copy(
            src_ref=landing,
            dst_ref=landing,
            send_sem=self.send_sems.at[slot],
            recv_sem=self.recv_sems.at[slot],
            device_id=self.device(c=1 - self.digits["c"]),
            device_id_type=MESH_ID,
        ).wait_recv()

    def arrived(self, *slots):
        for slot in slots:
            self.arrived_at(slot, self.landing(slot))

    def sent(self, count):
        for slot in range(count):
            self.copy(slot).wait_send()


class Gather(Transfers):
    SLOTS = 11

    def __init__(self, full, send_sems, recv_sems, digits, device):
        super().__init__(send_sems, recv_sems, digits, device)
        self.full = full

    def line_of(self, *flipped, z=slice(None)):
        d = {**self.digits, **self.flip(*flipped)}
        return self.full.at[z, d["y"], d["x"], d["c"]]

    def block_of(self, z):
        return self.line_of(z=z)

    def spec(self, slot):
        z = self.digits["z"]
        if slot < 3:
            own = self.block_of(z)
            return own, own, self.device(z=(z + slot + 1) % 4)
        held, towards = (
            (self.line_of(), "x"),
            (self.line_of(), "y"),
            (self.line_of(), "c"),
            (self.line_of("x", z=LOW), "y"),
            (self.line_of("y", z=HIGH), "x"),
            (self.line_of("x"), "c"),
            (self.line_of("y"), "c"),
            (self.line_of("x", "y"), "c"),
        )[slot - 3]
        return held, held, self.device(**self.flip(towards))

    def landing(self, slot):
        if slot < 3:
            return self.block_of((self.digits["z"] + 3 - slot) % 4)
        return (
            self.line_of("x"),
            self.line_of("y"),
            self.line_of("c"),
            self.line_of("x", "y", z=LOW),
            self.line_of("x", "y", z=HIGH),
            self.line_of("c", "x"),
            self.line_of("c", "y"),
            self.line_of("c", "x", "y"),
        )[slot - 3]

    def start(self):
        self.go(0, 1, 2)

    def line(self):
        self.arrived(0, 1, 2)
        self.go(3, 4, 5)

    def across(self):
        self.arrived(3)
        self.go(6, 8)
        self.arrived(4)
        self.go(7, 9)

    def along(self):
        self.arrived(6, 7)
        self.go(10)

    def finish(self):
        self.arrived(5, 8, 9, 10)
        self.sent(self.SLOTS)


class PlaneGather(Gather):
    def __init__(self, full, send_sems, recv_sems, digits, device, plane):
        super().__init__(full, send_sems, recv_sems, digits, device)
        self.plane = plane

    def spec(self, slot):
        if slot < 3:
            line = self.line_of()
            return line, line, self.device(z=(self.digits["z"] + slot + 1) % 4)
        return super().spec(slot)

    def start(self):
        @pl.when(self.digits["z"] == self.plane)
        def _():
            self.go(0, 1, 2)

    def line(self):
        z = self.digits["z"]
        for slot in range(3):

            @pl.when(z == (self.plane + slot + 1) % 4)
            def _(slot=slot):
                line = self.line_of()
                self.arrived_at(slot, line)

        self.go(3, 4, 5)

    def sent(self, count):
        for slot in range(3, count):
            self.copy(slot).wait_send()

        @pl.when(self.digits["z"] == self.plane)
        def _():
            for slot in range(3):
                self.copy(slot).wait_send()


class Reduce(Transfers):
    SLOTS = 11

    def __init__(self, parts, received, send_sems, recv_sems, digits, device, credits=None, grants=None):
        super().__init__(send_sems, recv_sems, digits, device)
        self.parts = parts
        self.from_core, self.from_first, self.from_second, self.from_line = received
        self.credits, self.grants = credits, grants

    def side(self, high, far, c=None):
        d = self.digits
        c = d["c"] if c is None else c
        if high:
            return (HIGH, 1 - d["y"] if far else d["y"], slice(None), c)
        return (LOW, slice(None), 1 - d["x"] if far else d["x"], c)

    def pair(self, high, far):
        d = self.digits
        if high:
            return (HIGH, d["y"], 1 - d["x"] if far else d["x"], d["c"])
        return (LOW, 1 - d["y"] if far else d["y"], d["x"], d["c"])

    def spec(self, slot):
        d = self.digits
        if slot < 4:
            high, near = slot % 2, slot // 2
            source = self.parts.at[self.side(high, not near, 1 - d["c"])]
            return source, self.from_core.at[near, high], self.device(**self.flip("c"))
        if slot < 6:
            high = slot - 4
            return self.parts.at[self.side(high, True)], self.from_first.at[high], self.device(**self.flip("xy"[high]))
        if slot < 8:
            high = slot - 6
            return self.parts.at[self.pair(high, True)], self.from_second.at[high], self.device(**self.flip("yx"[high]))
        z = (d["z"] + slot - 7) % 4
        return self.parts.at[z, d["y"], d["x"], d["c"]], self.from_line.at[slot - 8], self.device(z=z)

    def landing(self, slot):
        if slot < 4:
            return self.from_core.at[slot // 2, slot % 2]
        if slot < 8:
            return (self.from_first, self.from_second)[(slot - 4) // 2].at[slot % 2]
        return self.from_line.at[slot - 8]

    def spend(self, *kinds):
        if self.credits is not None:
            for kind in kinds:
                pl.semaphore_wait(self.credits.at[kind], 1)

    def grant(self):
        d = self.digits
        if self.grants is not None:
            others = [self.device(**self.flip(axis)) for axis in "cxy"]
            others += [self.device(z=(d["z"] + 4 - step) % 4) for step in (1, 2, 3)]
            for kind, other in enumerate(others):
                pl.semaphore_signal(self.grants.at[kind], inc=1, device_id=other, device_id_type=MESH_ID)

    def add(self, index, received):
        self.parts[index] = self.parts[index] + received

    def start(self):
        self.spend(0)
        self.go(0, 1, 2, 3)

    def core(self):
        self.spend(1, 2)
        for high in (0, 1):
            self.arrived(high)
            self.add(self.side(high, True), self.from_core[0, high])
            self.go(4 + high)
        for high in (0, 1):
            self.arrived(2 + high)
            self.add(self.side(high, False), self.from_core[1, high])

    def across(self):
        d = self.digits
        for high, other in ((0, "y"), (1, "x")):
            self.arrived(4 + high)
            self.add(self.pair(high, True), self.from_first[high, :, 1 - d[other]])
            self.go(6 + high)
        for high, other in ((0, "y"), (1, "x")):
            self.add(self.pair(high, False), self.from_first[high, :, d[other]])

    def collect(self):
        for high in (0, 1):
            self.arrived(6 + high)
            self.add(self.pair(high, False), self.from_second[high])
        self.spend(3, 4, 5)

    def along(self):
        self.collect()
        self.go(8, 9, 10)

    def finish(self, store):
        d = self.digits
        total = self.parts[d["z"], d["y"], d["x"], d["c"]].astype(f32)
        for slot in (8, 9, 10):
            self.arrived(slot)
            total = total + self.from_line[slot - 8].astype(f32)
        store(total)
        self.sent(self.SLOTS)
        self.grant()


class PlaneReduce(Reduce):
    def __init__(self, parts, received, plane_in, send_sems, recv_sems, digits, device, credits, grants, plane):
        super().__init__(parts, received, send_sems, recv_sems, digits, device, credits, grants)
        self.plane_in, self.plane = plane_in, plane

    def along(self):
        d = self.digits
        self.collect()
        for step in (1, 2, 3):

            @pl.when(d["z"] == (self.plane + step) % 4)
            def _(step=step):
                self.to_plane(step).start()

    def to_plane(self, step):
        d = self.digits
        return pltpu.make_async_remote_copy(
            src_ref=self.parts.at[:, d["y"], d["x"], d["c"]],
            dst_ref=self.plane_in.at[step - 1],
            send_sem=self.send_sems.at[7 + step],
            recv_sem=self.recv_sems.at[7 + step],
            device_id=self.device(z=self.plane),
            device_id_type=MESH_ID,
        )

    def finish(self, store):
        d = self.digits

        @pl.when(d["z"] == self.plane)
        def _():
            total = self.parts[:, d["y"], d["x"], d["c"]].astype(f32)
            for step in (1, 2, 3):
                self.arrived_at(7 + step, self.plane_in.at[step - 1])
                total = total + self.plane_in[step - 1].astype(f32)
            store(total)

        for step in (1, 2, 3):

            @pl.when(d["z"] == (self.plane + step) % 4)
            def _(step=step):
                self.to_plane(step).wait_send()

        for slot in range(8):
            self.copy(slot).wait_send()
        self.grant()


class SmallSum(Transfers):
    SLOTS = 6

    def __init__(self, total, buffer, send_sems, recv_sems, digits, device):
        super().__init__(send_sems, recv_sems, digits, device)
        self.total, self.buffer = total, buffer

    def spec(self, slot):
        z = self.digits["z"]
        if slot < 3:
            return self.buffer.at[2 * slot], self.buffer.at[2 * slot + 1], self.device(**self.flip("cxy"[slot]))
        mine = self.buffer.at[6 + z]
        return mine, mine, self.device(z=(z + slot - 2) % 4)

    def landing(self, slot):
        if slot < 3:
            return self.buffer.at[2 * slot + 1]
        return self.buffer.at[6 + (self.digits["z"] + 6 - slot) % 4]

    def start(self, slot):
        if slot < 3:
            self.buffer[2 * slot] = self.total[...]
            self.go(slot)
        else:
            self.buffer[6 + self.digits["z"]] = self.total[...]
            self.go(3, 4, 5)

    def finish(self, slot):
        if slot < 3:
            self.arrived(slot)
            self.total[...] = self.total[...] + self.buffer[2 * slot + 1]
        else:
            self.arrived(3, 4, 5)
            self.total[...] = (self.buffer[6] + self.buffer[7]) + (self.buffer[8] + self.buffer[9])
            self.sent(self.SLOTS)


def pack(block):
    rows = block.reshape(-1, 8, 2 * COLS)
    return jnp.concatenate([rows[:, :, :COLS], rows[:, :, COLS:]], axis=1).reshape(-1, COLS)


def unpack(block):
    rows = block.reshape(-1, 2, 8, COLS)
    return jnp.concatenate([rows[:, 0].reshape(-1, COLS), rows[:, 1].reshape(-1, COLS)], axis=1)


def unpack_piece(piece, target):
    def plane(z, carry):
        target[part_of(z, 192), :] = unpack(piece[z].astype(f32).reshape(8 * ROWS, COLS)).astype(bf16)
        return carry

    lax.fori_loop(0, 4, plane, 0)


def pack_piece(piece, z, grad):
    piece[z] = pack(grad).astype(bf16).reshape(2, 2, 2, ROWS, COLS)


def bucket_of(offsets):
    distance = jnp.abs(offsets)
    coarse = jnp.full_like(distance, 8)
    for cutoff in CUTOFFS:
        coarse = coarse + (distance >= cutoff).astype(jnp.int32)
    return jnp.where(distance < 8, distance, coarse) + jnp.where(offsets > 0, 16, 0)


def strip_onehot(shift):
    column = lax.broadcasted_iota(jnp.int32, (128, 512), 1)
    column = jnp.where(column >= shift, column - shift, column - shift + 512)
    offset = jnp.where(column < 384, 128 - column, 640 - column)
    return bucket_of(offset) == lax.broadcasted_iota(jnp.int32, (128, 512), 0)


def make_strips(table_t, strips):
    line = nn(table_t[...], strip_onehot(0).astype(bf16)[:NB])
    for head in range(H):
        rows = jnp.broadcast_to(line[head : head + 1], (128, 512))
        strips[head] = pltpu.roll(rows, 0, 1, stride=1, stride_axis=0)[:, :384].astype(strips.dtype)


def strip_sums(strip):
    wide = jnp.concatenate([strip, jnp.zeros((128, 128), f32)], axis=1)
    total = wide[:8]
    for r in range(1, 16):
        total = total + pltpu.roll(wide[8 * r : 8 * r + 8], 512 - 8 * r, 1)
    return total


def table_sums(sums, far_sums):
    row = lax.broadcasted_iota(jnp.int32, (8 * H, 8 * H), 0)
    column = lax.broadcasted_iota(jnp.int32, (8 * H, 8 * H), 1)
    turned = exact((column == (row // 8) * 8 + 7 - row % 8).astype(f32), sums)
    lines = [
        jnp.sum(pltpu.roll(turned[8 * h : 8 * h + 8], 0, 1, stride=1, stride_axis=0), axis=0, keepdims=True)
        for h in range(H)
    ]
    lines.append(jnp.zeros((16 - H, 512), f32))
    table = exact(jnp.concatenate(lines, axis=0), strip_onehot(7).astype(f32), (((1,), (1,)), ((), ())))
    head = lax.broadcasted_iota(jnp.int32, (16, 128), 0)
    bucket = lax.broadcasted_iota(jnp.int32, (16, 128), 1)
    for side, index in ((0, 15), (1, 31)):
        rows = [jnp.sum(far_sums[h, side], axis=0, keepdims=True) for h in range(H)] + [jnp.zeros((16 - H, 128), f32)]
        total = jnp.sum(jnp.concatenate(rows, axis=0), axis=1, keepdims=True)
        table = table + jnp.where((bucket == index) & (head < H), total, 0.0)
    return table


def make_marks(lengths, key_marks, query_marks):
    position = lax.broadcasted_iota(jnp.int32, (SEQ, 128), 0)
    lane = lax.broadcasted_iota(jnp.int32, (SEQ, 128), 1)
    for row in range(key_marks.shape[0] // SEQ):
        segment = jnp.zeros((SEQ, 128), jnp.int32)
        end = 0
        for k in range(1, 5):
            end = end + lengths[row, k]
            segment = segment + (position >= end).astype(jnp.int32)
        own = segment == lane
        rows = slice(row * SEQ, (row + 1) * SEQ)
        key_marks[rows, :] = jnp.where(own, 1.0, 0.0).astype(bf16)
        query_marks[rows, :] = jnp.where(own | (lane >= 5), 0.0, -1e30).astype(bf16)


def lane_mask(h):
    lane = lax.broadcasted_iota(jnp.int32, (1, 128), 1)
    return lane < 64 if h == 0 else lane >= 64


def biased(raw, strip, half):
    low, high = strip[0:1, 383:384].astype(f32), strip[127:128, 0:1].astype(f32)
    rows = []
    for bj in range(4):
        blocks = []
        for bi in (0, 1):
            d = bj - bi - 2 * half
            block = raw[128 * bj : 128 * (bj + 1), 128 * bi : 128 * (bi + 1)]
            if d <= -2:
                block = block + low
            elif d >= 2:
                block = block + high
            else:
                block = block + strip[:, 128 * (1 - d) : 128 * (2 - d)].astype(f32)
            blocks.append(block)
        rows.append(jnp.concatenate(blocks, axis=1))
    return jnp.concatenate(rows, axis=0)


def heads_of(ref, rows, which, pair):
    return ref[rows, pl.ds(pl.multiple_of(which * 256 + pair * 128, 128), 128)]


def raw_scores(q2, k2, key_marks, query_marks):
    queries = jnp.concatenate([q2, query_marks], axis=1)
    return [nt(jnp.concatenate([jnp.where(lane_mask(h), k2, 0), key_marks], axis=1), queries) for h in range(2)]


def attend(qkv, key_marks, query_marks, strips, mix, lse, group, pair):
    count = mix.shape[0] // SEQ
    raws, values = [], []
    for row in range(count):
        rows = slice(row * SEQ, (row + 1) * SEQ)
        q2, k2, v2 = (heads_of(qkv, rows, which, pair) for which in range(3))
        raws.append(raw_scores(q2, k2, key_marks[rows, :], query_marks[rows, :]))
        values.append(v2.T)
    for row in range(count):
        outs = []
        for h in range(2):
            head = (group * 2 + pair) * 2 + h
            halves = []
            for half in range(2):
                span = slice(256 * half, 256 * half + 256)
                scores = biased(raws[row][h][:, span], strips[head], half)
                peak = jnp.max(scores, axis=0, keepdims=True)
                expo = jnp.exp(scores - peak)
                total = jnp.sum(expo, axis=0, keepdims=True)
                lse[row, pl.ds(head, 1), span] = peak + jnp.log(total)
                halves.append(nn(values[row][64 * h : 64 * h + 64], expo.astype(bf16)) * (1.0 / total))
            outs.append(jnp.concatenate(halves, axis=1))
        mix[row * SEQ : (row + 1) * SEQ, part_of(group * 2 + pair, 128)] = jnp.concatenate(outs, axis=0).T.astype(bf16)


def attend_back(qkv, gmix, key_marks, query_marks, strips, lse, inner, strip_grads, far_sums, group, pair):
    count = gmix.shape[0] // SEQ
    lanes = part_of(group * 2 + pair, 128)
    held = []
    for row in range(count):
        rows = slice(row * SEQ, (row + 1) * SEQ)
        q2, k2, v2 = (heads_of(qkv, rows, which, pair) for which in range(3))
        g2 = gmix[rows, lanes]
        raws = raw_scores(q2, k2, key_marks[rows, :], query_marks[rows, :])
        held.append((q2, k2.T, v2, g2, raws))
    for row in range(count):
        rows = slice(row * SEQ, (row + 1) * SEQ)
        q2, k2t, v2, g2, raws = held[row]
        grads = [nt(jnp.where(lane_mask(h), v2, 0), g2) for h in range(2)]
        grad_v, grad_k, grad_q = 0.0, 0.0, []
        for h in range(2):
            head = (group * 2 + pair) * 2 + h
            mask = lane_mask(h)
            near, far = {}, ([], [])
            probs_low, scores_low = [], []
            for half in range(2):
                span = slice(256 * half, 256 * half + 256)
                probs = jnp.exp(biased(raws[h][:, span], strips[head], half) - lse[row, pl.ds(head, 1), span])
                grad = probs * (grads[h][:, span] - inner[row, pl.ds(head, 1), span])
                probs_low.append(probs.astype(bf16))
                scores_low.append(grad.astype(bf16))
                for bi in (0, 1):
                    for bj in range(4):
                        d = bj - bi - 2 * half
                        block = grad[128 * bj : 128 * (bj + 1), 128 * bi : 128 * (bi + 1)]
                        if abs(d) <= 1:
                            near[d] = near[d] + block if d in near else block
                        else:
                            far[d > 0].append(jnp.sum(block.reshape(16, 8, 128), axis=0))
            strip_rows = part_of(group * 2 + pair, 128)
            for d, block in near.items():
                strip_grads[strip_rows, 384 * h + 128 * (1 - d) : 384 * h + 128 * (2 - d)] += block
            for side in (0, 1):
                far_sums[head, side] += sum(far[side][1:], far[side][0])
            grad_v = grad_v + nn(jnp.concatenate(probs_low, axis=1), jnp.where(mask, g2, 0))
            low = jnp.concatenate(scores_low, axis=1)
            grad_k = grad_k + nn(low, jnp.where(mask, q2, 0))
            grad_q.append(nn(k2t[64 * h : 64 * h + 64], low))
        for which, value in enumerate((jnp.concatenate(grad_q, axis=0).T, grad_k, grad_v)):
            qkv[rows, pl.ds(pl.multiple_of(which * 256 + pair * 128, 128), 128)] = value.astype(bf16)


def inner_sums(gmix, mix):
    product = gmix.astype(f32) * mix.astype(f32)
    high = product.astype(bf16)
    low = (product - high.astype(f32)).astype(bf16)
    feature = lax.broadcasted_iota(jnp.int32, (16, D), 1)
    first = lax.broadcasted_iota(jnp.int32, (16, D), 0) * 64
    own = jnp.where((feature >= first) & (feature < first + 64), 1.0, 0.0).astype(bf16)
    return nt(own, high) + nt(own, low)


def inv_rms(x):
    return lax.rsqrt(jnp.mean(x * x, axis=-1, keepdims=True) + EPSILON)


def norm_back(grad, x, gain):
    s = inv_rms(x)
    gg = grad * gain
    return s * gg - x * (s * s * s * jnp.mean(gg * x, axis=-1, keepdims=True)), jnp.sum(grad * x * s, axis=0, keepdims=True)


def gelu_both(x):
    cdf = 0.5 + 0.5 * lax.erf(x * 0.7071067811865476)
    return x * cdf, cdf + x * (jnp.exp(x * x * -0.5) * 0.3989422804014327)


def gain_line(gains, which):
    blocks = gains[...].reshape(8 * RANKS, 128).astype(bf16)
    lane = lax.broadcasted_iota(jnp.int32, (128, D), 1)
    spread = nn(blocks, (lane % 24 == lax.broadcasted_iota(jnp.int32, (128, D), 0)).astype(bf16))
    row = lax.broadcasted_iota(jnp.int32, (8 * RANKS, D), 0)
    column = lax.broadcasted_iota(jnp.int32, (8 * RANKS, D), 1)
    return jnp.sum(jnp.where(row == (column // 24) * 8 + which, spread, 0.0), axis=0, keepdims=True)


def run_at(step, plan):
    for when, stages in plan.items():

        @pl.when(step == when)
        def _(stages=stages):
            for stage in stages:
                stage()


def layer_kernel(
    tokens_hbm, cot_hbm, lengths, norm_gain, ffn_gain, w_query, w_key, w_value, w_out, w_in, w_ffn, table_t,
    out_hbm, gtok_hbm, grad_one, grad_two, grad_table, grad_q, grad_k, grad_v, grad_o, grad_in, grad_ffn,
    pieces, gains, weights, win, wff, qkv, mix, normed, tokens, cot, resid, out_sum, grad_sum, act, grad_inner,
    strips, key_marks, query_marks, lse, inner, far_sums, small, from_core, from_first, from_second, from_line,
    plane_in, small_buffer,
    gather_send, gather_recv, gain_send, gain_recv, reduce_send, reduce_recv, small_send, small_recv, credits, local_sems,
):
    count = tokens.shape[0]
    digits, device = place()
    me = (digits["z"], digits["y"], digits["x"], digits["c"])
    all_here = greet(digits, device)

    load_tokens = pltpu.make_async_copy(tokens_hbm, tokens, local_sems.at[0])
    load_tokens.start()
    load_cot = pltpu.make_async_copy(cot_hbm, cot, local_sems.at[1])
    load_cot.start()

    gain_gather = Gather(gains, gain_send, gain_recv, digits, device)
    gathers = []
    for i in range(PIECES):
        common = (pieces.at[i], gather_send.at[i], gather_recv.at[i], digits, device)
        gathers.append(PlaneGather(*common, FFN_PIECES.index(i)) if i in FFN_PIECES else Gather(*common))
    order = [i for t in range(TILES) for i in (IN_PIECES[t], FFN_PIECES[t])] + [OUT_PIECE, 0, 1, 2]
    reduces = []
    for n, i in enumerate(order):
        slot = n % LANDINGS
        received = (from_core.at[slot], from_first.at[slot], from_second.at[slot], from_line.at[slot])
        sems = (reduce_send.at[n], reduce_recv.at[n], digits, device)
        limits = (credits.at[slot] if n >= LANDINGS else None, credits.at[slot] if n + LANDINGS < PIECES else None)
        if i in FFN_PIECES:
            reduces.append(PlaneReduce(pieces.at[i], received, plane_in, *sems, *limits, FFN_PIECES.index(i)))
        else:
            reduces.append(Reduce(pieces.at[i], received, *sems, *limits))

    def store_in(t):
        def store(total):
            grad_in[:, TILE * t : TILE * (t + 1)] = unpack(total)

        return store

    def store_ffn(total):
        for i in range(4):
            grad_ffn[ROWS * (i // 2) : ROWS * (i // 2 + 1), COLS * (i % 2) : COLS * (i % 2 + 1)] = total[i]

    def store_out(total):
        grad_o[...] = unpack(total)

    def store_group(g):
        def store(total):
            block = unpack(total)
            for which, target in enumerate((grad_q, grad_k, grad_v)):
                target[:, 256 * g : 256 * (g + 1)] = block[:, 256 * which : 256 * (which + 1)]

        return store

    stores = [store for t in range(TILES) for store in (store_in(t), store_ffn)] + [store_out]
    stores += [store_group(g) for g in range(GROUPS)]

    def stage(kind, n, name):
        if kind == "r":
            return partial(reduces[n].finish, stores[n]) if name == "finish" else getattr(reduces[n], name)
        if name == "finish" and n <= OUT_PIECE:
            return partial(arrive, n)
        return getattr(gathers[n], name)

    def arrive(n):
        gathers[n].finish()
        unpack_piece(pieces.at[n], weights.at[n])

    def plan(letter):
        return {int(key[1:]): [stage(*entry) for entry in PLAN[key]] for key in PLAN if key[0] == letter}

    def run(stages):
        for each in stages:
            each()

    for g in range(GROUPS):
        span = slice(256 * g, 256 * g + 256)
        block = jnp.concatenate([w[:, span] for w in (w_query, w_key, w_value)], axis=1)
        pieces[(GROUP_PIECE + g, *me)] = pack(block.astype(f32)).astype(bf16)
    gains[me] = jnp.zeros((8, 128), f32)
    gains[(*me, slice(0, 1), slice(0, 24))] = norm_gain[...].astype(f32)
    gains[(*me, slice(1, 2), slice(0, 24))] = ffn_gain[...].astype(f32)
    all_here()
    gathers[0].start()
    gain_gather.start()
    gathers[1].start()
    gathers[2].start()
    pieces[(OUT_PIECE, *me)] = pack(w_out[...].astype(f32)).astype(bf16)
    gathers[3].start()
    for t in range(TILES):

        @pl.when(digits["z"] == t)
        def _(t=t):
            for i in range(4):
                block = w_ffn[ROWS * (i // 2) : ROWS * (i // 2 + 1), COLS * (i % 2) : COLS * (i % 2 + 1)]
                pieces[FFN_PIECES[t], i, digits["y"], digits["x"], digits["c"]] = block

        gathers[FFN_PIECES[t]].start()
        pieces[(IN_PIECES[t], *me)] = pack(w_in[:, TILE * t : TILE * (t + 1)].astype(f32)).astype(bf16)
        gathers[IN_PIECES[t]].start()

    make_marks(lengths, key_marks, query_marks)
    make_strips(table_t, strips)
    for i, gain_stage in enumerate((gain_gather.line, gain_gather.across, gain_gather.along, gain_gather.finish)):
        run([stage(*entry) for entry in PLAN[f"S{i}"]])
        gain_stage()
    gain_one, gain_two = gain_line(gains, 0), gain_line(gains, 1)
    load_tokens.wait()

    def norm_one(i, carry):
        rows = part_of(i, 256)
        x = tokens[rows, :].astype(f32)
        normed[rows, :] = (x * inv_rms(x) * gain_one).astype(bf16)
        return carry

    lax.fori_loop(0, count // 256, norm_one, 0)
    run([stage(*entry) for entry in PLAN["S"]])

    forward_plan, project_plan = plan("F"), plan("P")

    def forward_group(g, carry):
        qkv[g] = nn(normed[...], weights[GROUP_PIECE + g]).astype(bf16)
        run_at(g, project_plan)

        def forward(pair, carry):
            attend(qkv.at[g], key_marks, query_marks, strips, mix, lse, g, pair)
            run_at(2 * g + pair, forward_plan)
            return carry

        lax.fori_loop(0, 2, forward, 0)
        return carry

    lax.fori_loop(0, GROUPS, forward_group, 0)

    def after_attention(i, carry):
        rows = part_of(i, 512)
        r = tokens[rows, :].astype(f32) + nn(mix[rows, :], weights[OUT_PIECE])
        resid[rows, :] = r
        normed[rows, :] = (r * inv_rms(r) * gain_two).astype(bf16)
        return carry

    lax.fori_loop(0, count // 512, after_attention, 0)
    load_cot.wait()
    run([stage(*entry) for entry in PLAN["A"]])

    ffn_plan = plan("T")
    width = 256

    def tile_piece(t, which):
        return pieces.at[4 + 2 * t + which]

    def ffn_tile(t, carry):
        unpack_piece(tile_piece(t, 1), win)
        for b in range(8):
            for i in range(4):
                rows = slice(96 * b + ROWS * (i // 2), 96 * b + ROWS * (i // 2 + 1))
                block = pieces[4 + 2 * t, i, b // 4, (b // 2) % 2, b % 2]
                wff[rows, COLS * (i % 2) : COLS * (i % 2 + 1)] = block

        def columns(w, carry):
            span = part_of(w, width)
            ffn_in = nn(normed[...], win[:, span])
            grad_act = nt(cot[...], wff[span, :])
            value, slope = gelu_both(ffn_in)
            act[:, span] = value.astype(bf16)
            grad_inner[:, span] = (slope * grad_act).astype(bf16)
            run_at(7 * t + w, ffn_plan)
            return carry

        lax.fori_loop(0, TILE // width, columns, 0)

        for i in range(2):
            rows = slice(i * count // 2, (i + 1) * count // 2)
            value = nn(act[rows, :], wff[...])
            out_sum[rows, :] = jnp.where(t == 0, resid[rows, :], out_sum[rows, :]) + value

        run_at(7 * t + 3, ffn_plan)

        for i in range(2):
            rows = slice(i * count // 2, (i + 1) * count // 2)
            value = nt(grad_inner[rows, :], win[...])
            grad_sum[rows, :] = jnp.where(t == 0, 0.0, grad_sum[rows, :]) + value

        run_at(7 * t + 4, ffn_plan)
        grad = tn(normed[...], grad_inner[...])
        for z in range(4):
            pack_piece(tile_piece(t, 1), z, grad[192 * z : 192 * (z + 1)])
        run_at(t, {k: [reduces[2 * k].start] for k in range(TILES)})
        run_at(7 * t + 5, ffn_plan)
        grad = tn(act[...], cot[...]).astype(bf16)
        for b in range(8):
            for i in range(4):
                block = grad[96 * b + ROWS * (i // 2) : 96 * b + ROWS * (i // 2 + 1), COLS * (i % 2) : COLS * (i % 2 + 1)]
                pieces[4 + 2 * t, i, b // 4, (b // 2) % 2, b % 2] = block
        run_at(t, {k: [reduces[2 * k + 1].start] for k in range(TILES)})
        run_at(7 * t + 6, ffn_plan)
        return carry

    lax.fori_loop(0, TILES, ffn_tile, 0)

    before_plan = plan("B")
    small[...] = jnp.zeros(small.shape, f32)

    def spread_line(row, line):
        for j in range(D // 128):
            small[row + j : row + j + 1, :] += line[:, 128 * j : 128 * (j + 1)]

    def before_back(i, carry):
        rows = part_of(i, 256)
        act[rows, :] = out_sum[rows, :].astype(bf16)
        into, gain_sum = norm_back(grad_sum[rows, :], resid[rows, :], gain_two)
        spread_line(6, gain_sum)
        grad = cot[rows, :].astype(f32) + into
        grad_sum[rows, :] = grad
        low = grad.astype(bf16)
        cot[rows, :] = low
        gmix = nt(low, weights[OUT_PIECE]).astype(bf16)
        inner[i // 2, :, part_of(i % 2, 256)] = inner_sums(gmix, mix[rows, :])
        x = tokens[rows, :].astype(f32)
        grad_inner[rows, :] = (x * inv_rms(x) * gain_one).astype(bf16)
        normed[rows, :] = gmix
        run_at(i, before_plan)
        return carry

    lax.fori_loop(0, count // 256, before_back, 0)
    store_output = pltpu.make_async_copy(act, out_hbm, local_sems.at[2])
    store_output.start()
    out_sum[...] = jnp.zeros(out_sum.shape, f32)
    far_sums[...] = jnp.zeros(far_sums.shape, f32)
    grad = tn(mix[...], cot[...])
    for z in range(4):
        pack_piece(pieces.at[OUT_PIECE], z, grad[192 * z : 192 * (z + 1)])
    run(before_plan.get(4, []))
    back_plan, group_plan = plan("K"), plan("G")

    def back_group(g, carry):
        def back(pair, carry):
            attend_back(qkv.at[g], normed, key_marks, query_marks, strips, lse, inner, out_sum, far_sums, g, pair)
            run_at(2 * g + pair, back_plan)
            return carry

        lax.fori_loop(0, 2, back, 0)
        grad = tn(grad_inner[...], qkv[g])
        for z in range(4):
            pack_piece(pieces.at[GROUP_PIECE + g], z, grad[192 * z : 192 * (z + 1)])
        run_at(g, {k: [reduces[9 + k].start] for k in range(GROUPS)})
        run_at(g, group_plan)
        return carry

    lax.fori_loop(0, GROUPS, back_group, 0)
    last_plan = plan("L")

    def last(i, carry):
        rows = part_of(i, 512)
        grad = nt(qkv[0, rows, :], weights[0]) + nt(qkv[1, rows, :], weights[1]) + nt(qkv[2, rows, :], weights[2])
        into, gain_sum = norm_back(grad, tokens[rows, :].astype(f32), gain_one)
        spread_line(0, gain_sum)
        grad_sum[rows, :] = grad_sum[rows, :] + into
        run_at(i, last_plan)
        return carry

    lax.fori_loop(0, count // 512, last, 0)
    store_gtok = pltpu.make_async_copy(grad_sum, gtok_hbm, local_sems.at[3])
    store_gtok.start()
    for pair in range(H // 2):
        for h in range(2):
            head = 2 * pair + h
            strip = out_sum[128 * pair : 128 * pair + 128, 384 * h : 384 * h + 384]
            resid[8 * head : 8 * head + 8, :512] = strip_sums(strip)
    small[16:32, :] = table_sums(resid[: 8 * H, :512], far_sums)
    sums = SmallSum(small, small_buffer, small_send, small_recv, digits, device)
    tail = [stage(*entry) for entry in PLAN["E"]]
    for slot in range(4):
        sums.start(slot)
        share = -(-len(tail) // (4 - slot))
        run(tail[:share])
        tail = tail[share:]
        sums.finish(slot)
    for target, row in ((grad_one, 0), (grad_two, 6)):
        line = jnp.concatenate([small[row + j : row + j + 1, :] for j in range(D // 128)], axis=1)
        rank = (lax.axis_index("dp") // (lax.axis_size("dp") // RANKS)).astype(jnp.int32)
        own = pltpu.roll(jnp.broadcast_to(line, (8, D)), (D - 24 * rank) % D, 1)
        target[...] = own[0:1, :24]
    grad_table[...] = small[16 : 16 + H, :NB]
    run(tail)
    store_output.wait()
    store_gtok.wait()


def deliver_kernel(*refs):
    count = (len(refs) - 1) // 3
    sources, targets, held, sems = refs[:count], refs[count : 2 * count], refs[2 * count : 3 * count], refs[-1]
    loads = [pltpu.make_async_copy(sources[i], held[i], sems.at[0, i]) for i in range(count)]
    stores = [pltpu.make_async_copy(held[i], targets[i], sems.at[1, i]) for i in range(count)]
    for load in loads:
        load.start()
    for load, store in zip(loads, stores):
        load.wait()
        store.start()
    for store in stores:
        store.wait()


def inner_groups():
    total = lax.axis_size("dp")
    group = total // RANKS
    return group, [list(range(i * group, (i + 1) * group)) for i in range(RANKS)]


def widen(block):
    group, groups = inner_groups()
    if group == 1:
        return block
    return lax.all_gather(block, "dp", axis=0, tiled=True, axis_index_groups=groups)


def narrow(block):
    group, groups = inner_groups()
    if group == 1:
        return block
    return lax.psum_scatter(block, "dp", scatter_dimension=0, tiled=True, axis_index_groups=groups)


def per_device(
    tokens, lengths, norm_gain, w_query, w_key, w_value, w_out, bias_table, ffn_gain, w_in, w_ffn_out, cotangent
):
    count = tokens.shape[0]
    norm_gain, ffn_gain, w_query, w_key, w_value, w_out, w_in, w_ffn_out = (
        widen(w) for w in (norm_gain, ffn_gain, w_query, w_key, w_value, w_out, w_in, w_ffn_out)
    )
    any_space = pl.BlockSpec(memory_space=pl.ANY)
    vmem = pl.BlockSpec(memory_space=pltpu.VMEM)
    smem = pl.BlockSpec(memory_space=pltpu.SMEM)
    full = (4, 2, 2, 2)
    out = jax.ShapeDtypeStruct
    shapes = [out((count, D), bf16), out((count, D), f32), out((1, 24), f32), out((1, 24), f32), out((H, NB), f32)]
    shapes += [out((24, D), f32)] * 4 + [out((24, FF), f32), out((96, D), f32)]
    results = pl.pallas_call(
        layer_kernel,
        out_shape=shapes,
        in_specs=[any_space] * 2 + [smem] + [vmem] * 9,
        out_specs=[any_space] * 2 + [vmem] * 9,
        scratch_shapes=[
            pltpu.VMEM((PIECES,) + full + (ROWS, COLS), bf16),
            pltpu.VMEM(full + (8, 128), f32),
            pltpu.VMEM((4, D, D), bf16),
            pltpu.VMEM((D, TILE), bf16),
            pltpu.VMEM((TILE, D), bf16),
            pltpu.VMEM((GROUPS, count, D), bf16),
            pltpu.VMEM((count, D), bf16),
            pltpu.VMEM((count, D), bf16),
            pltpu.VMEM((count, D), bf16),
            pltpu.VMEM((count, D), bf16),
            pltpu.VMEM((count, D), f32),
            pltpu.VMEM((count, D), f32),
            pltpu.VMEM((count, D), f32),
            pltpu.VMEM((count, TILE), bf16),
            pltpu.VMEM((count, TILE), bf16),
            pltpu.VMEM((H, 128, 384), bf16),
            pltpu.VMEM((count, 128), bf16),
            pltpu.VMEM((count, 128), bf16),
            pltpu.VMEM((count // SEQ, H, SEQ), f32),
            pltpu.VMEM((count // SEQ, 16, SEQ), f32),
            pltpu.VMEM((H, 2, 8, 128), f32),
            pltpu.VMEM((32, 128), f32),
            pltpu.VMEM((LANDINGS, 2, 2, 2, 2, ROWS, COLS), bf16),
            pltpu.VMEM((LANDINGS, 2, 2, 2, ROWS, COLS), bf16),
            pltpu.VMEM((LANDINGS, 2, 2, ROWS, COLS), bf16),
            pltpu.VMEM((LANDINGS, 3, ROWS, COLS), bf16),
            pltpu.VMEM((3, 4, ROWS, COLS), bf16),
            pltpu.VMEM((10, 32, 128), f32),
            pltpu.SemaphoreType.DMA((PIECES, Gather.SLOTS)),
            pltpu.SemaphoreType.DMA((PIECES, Gather.SLOTS)),
            pltpu.SemaphoreType.DMA((Gather.SLOTS,)),
            pltpu.SemaphoreType.DMA((Gather.SLOTS,)),
            pltpu.SemaphoreType.DMA((PIECES, Reduce.SLOTS)),
            pltpu.SemaphoreType.DMA((PIECES, Reduce.SLOTS)),
            pltpu.SemaphoreType.DMA((SmallSum.SLOTS,)),
            pltpu.SemaphoreType.DMA((SmallSum.SLOTS,)),
            pltpu.SemaphoreType.REGULAR((LANDINGS, 6)),
            pltpu.SemaphoreType.DMA((4,)),
        ],
        compiler_params=pltpu.CompilerParams(collective_id=1, has_side_effects=True, vmem_limit_bytes=63 << 20),
    )(
        tokens,
        cotangent,
        lengths,
        norm_gain.reshape(1, -1),
        ffn_gain.reshape(1, -1),
        w_query,
        w_key,
        w_value,
        w_out,
        w_in,
        w_ffn_out,
        bias_table.T,
    )
    results = pl.pallas_call(
        deliver_kernel,
        out_shape=shapes,
        in_specs=[any_space] * len(shapes),
        out_specs=[any_space] * len(shapes),
        scratch_shapes=[pltpu.VMEM(shape.shape, shape.dtype) for shape in shapes]
        + [pltpu.SemaphoreType.DMA((2, len(shapes)))],
        compiler_params=pltpu.CompilerParams(vmem_limit_bytes=63 << 20),
    )(*results)
    output, grad_tokens, grad_one, grad_two, grad_table, *weight_grads = results
    group, groups = inner_groups()
    if group > 1:
        grad_table = lax.psum(grad_table, "dp", axis_index_groups=groups)
    grad_q, grad_k, grad_v, grad_o, grad_in, grad_ffn = (narrow(grad) for grad in weight_grads)
    return (
        output,
        grad_tokens,
        narrow(grad_one[0]),
        grad_q,
        grad_k,
        grad_v,
        grad_o,
        grad_table.T,
        narrow(grad_two[0]),
        grad_in,
        grad_ffn,
    )


def solution(mesh):
    rows, whole = P("dp", None), P("dp")
    return jax.shard_map(
        per_device,
        mesh=mesh,
        in_specs=(rows, rows, whole, rows, rows, rows, rows, P(), whole, rows, rows, rows),
        out_specs=(rows, rows, whole, rows, rows, rows, rows, P(), whole, rows, rows),
        check_vma=False,
    )
```

```python
from functools import partial

import jax
import jax.numpy as jnp
from jax import lax
from jax.experimental import pallas as pl
from jax.experimental.pallas import tpu as pltpu
from jax.sharding import PartitionSpec as P

D = 768
H = 12
NB = 32
SEQ = 512
FF = 3072
EPSILON = 1e-6
CUTOFFS = (12, 16, 23, 32, 46, 64, 91)
RANKS = 32
GROUPS = 3
TILES = 4
TILE = 768
MESH_ID = pl.DeviceIdType.MESH
f32, bf16 = jnp.float32, jnp.bfloat16

GROUP_PIECE, OUT_PIECE, PIECES = 0, 3, 12
FFN_PIECES, IN_PIECES = (4, 6, 8, 10), (5, 7, 9, 11)
ROWS, COLS = 48, 384
LANDINGS = 6
LOW, HIGH = slice(0, 2), slice(2, 4)


PLAN = {
    "S": [("g", 0, "finish")],
    "P0": [("g", 3, "across"), ("g", 4, "line")],
    "F0": [("g", 1, "along"), ("g", 2, "along")],
    "F1": [("g", 1, "finish")],
    "P1": [("g", 2, "finish"), ("g", 5, "across")],
    "F2": [("g", 3, "along"), ("g", 6, "line")],
    "P2": [("g", 3, "finish"), ("g", 4, "across"), ("g", 7, "line")],
    "F4": [("g", 5, "along"), ("g", 8, "line")],
    "F5": [("g", 6, "across"), ("g", 9, "line")],
    "A": [("g", 4, "along"), ("g", 5, "finish"), ("g", 7, "across"), ("g", 10, "line"), ("g", 4, "finish")],
    "T1": [("g", 8, "across"), ("g", 11, "line")],
    "T2": [("g", 6, "along")],
    "T4": [("g", 6, "finish"), ("g", 9, "across")],
    "T5": [("g", 7, "along")],
    "T6": [("g", 10, "across"), ("r", 0, "core"), ("g", 7, "finish")],
    "T7": [("g", 8, "along"), ("r", 1, "core")],
    "T9": [("g", 8, "finish"), ("g", 11, "across")],
    "T10": [("g", 9, "along")],
    "T11": [("g", 10, "along")],
    "T12": [("g", 9, "finish")],
    "T13": [("g", 10, "finish"), ("r", 0, "across")],
    "T14": [("r", 2, "core")],
    "T15": [("r", 1, "across"), ("r", 3, "core")],
    "T16": [("g", 11, "along")],
    "T17": [("r", 0, "along")],
    "T18": [("g", 11, "finish")],
    "T19": [("r", 2, "across")],
    "T20": [("r", 1, "along")],
    "T21": [("r", 0, "finish"), ("r", 4, "core")],
    "T22": [("r", 3, "across"), ("r", 5, "core")],
    "T23": [("r", 2, "along")],
    "T26": [("r", 4, "across"), ("r", 3, "along"), ("r", 2, "finish"), ("r", 1, "finish")],
    "T27": [("r", 5, "across"), ("r", 6, "core")],
    "B0": [("r", 4, "along")],
    "B2": [("r", 7, "core")],
    "B3": [("r", 5, "along")],
    "B4": [("r", 8, "start")],
    "K0": [("r", 3, "finish"), ("r", 4, "finish"), ("r", 6, "across"), ("r", 8, "core")],
    "K1": [("r", 7, "across")],
    "G0": [("r", 6, "along")],
    "K2": [("r", 5, "finish"), ("r", 8, "across"), ("r", 9, "core")],
    "K3": [("r", 6, "finish"), ("r", 7, "along")],
    "G1": [("r", 8, "along")],
    "K4": [("r", 9, "across"), ("r", 10, "core")],
    "G2": [("r", 8, "finish"), ("r", 9, "along")],
    "L0": [("r", 7, "finish"), ("r", 10, "across"), ("r", 11, "core")],
    "E": [("r", 11, "across"), ("r", 10, "along"), ("r", 9, "finish"), ("r", 11, "along"), ("r", 10, "finish"), ("r", 11, "finish")],
    "S0": [("g", 0, "line")],
    "S1": [("g", 1, "line"), ("g", 2, "line"), ("g", 0, "across")],
    "S2": [("g", 3, "line"), ("g", 1, "across"), ("g", 2, "across"), ("g", 0, "along")],
    "S3": [("g", 5, "line")],
}


def nt(a, b):
    return lax.dot_general(a, b, (((1,), (1,)), ((), ())), preferred_element_type=f32)


def nn(a, b):
    return jnp.dot(a, b, preferred_element_type=f32)


def tn(a, b):
    return lax.dot_general(a, b, (((0,), (0,)), ((), ())), preferred_element_type=f32)


def exact(a, b, dims=(((1,), (0,)), ((), ()))):
    return lax.dot_general(a, b, dims, precision=lax.Precision.HIGHEST, preferred_element_type=f32)


def part_of(index, size):
    return pl.ds(pl.multiple_of(index * size, size), size)


def place():
    me = lax.axis_index("dp")
    group = lax.axis_size("dp") // RANKS
    rank, low = me // group, me % group
    digits = dict(z=rank // 8, y=(rank // 4) % 2, x=(rank // 2) % 2, c=rank % 2)

    def device(**changed):
        d = {**digits, **changed}
        return ((((d["z"] * 2 + d["y"]) * 2 + d["x"]) * 2 + d["c"]) * group + low,)

    return digits, device


def partners(digits, device):
    line = [device(z=(digits["z"] + step) % 4) for step in (1, 2, 3)]
    return line + [device(**{axis: 1 - digits[axis]}) for axis in "yxc"]


def greet(digits, device):
    barrier = pltpu.get_barrier_semaphore()
    others = partners(digits, device)
    for other in others:
        pl.semaphore_signal(barrier, inc=1, device_id=other, device_id_type=MESH_ID)
    return lambda: pl.semaphore_wait(barrier, len(others))


class Transfers:
    def __init__(self, send_sems, recv_sems, digits, device):
        self.send_sems, self.recv_sems, self.digits, self.device = send_sems, recv_sems, digits, device

    def flip(self, *axes):
        return {axis: 1 - self.digits[axis] for axis in axes}

    def copy(self, slot):
        source, target, device_id = self.spec(slot)
        return pltpu.make_async_remote_copy(
            src_ref=source,
            dst_ref=target,
            send_sem=self.send_sems.at[slot],
            recv_sem=self.recv_sems.at[slot],
            device_id=device_id,
            device_id_type=MESH_ID,
        )

    def go(self, *slots):
        for slot in slots:
            self.copy(slot).start()

    def arrived_at(self, slot, landing):
        pltpu.make_async_remote_copy(
            src_ref=landing,
            dst_ref=landing,
            send_sem=self.send_sems.at[slot],
            recv_sem=self.recv_sems.at[slot],
            device_id=self.device(c=1 - self.digits["c"]),
            device_id_type=MESH_ID,
        ).wait_recv()

    def arrived(self, *slots):
        for slot in slots:
            self.arrived_at(slot, self.landing(slot))

    def sent(self, count):
        for slot in range(count):
            self.copy(slot).wait_send()


class Gather(Transfers):
    SLOTS = 11

    def __init__(self, full, send_sems, recv_sems, digits, device):
        super().__init__(send_sems, recv_sems, digits, device)
        self.full = full

    def line_of(self, *flipped, z=slice(None)):
        d = {**self.digits, **self.flip(*flipped)}
        return self.full.at[z, d["y"], d["x"], d["c"]]

    def block_of(self, z):
        return self.line_of(z=z)

    def spec(self, slot):
        z = self.digits["z"]
        if slot < 3:
            own = self.block_of(z)
            return own, own, self.device(z=(z + slot + 1) % 4)
        held, towards = (
            (self.line_of(), "x"),
            (self.line_of(), "y"),
            (self.line_of(), "c"),
            (self.line_of("x", z=LOW), "y"),
            (self.line_of("y", z=HIGH), "x"),
            (self.line_of("x"), "c"),
            (self.line_of("y"), "c"),
            (self.line_of("x", "y"), "c"),
        )[slot - 3]
        return held, held, self.device(**self.flip(towards))

    def landing(self, slot):
        if slot < 3:
            return self.block_of((self.digits["z"] + 3 - slot) % 4)
        return (
            self.line_of("x"),
            self.line_of("y"),
            self.line_of("c"),
            self.line_of("x", "y", z=LOW),
            self.line_of("x", "y", z=HIGH),
            self.line_of("c", "x"),
            self.line_of("c", "y"),
            self.line_of("c", "x", "y"),
        )[slot - 3]

    def start(self):
        self.go(0, 1, 2)

    def line(self):
        self.arrived(0, 1, 2)
        self.go(3, 4, 5)

    def across(self):
        self.arrived(3)
        self.go(6, 8)
        self.arrived(4)
        self.go(7, 9)

    def along(self):
        self.arrived(6, 7)
        self.go(10)

    def finish(self):
        self.arrived(5, 8, 9, 10)
        self.sent(self.SLOTS)


class PlaneGather(Gather):
    def __init__(self, full, send_sems, recv_sems, digits, device, plane):
        super().__init__(full, send_sems, recv_sems, digits, device)
        self.plane = plane

    def spec(self, slot):
        if slot < 3:
            line = self.line_of()
            return line, line, self.device(z=(self.digits["z"] + slot + 1) % 4)
        return super().spec(slot)

    def start(self):
        @pl.when(self.digits["z"] == self.plane)
        def _():
            self.go(0, 1, 2)

    def line(self):
        z = self.digits["z"]
        for slot in range(3):

            @pl.when(z == (self.plane + slot + 1) % 4)
            def _(slot=slot):
                line = self.line_of()
                self.arrived_at(slot, line)

        self.go(3, 4, 5)

    def sent(self, count):
        for slot in range(3, count):
            self.copy(slot).wait_send()

        @pl.when(self.digits["z"] == self.plane)
        def _():
            for slot in range(3):
                self.copy(slot).wait_send()


class Reduce(Transfers):
    SLOTS = 11

    def __init__(self, parts, received, send_sems, recv_sems, digits, device, credits=None, grants=None):
        super().__init__(send_sems, recv_sems, digits, device)
        self.parts = parts
        self.from_core, self.from_first, self.from_second, self.from_line = received
        self.credits, self.grants = credits, grants

    def side(self, high, far, c=None):
        d = self.digits
        c = d["c"] if c is None else c
        if high:
            return (HIGH, 1 - d["y"] if far else d["y"], slice(None), c)
        return (LOW, slice(None), 1 - d["x"] if far else d["x"], c)

    def pair(self, high, far):
        d = self.digits
        if high:
            return (HIGH, d["y"], 1 - d["x"] if far else d["x"], d["c"])
        return (LOW, 1 - d["y"] if far else d["y"], d["x"], d["c"])

    def spec(self, slot):
        d = self.digits
        if slot < 4:
            high, near = slot % 2, slot // 2
            source = self.parts.at[self.side(high, not near, 1 - d["c"])]
            return source, self.from_core.at[near, high], self.device(**self.flip("c"))
        if slot < 6:
            high = slot - 4
            return self.parts.at[self.side(high, True)], self.from_first.at[high], self.device(**self.flip("xy"[high]))
        if slot < 8:
            high = slot - 6
            return self.parts.at[self.pair(high, True)], self.from_second.at[high], self.device(**self.flip("yx"[high]))
        z = (d["z"] + slot - 7) % 4
        return self.parts.at[z, d["y"], d["x"], d["c"]], self.from_line.at[slot - 8], self.device(z=z)

    def landing(self, slot):
        if slot < 4:
            return self.from_core.at[slot // 2, slot % 2]
        if slot < 8:
            return (self.from_first, self.from_second)[(slot - 4) // 2].at[slot % 2]
        return self.from_line.at[slot - 8]

    def spend(self, *kinds):
        if self.credits is not None:
            for kind in kinds:
                pl.semaphore_wait(self.credits.at[kind], 1)

    def grant(self):
        d = self.digits
        if self.grants is not None:
            others = [self.device(**self.flip(axis)) for axis in "cxy"]
            others += [self.device(z=(d["z"] + 4 - step) % 4) for step in (1, 2, 3)]
            for kind, other in enumerate(others):
                pl.semaphore_signal(self.grants.at[kind], inc=1, device_id=other, device_id_type=MESH_ID)

    def add(self, index, received):
        self.parts[index] = self.parts[index] + received

    def start(self):
        self.spend(0)
        self.go(0, 1, 2, 3)

    def core(self):
        self.spend(1, 2)
        for high in (0, 1):
            self.arrived(high)
            self.add(self.side(high, True), self.from_core[0, high])
            self.go(4 + high)
        for high in (0, 1):
            self.arrived(2 + high)
            self.add(self.side(high, False), self.from_core[1, high])

    def across(self):
        d = self.digits
        for high, other in ((0, "y"), (1, "x")):
            self.arrived(4 + high)
            self.add(self.pair(high, True), self.from_first[high, :, 1 - d[other]])
            self.go(6 + high)
        for high, other in ((0, "y"), (1, "x")):
            self.add(self.pair(high, False), self.from_first[high, :, d[other]])

    def collect(self):
        for high in (0, 1):
            self.arrived(6 + high)
            self.add(self.pair(high, False), self.from_second[high])
        self.spend(3, 4, 5)

    def along(self):
        self.collect()
        self.go(8, 9, 10)

    def finish(self, store):
        d = self.digits
        total = self.parts[d["z"], d["y"], d["x"], d["c"]].astype(f32)
        for slot in (8, 9, 10):
            self.arrived(slot)
            total = total + self.from_line[slot - 8].astype(f32)
        store(total)
        self.sent(self.SLOTS)
        self.grant()


class PlaneReduce(Reduce):
    def __init__(self, parts, received, plane_in, send_sems, recv_sems, digits, device, credits, grants, plane):
        super().__init__(parts, received, send_sems, recv_sems, digits, device, credits, grants)
        self.plane_in, self.plane = plane_in, plane

    def along(self):
        d = self.digits
        self.collect()
        for step in (1, 2, 3):

            @pl.when(d["z"] == (self.plane + step) % 4)
            def _(step=step):
                self.to_plane(step).start()

    def to_plane(self, step):
        d = self.digits
        return pltpu.make_async_remote_copy(
            src_ref=self.parts.at[:, d["y"], d["x"], d["c"]],
            dst_ref=self.plane_in.at[step - 1],
            send_sem=self.send_sems.at[7 + step],
            recv_sem=self.recv_sems.at[7 + step],
            device_id=self.device(z=self.plane),
            device_id_type=MESH_ID,
        )

    def finish(self, store):
        d = self.digits

        @pl.when(d["z"] == self.plane)
        def _():
            total = self.parts[:, d["y"], d["x"], d["c"]].astype(f32)
            for step in (1, 2, 3):
                self.arrived_at(7 + step, self.plane_in.at[step - 1])
                total = total + self.plane_in[step - 1].astype(f32)
            store(total)

        for step in (1, 2, 3):

            @pl.when(d["z"] == (self.plane + step) % 4)
            def _(step=step):
                self.to_plane(step).wait_send()

        for slot in range(8):
            self.copy(slot).wait_send()
        self.grant()


class SmallSum(Transfers):
    SLOTS = 6

    def __init__(self, total, buffer, send_sems, recv_sems, digits, device):
        super().__init__(send_sems, recv_sems, digits, device)
        self.total, self.buffer = total, buffer

    def spec(self, slot):
        z = self.digits["z"]
        if slot < 3:
            return self.buffer.at[2 * slot], self.buffer.at[2 * slot + 1], self.device(**self.flip("cxy"[slot]))
        mine = self.buffer.at[6 + z]
        return mine, mine, self.device(z=(z + slot - 2) % 4)

    def landing(self, slot):
        if slot < 3:
            return self.buffer.at[2 * slot + 1]
        return self.buffer.at[6 + (self.digits["z"] + 6 - slot) % 4]

    def start(self, slot):
        if slot < 3:
            self.buffer[2 * slot] = self.total[...]
            self.go(slot)
        else:
            self.buffer[6 + self.digits["z"]] = self.total[...]
            self.go(3, 4, 5)

    def finish(self, slot):
        if slot < 3:
            self.arrived(slot)
            self.total[...] = self.total[...] + self.buffer[2 * slot + 1]
        else:
            self.arrived(3, 4, 5)
            self.total[...] = (self.buffer[6] + self.buffer[7]) + (self.buffer[8] + self.buffer[9])
            self.sent(self.SLOTS)


def pack(block):
    rows = block.reshape(-1, 8, 2 * COLS)
    return jnp.concatenate([rows[:, :, :COLS], rows[:, :, COLS:]], axis=1).reshape(-1, COLS)


def unpack(block):
    rows = block.reshape(-1, 2, 8, COLS)
    return jnp.concatenate([rows[:, 0].reshape(-1, COLS), rows[:, 1].reshape(-1, COLS)], axis=1)


def unpack_piece(piece, target):
    def plane(z, carry):
        target[part_of(z, 192), :] = unpack(piece[z].astype(f32).reshape(8 * ROWS, COLS)).astype(bf16)
        return carry

    lax.fori_loop(0, 4, plane, 0)


def pack_piece(piece, z, grad):
    piece[z] = pack(grad).astype(bf16).reshape(2, 2, 2, ROWS, COLS)


def bucket_of(offsets):
    distance = jnp.abs(offsets)
    coarse = jnp.full_like(distance, 8)
    for cutoff in CUTOFFS:
        coarse = coarse + (distance >= cutoff).astype(jnp.int32)
    return jnp.where(distance < 8, distance, coarse) + jnp.where(offsets > 0, 16, 0)


def strip_onehot(shift):
    column = lax.broadcasted_iota(jnp.int32, (128, 512), 1)
    column = jnp.where(column >= shift, column - shift, column - shift + 512)
    offset = jnp.where(column < 384, 128 - column, 640 - column)
    return bucket_of(offset) == lax.broadcasted_iota(jnp.int32, (128, 512), 0)


def make_strips(table_t, strips):
    line = nn(table_t[...], strip_onehot(0).astype(bf16)[:NB])
    for head in range(H):
        rows = jnp.broadcast_to(line[head : head + 1], (128, 512))
        strips[head] = pltpu.roll(rows, 0, 1, stride=1, stride_axis=0)[:, :384].astype(strips.dtype)


def strip_sums(strip):
    wide = jnp.concatenate([strip, jnp.zeros((128, 128), f32)], axis=1)
    total = wide[:8]
    for r in range(1, 16):
        total = total + pltpu.roll(wide[8 * r : 8 * r + 8], 512 - 8 * r, 1)
    return total


def table_sums(sums, far_sums):
    row = lax.broadcasted_iota(jnp.int32, (8 * H, 8 * H), 0)
    column = lax.broadcasted_iota(jnp.int32, (8 * H, 8 * H), 1)
    turned = exact((column == (row // 8) * 8 + 7 - row % 8).astype(f32), sums)
    lines = [
        jnp.sum(pltpu.roll(turned[8 * h : 8 * h + 8], 0, 1, stride=1, stride_axis=0), axis=0, keepdims=True)
        for h in range(H)
    ]
    lines.append(jnp.zeros((16 - H, 512), f32))
    table = exact(jnp.concatenate(lines, axis=0), strip_onehot(7).astype(f32), (((1,), (1,)), ((), ())))
    head = lax.broadcasted_iota(jnp.int32, (16, 128), 0)
    bucket = lax.broadcasted_iota(jnp.int32, (16, 128), 1)
    for side, index in ((0, 15), (1, 31)):
        rows = [jnp.sum(far_sums[h, side], axis=0, keepdims=True) for h in range(H)] + [jnp.zeros((16 - H, 128), f32)]
        total = jnp.sum(jnp.concatenate(rows, axis=0), axis=1, keepdims=True)
        table = table + jnp.where((bucket == index) & (head < H), total, 0.0)
    return table


def make_marks(lengths, key_marks, query_marks):
    position = lax.broadcasted_iota(jnp.int32, (SEQ, 128), 0)
    lane = lax.broadcasted_iota(jnp.int32, (SEQ, 128), 1)
    for row in range(key_marks.shape[0] // SEQ):
        segment = jnp.zeros((SEQ, 128), jnp.int32)
        end = 0
        for k in range(1, 5):
            end = end + lengths[row, k]
            segment = segment + (position >= end).astype(jnp.int32)
        own = segment == lane
        rows = slice(row * SEQ, (row + 1) * SEQ)
        key_marks[rows, :] = jnp.where(own, 1.0, 0.0).astype(bf16)
        query_marks[rows, :] = jnp.where(own | (lane >= 5), 0.0, -1e30).astype(bf16)


def lane_mask(h):
    lane = lax.broadcasted_iota(jnp.int32, (1, 128), 1)
    return lane < 64 if h == 0 else lane >= 64


def biased(raw, strip, half):
    low, high = strip[0:1, 383:384].astype(f32), strip[127:128, 0:1].astype(f32)
    rows = []
    for bj in range(4):
        blocks = []
        for bi in (0, 1):
            d = bj - bi - 2 * half
            block = raw[128 * bj : 128 * (bj + 1), 128 * bi : 128 * (bi + 1)]
            if d <= -2:
                block = block + low
            elif d >= 2:
                block = block + high
            else:
                block = block + strip[:, 128 * (1 - d) : 128 * (2 - d)].astype(f32)
            blocks.append(block)
        rows.append(jnp.concatenate(blocks, axis=1))
    return jnp.concatenate(rows, axis=0)


def heads_of(ref, rows, which, pair):
    return ref[rows, pl.ds(pl.multiple_of(which * 256 + pair * 128, 128), 128)]


def raw_scores(q2, k2, key_marks, query_marks):
    queries = jnp.concatenate([q2, query_marks], axis=1)
    return [nt(jnp.concatenate([jnp.where(lane_mask(h), k2, 0), key_marks], axis=1), queries) for h in range(2)]


def attend(qkv, key_marks, query_marks, strips, mix, lse, group, pair):
    count = mix.shape[0] // SEQ
    raws, values = [], []
    for row in range(count):
        rows = slice(row * SEQ, (row + 1) * SEQ)
        q2, k2, v2 = (heads_of(qkv, rows, which, pair) for which in range(3))
        raws.append(raw_scores(q2, k2, key_marks[rows, :], query_marks[rows, :]))
        values.append(v2.T)
    for row in range(count):
        outs = []
        for h in range(2):
            head = (group * 2 + pair) * 2 + h
            halves = []
            for half in range(2):
                span = slice(256 * half, 256 * half + 256)
                scores = biased(raws[row][h][:, span], strips[head], half)
                peak = jnp.max(scores, axis=0, keepdims=True)
                expo = jnp.exp(scores - peak)
                total = jnp.sum(expo, axis=0, keepdims=True)
                lse[row, pl.ds(head, 1), span] = peak + jnp.log(total)
                halves.append(nn(values[row][64 * h : 64 * h + 64], expo.astype(bf16)) * (1.0 / total))
            outs.append(jnp.concatenate(halves, axis=1))
        mix[row * SEQ : (row + 1) * SEQ, part_of(group * 2 + pair, 128)] = jnp.concatenate(outs, axis=0).T.astype(bf16)


def attend_back(qkv, gmix, key_marks, query_marks, strips, lse, inner, strip_grads, far_sums, group, pair):
    count = gmix.shape[0] // SEQ
    lanes = part_of(group * 2 + pair, 128)
    held = []
    for row in range(count):
        rows = slice(row * SEQ, (row + 1) * SEQ)
        q2, k2, v2 = (heads_of(qkv, rows, which, pair) for which in range(3))
        g2 = gmix[rows, lanes]
        raws = raw_scores(q2, k2, key_marks[rows, :], query_marks[rows, :])
        held.append((q2, k2.T, v2, g2, raws))
    for row in range(count):
        rows = slice(row * SEQ, (row + 1) * SEQ)
        q2, k2t, v2, g2, raws = held[row]
        grads = [nt(jnp.where(lane_mask(h), v2, 0), g2) for h in range(2)]
        grad_v, grad_k, grad_q = 0.0, 0.0, []
        for h in range(2):
            head = (group * 2 + pair) * 2 + h
            mask = lane_mask(h)
            near, far = {}, ([], [])
            probs_low, scores_low = [], []
            for half in range(2):
                span = slice(256 * half, 256 * half + 256)
                probs = jnp.exp(biased(raws[h][:, span], strips[head], half) - lse[row, pl.ds(head, 1), span])
                grad = probs * (grads[h][:, span] - inner[row, pl.ds(head, 1), span])
                probs_low.append(probs.astype(bf16))
                scores_low.append(grad.astype(bf16))
                for bi in (0, 1):
                    for bj in range(4):
                        d = bj - bi - 2 * half
                        block = grad[128 * bj : 128 * (bj + 1), 128 * bi : 128 * (bi + 1)]
                        if abs(d) <= 1:
                            near[d] = near[d] + block if d in near else block
                        else:
                            far[d > 0].append(jnp.sum(block.reshape(16, 8, 128), axis=0))
            strip_rows = part_of(group * 2 + pair, 128)
            for d, block in near.items():
                strip_grads[strip_rows, 384 * h + 128 * (1 - d) : 384 * h + 128 * (2 - d)] += block
            for side in (0, 1):
                far_sums[head, side] += sum(far[side][1:], far[side][0])
            grad_v = grad_v + nn(jnp.concatenate(probs_low, axis=1), jnp.where(mask, g2, 0))
            low = jnp.concatenate(scores_low, axis=1)
            grad_k = grad_k + nn(low, jnp.where(mask, q2, 0))
            grad_q.append(nn(k2t[64 * h : 64 * h + 64], low))
        for which, value in enumerate((jnp.concatenate(grad_q, axis=0).T, grad_k, grad_v)):
            qkv[rows, pl.ds(pl.multiple_of(which * 256 + pair * 128, 128), 128)] = value.astype(bf16)


def inner_sums(gmix, mix):
    product = gmix.astype(f32) * mix.astype(f32)
    high = product.astype(bf16)
    low = (product - high.astype(f32)).astype(bf16)
    feature = lax.broadcasted_iota(jnp.int32, (16, D), 1)
    first = lax.broadcasted_iota(jnp.int32, (16, D), 0) * 64
    own = jnp.where((feature >= first) & (feature < first + 64), 1.0, 0.0).astype(bf16)
    return nt(own, high) + nt(own, low)


def inv_rms(x):
    return lax.rsqrt(jnp.mean(x * x, axis=-1, keepdims=True) + EPSILON)


def norm_back(grad, x, gain):
    s = inv_rms(x)
    gg = grad * gain
    return s * gg - x * (s * s * s * jnp.mean(gg * x, axis=-1, keepdims=True)), jnp.sum(grad * x * s, axis=0, keepdims=True)


def gelu_both(x):
    cdf = 0.5 + 0.5 * lax.erf(x * 0.7071067811865476)
    return x * cdf, cdf + x * (jnp.exp(x * x * -0.5) * 0.3989422804014327)


def gain_line(gains, which):
    blocks = gains[...].reshape(8 * RANKS, 128).astype(bf16)
    lane = lax.broadcasted_iota(jnp.int32, (128, D), 1)
    spread = nn(blocks, (lane % 24 == lax.broadcasted_iota(jnp.int32, (128, D), 0)).astype(bf16))
    row = lax.broadcasted_iota(jnp.int32, (8 * RANKS, D), 0)
    column = lax.broadcasted_iota(jnp.int32, (8 * RANKS, D), 1)
    return jnp.sum(jnp.where(row == (column // 24) * 8 + which, spread, 0.0), axis=0, keepdims=True)


def run_at(step, plan):
    for when, stages in plan.items():

        @pl.when(step == when)
        def _(stages=stages):
            for stage in stages:
                stage()


def layer_kernel(
    tokens_hbm, cot_hbm, lengths, norm_gain, ffn_gain, w_query, w_key, w_value, w_out, w_in, w_ffn, table_t,
    out_hbm, gtok_hbm, grad_one, grad_two, grad_table, grad_q, grad_k, grad_v, grad_o, grad_in, grad_ffn,
    pieces, gains, weights, win, wff, qkv, mix, normed, tokens, cot, resid, out_sum, grad_sum, act, grad_inner,
    strips, key_marks, query_marks, lse, inner, far_sums, small, from_core, from_first, from_second, from_line,
    plane_in, small_buffer,
    gather_send, gather_recv, gain_send, gain_recv, reduce_send, reduce_recv, small_send, small_recv, credits, local_sems,
):
    count = tokens.shape[0]
    digits, device = place()
    me = (digits["z"], digits["y"], digits["x"], digits["c"])
    all_here = greet(digits, device)

    load_tokens = pltpu.make_async_copy(tokens_hbm, tokens, local_sems.at[0])
    load_tokens.start()
    load_cot = pltpu.make_async_copy(cot_hbm, cot, local_sems.at[1])
    load_cot.start()

    gain_gather = Gather(gains, gain_send, gain_recv, digits, device)
    gathers = []
    for i in range(PIECES):
        common = (pieces.at[i], gather_send.at[i], gather_recv.at[i], digits, device)
        gathers.append(PlaneGather(*common, FFN_PIECES.index(i)) if i in FFN_PIECES else Gather(*common))
    order = [i for t in range(TILES) for i in (IN_PIECES[t], FFN_PIECES[t])] + [OUT_PIECE, 0, 1, 2]
    reduces = []
    for n, i in enumerate(order):
        slot = n % LANDINGS
        received = (from_core.at[slot], from_first.at[slot], from_second.at[slot], from_line.at[slot])
        sems = (reduce_send.at[n], reduce_recv.at[n], digits, device)
        limits = (credits.at[slot] if n >= LANDINGS else None, credits.at[slot] if n + LANDINGS < PIECES else None)
        if i in FFN_PIECES:
            reduces.append(PlaneReduce(pieces.at[i], received, plane_in, *sems, *limits, FFN_PIECES.index(i)))
        else:
            reduces.append(Reduce(pieces.at[i], received, *sems, *limits))

    def store_in(t):
        def store(total):
            grad_in[:, TILE * t : TILE * (t + 1)] = unpack(total)

        return store

    def store_ffn(total):
        for i in range(4):
            grad_ffn[ROWS * (i // 2) : ROWS * (i // 2 + 1), COLS * (i % 2) : COLS * (i % 2 + 1)] = total[i]

    def store_out(total):
        grad_o[...] = unpack(total)

    def store_group(g):
        def store(total):
            block = unpack(total)
            for which, target in enumerate((grad_q, grad_k, grad_v)):
                target[:, 256 * g : 256 * (g + 1)] = block[:, 256 * which : 256 * (which + 1)]

        return store

    stores = [store for t in range(TILES) for store in (store_in(t), store_ffn)] + [store_out]
    stores += [store_group(g) for g in range(GROUPS)]

    def stage(kind, n, name):
        if kind == "r":
            return partial(reduces[n].finish, stores[n]) if name == "finish" else getattr(reduces[n], name)
        if name == "finish" and n <= OUT_PIECE:
            return partial(arrive, n)
        return getattr(gathers[n], name)

    def arrive(n):
        gathers[n].finish()
        unpack_piece(pieces.at[n], weights.at[n])

    def plan(letter):
        return {int(key[1:]): [stage(*entry) for entry in PLAN[key]] for key in PLAN if key[0] == letter}

    def run(stages):
        for each in stages:
            each()

    for g in range(GROUPS):
        span = slice(256 * g, 256 * g + 256)
        block = jnp.concatenate([w[:, span] for w in (w_query, w_key, w_value)], axis=1)
        pieces[(GROUP_PIECE + g, *me)] = pack(block.astype(f32)).astype(bf16)
    gains[me] = jnp.zeros((8, 128), f32)
    gains[(*me, slice(0, 1), slice(0, 24))] = norm_gain[...].astype(f32)
    gains[(*me, slice(1, 2), slice(0, 24))] = ffn_gain[...].astype(f32)
    all_here()
    gathers[0].start()
    gain_gather.start()
    gathers[1].start()
    gathers[2].start()
    pieces[(OUT_PIECE, *me)] = pack(w_out[...].astype(f32)).astype(bf16)
    gathers[3].start()
    for t in range(TILES):

        @pl.when(digits["z"] == t)
        def _(t=t):
            for i in range(4):
                block = w_ffn[ROWS * (i // 2) : ROWS * (i // 2 + 1), COLS * (i % 2) : COLS * (i % 2 + 1)]
                pieces[FFN_PIECES[t], i, digits["y"], digits["x"], digits["c"]] = block

        gathers[FFN_PIECES[t]].start()
        pieces[(IN_PIECES[t], *me)] = pack(w_in[:, TILE * t : TILE * (t + 1)].astype(f32)).astype(bf16)
        gathers[IN_PIECES[t]].start()

    make_marks(lengths, key_marks, query_marks)
    make_strips(table_t, strips)
    for i, gain_stage in enumerate((gain_gather.line, gain_gather.across, gain_gather.along, gain_gather.finish)):
        run([stage(*entry) for entry in PLAN[f"S{i}"]])
        gain_stage()
    gain_one, gain_two = gain_line(gains, 0), gain_line(gains, 1)
    load_tokens.wait()

    def norm_one(i, carry):
        rows = part_of(i, 256)
        x = tokens[rows, :].astype(f32)
        normed[rows, :] = (x * inv_rms(x) * gain_one).astype(bf16)
        return carry

    lax.fori_loop(0, count // 256, norm_one, 0)
    run([stage(*entry) for entry in PLAN["S"]])

    forward_plan, project_plan = plan("F"), plan("P")

    def forward_group(g, carry):
        qkv[g] = nn(normed[...], weights[GROUP_PIECE + g]).astype(bf16)
        run_at(g, project_plan)

        def forward(pair, carry):
            attend(qkv.at[g], key_marks, query_marks, strips, mix, lse, g, pair)
            run_at(2 * g + pair, forward_plan)
            return carry

        lax.fori_loop(0, 2, forward, 0)
        return carry

    lax.fori_loop(0, GROUPS, forward_group, 0)

    def after_attention(i, carry):
        rows = part_of(i, 512)
        r = tokens[rows, :].astype(f32) + nn(mix[rows, :], weights[OUT_PIECE])
        resid[rows, :] = r
        normed[rows, :] = (r * inv_rms(r) * gain_two).astype(bf16)
        return carry

    lax.fori_loop(0, count // 512, after_attention, 0)
    load_cot.wait()
    run([stage(*entry) for entry in PLAN["A"]])

    ffn_plan = plan("T")
    width = 256

    def tile_piece(t, which):
        return pieces.at[4 + 2 * t + which]

    def ffn_tile(t, carry):
        unpack_piece(tile_piece(t, 1), win)
        for b in range(8):
            for i in range(4):
                rows = slice(96 * b + ROWS * (i // 2), 96 * b + ROWS * (i // 2 + 1))
                block = pieces[4 + 2 * t, i, b // 4, (b // 2) % 2, b % 2]
                wff[rows, COLS * (i % 2) : COLS * (i % 2 + 1)] = block

        def columns(w, carry):
            span = part_of(w, width)
            ffn_in = nn(normed[...], win[:, span])
            grad_act = nt(cot[...], wff[span, :])
            value, slope = gelu_both(ffn_in)
            act[:, span] = value.astype(bf16)
            grad_inner[:, span] = (slope * grad_act).astype(bf16)
            run_at(7 * t + w, ffn_plan)
            return carry

        lax.fori_loop(0, TILE // width, columns, 0)

        for i in range(2):
            rows = slice(i * count // 2, (i + 1) * count // 2)
            value = nn(act[rows, :], wff[...])
            out_sum[rows, :] = jnp.where(t == 0, resid[rows, :], out_sum[rows, :]) + value

        run_at(7 * t + 3, ffn_plan)

        for i in range(2):
            rows = slice(i * count // 2, (i + 1) * count // 2)
            value = nt(grad_inner[rows, :], win[...])
            grad_sum[rows, :] = jnp.where(t == 0, 0.0, grad_sum[rows, :]) + value

        run_at(7 * t + 4, ffn_plan)
        grad = tn(normed[...], grad_inner[...])
        for z in range(4):
            pack_piece(tile_piece(t, 1), z, grad[192 * z : 192 * (z + 1)])
        run_at(t, {k: [reduces[2 * k].start] for k in range(TILES)})
        run_at(7 * t + 5, ffn_plan)
        grad = tn(act[...], cot[...]).astype(bf16)
        for b in range(8):
            for i in range(4):
                block = grad[96 * b + ROWS * (i // 2) : 96 * b + ROWS * (i // 2 + 1), COLS * (i % 2) : COLS * (i % 2 + 1)]
                pieces[4 + 2 * t, i, b // 4, (b // 2) % 2, b % 2] = block
        run_at(t, {k: [reduces[2 * k + 1].start] for k in range(TILES)})
        run_at(7 * t + 6, ffn_plan)
        return carry

    lax.fori_loop(0, TILES, ffn_tile, 0)

    before_plan = plan("B")
    small[...] = jnp.zeros(small.shape, f32)

    def spread_line(row, line):
        for j in range(D // 128):
            small[row + j : row + j + 1, :] += line[:, 128 * j : 128 * (j + 1)]

    def before_back(i, carry):
        rows = part_of(i, 256)
        act[rows, :] = out_sum[rows, :].astype(bf16)
        into, gain_sum = norm_back(grad_sum[rows, :], resid[rows, :], gain_two)
        spread_line(6, gain_sum)
        grad = cot[rows, :].astype(f32) + into
        grad_sum[rows, :] = grad
        low = grad.astype(bf16)
        cot[rows, :] = low
        gmix = nt(low, weights[OUT_PIECE]).astype(bf16)
        inner[i // 2, :, part_of(i % 2, 256)] = inner_sums(gmix, mix[rows, :])
        x = tokens[rows, :].astype(f32)
        grad_inner[rows, :] = (x * inv_rms(x) * gain_one).astype(bf16)
        normed[rows, :] = gmix
        run_at(i, before_plan)
        return carry

    lax.fori_loop(0, count // 256, before_back, 0)
    store_output = pltpu.make_async_copy(act, out_hbm, local_sems.at[2])
    store_output.start()
    out_sum[...] = jnp.zeros(out_sum.shape, f32)
    far_sums[...] = jnp.zeros(far_sums.shape, f32)
    grad = tn(mix[...], cot[...])
    for z in range(4):
        pack_piece(pieces.at[OUT_PIECE], z, grad[192 * z : 192 * (z + 1)])
    run(before_plan.get(4, []))
    back_plan, group_plan = plan("K"), plan("G")

    def back_group(g, carry):
        def back(pair, carry):
            attend_back(qkv.at[g], normed, key_marks, query_marks, strips, lse, inner, out_sum, far_sums, g, pair)
            run_at(2 * g + pair, back_plan)
            return carry

        lax.fori_loop(0, 2, back, 0)
        grad = tn(grad_inner[...], qkv[g])
        for z in range(4):
            pack_piece(pieces.at[GROUP_PIECE + g], z, grad[192 * z : 192 * (z + 1)])
        run_at(g, {k: [reduces[9 + k].start] for k in range(GROUPS)})
        run_at(g, group_plan)
        return carry

    lax.fori_loop(0, GROUPS, back_group, 0)
    last_plan = plan("L")

    def last(i, carry):
        rows = part_of(i, 512)
        grad = nt(qkv[0, rows, :], weights[0]) + nt(qkv[1, rows, :], weights[1]) + nt(qkv[2, rows, :], weights[2])
        into, gain_sum = norm_back(grad, tokens[rows, :].astype(f32), gain_one)
        spread_line(0, gain_sum)
        grad_sum[rows, :] = grad_sum[rows, :] + into
        run_at(i, last_plan)
        return carry

    lax.fori_loop(0, count // 512, last, 0)
    store_gtok = pltpu.make_async_copy(grad_sum, gtok_hbm, local_sems.at[3])
    store_gtok.start()
    for pair in range(H // 2):
        for h in range(2):
            head = 2 * pair + h
            strip = out_sum[128 * pair : 128 * pair + 128, 384 * h : 384 * h + 384]
            resid[8 * head : 8 * head + 8, :512] = strip_sums(strip)
    small[16:32, :] = table_sums(resid[: 8 * H, :512], far_sums)
    sums = SmallSum(small, small_buffer, small_send, small_recv, digits, device)
    tail = [stage(*entry) for entry in PLAN["E"]]
    for slot in range(4):
        sums.start(slot)
        share = -(-len(tail) // (4 - slot))
        run(tail[:share])
        tail = tail[share:]
        sums.finish(slot)
    for target, row in ((grad_one, 0), (grad_two, 6)):
        line = jnp.concatenate([small[row + j : row + j + 1, :] for j in range(D // 128)], axis=1)
        rank = (lax.axis_index("dp") // (lax.axis_size("dp") // RANKS)).astype(jnp.int32)
        own = pltpu.roll(jnp.broadcast_to(line, (8, D)), (D - 24 * rank) % D, 1)
        target[...] = own[0:1, :24]
    grad_table[...] = small[16 : 16 + H, :NB]
    run(tail)
    store_output.wait()
    store_gtok.wait()


def deliver_kernel(*refs):
    count = (len(refs) - 1) // 3
    sources, targets, held, sems = refs[:count], refs[count : 2 * count], refs[2 * count : 3 * count], refs[-1]
    loads = [pltpu.make_async_copy(sources[i], held[i], sems.at[0, i]) for i in range(count)]
    stores = [pltpu.make_async_copy(held[i], targets[i], sems.at[1, i]) for i in range(count)]
    for load in loads:
        load.start()
    for load, store in zip(loads, stores):
        load.wait()
        store.start()
    for store in stores:
        store.wait()


def inner_groups():
    total = lax.axis_size("dp")
    group = total // RANKS
    return group, [list(range(i * group, (i + 1) * group)) for i in range(RANKS)]


def widen(block):
    group, groups = inner_groups()
    if group == 1:
        return block
    return lax.all_gather(block, "dp", axis=0, tiled=True, axis_index_groups=groups)


def narrow(block):
    group, groups = inner_groups()
    if group == 1:
        return block
    return lax.psum_scatter(block, "dp", scatter_dimension=0, tiled=True, axis_index_groups=groups)


def per_device(
    tokens, lengths, norm_gain, w_query, w_key, w_value, w_out, bias_table, ffn_gain, w_in, w_ffn_out, cotangent
):
    count = tokens.shape[0]
    norm_gain, ffn_gain, w_query, w_key, w_value, w_out, w_in, w_ffn_out = (
        widen(w) for w in (norm_gain, ffn_gain, w_query, w_key, w_value, w_out, w_in, w_ffn_out)
    )
    any_space = pl.BlockSpec(memory_space=pl.ANY)
    vmem = pl.BlockSpec(memory_space=pltpu.VMEM)
    smem = pl.BlockSpec(memory_space=pltpu.SMEM)
    full = (4, 2, 2, 2)
    out = jax.ShapeDtypeStruct
    shapes = [out((count, D), bf16), out((count, D), f32), out((1, 24), f32), out((1, 24), f32), out((H, NB), f32)]
    shapes += [out((24, D), f32)] * 4 + [out((24, FF), f32), out((96, D), f32)]
    results = pl.pallas_call(
        layer_kernel,
        out_shape=shapes,
        in_specs=[any_space] * 2 + [smem] + [vmem] * 9,
        out_specs=[any_space] * 2 + [vmem] * 9,
        scratch_shapes=[
            pltpu.VMEM((PIECES,) + full + (ROWS, COLS), bf16),
            pltpu.VMEM(full + (8, 128), f32),
            pltpu.VMEM((4, D, D), bf16),
            pltpu.VMEM((D, TILE), bf16),
            pltpu.VMEM((TILE, D), bf16),
            pltpu.VMEM((GROUPS, count, D), bf16),
            pltpu.VMEM((count, D), bf16),
            pltpu.VMEM((count, D), bf16),
            pltpu.VMEM((count, D), bf16),
            pltpu.VMEM((count, D), bf16),
            pltpu.VMEM((count, D), f32),
            pltpu.VMEM((count, D), f32),
            pltpu.VMEM((count, D), f32),
            pltpu.VMEM((count, TILE), bf16),
            pltpu.VMEM((count, TILE), bf16),
            pltpu.VMEM((H, 128, 384), bf16),
            pltpu.VMEM((count, 128), bf16),
            pltpu.VMEM((count, 128), bf16),
            pltpu.VMEM((count // SEQ, H, SEQ), f32),
            pltpu.VMEM((count // SEQ, 16, SEQ), f32),
            pltpu.VMEM((H, 2, 8, 128), f32),
            pltpu.VMEM((32, 128), f32),
            pltpu.VMEM((LANDINGS, 2, 2, 2, 2, ROWS, COLS), bf16),
            pltpu.VMEM((LANDINGS, 2, 2, 2, ROWS, COLS), bf16),
            pltpu.VMEM((LANDINGS, 2, 2, ROWS, COLS), bf16),
            pltpu.VMEM((LANDINGS, 3, ROWS, COLS), bf16),
            pltpu.VMEM((3, 4, ROWS, COLS), bf16),
            pltpu.VMEM((10, 32, 128), f32),
            pltpu.SemaphoreType.DMA((PIECES, Gather.SLOTS)),
            pltpu.SemaphoreType.DMA((PIECES, Gather.SLOTS)),
            pltpu.SemaphoreType.DMA((Gather.SLOTS,)),
            pltpu.SemaphoreType.DMA((Gather.SLOTS,)),
            pltpu.SemaphoreType.DMA((PIECES, Reduce.SLOTS)),
            pltpu.SemaphoreType.DMA((PIECES, Reduce.SLOTS)),
            pltpu.SemaphoreType.DMA((SmallSum.SLOTS,)),
            pltpu.SemaphoreType.DMA((SmallSum.SLOTS,)),
            pltpu.SemaphoreType.REGULAR((LANDINGS, 6)),
            pltpu.SemaphoreType.DMA((4,)),
        ],
        compiler_params=pltpu.CompilerParams(collective_id=1, has_side_effects=True, vmem_limit_bytes=63 << 20),
    )(
        tokens,
        cotangent,
        lengths,
        norm_gain.reshape(1, -1),
        ffn_gain.reshape(1, -1),
        w_query,
        w_key,
        w_value,
        w_out,
        w_in,
        w_ffn_out,
        bias_table.T,
    )
    results = pl.pallas_call(
        deliver_kernel,
        out_shape=shapes,
        in_specs=[any_space] * len(shapes),
        out_specs=[any_space] * len(shapes),
        scratch_shapes=[pltpu.VMEM(shape.shape, shape.dtype) for shape in shapes]
        + [pltpu.SemaphoreType.DMA((2, len(shapes)))],
        compiler_params=pltpu.CompilerParams(vmem_limit_bytes=63 << 20),
    )(*results)
    output, grad_tokens, grad_one, grad_two, grad_table, *weight_grads = results
    group, groups = inner_groups()
    if group > 1:
        grad_table = lax.psum(grad_table, "dp", axis_index_groups=groups)
    grad_q, grad_k, grad_v, grad_o, grad_in, grad_ffn = (narrow(grad) for grad in weight_grads)
    return (
        output,
        grad_tokens,
        narrow(grad_one[0]),
        grad_q,
        grad_k,
        grad_v,
        grad_o,
        grad_table.T,
        narrow(grad_two[0]),
        grad_in,
        grad_ffn,
    )


def solution(mesh):
    rows, whole = P("dp", None), P("dp")
    return jax.shard_map(
        per_device,
        mesh=mesh,
        in_specs=(rows, rows, whole, rows, rows, rows, rows, P(), whole, rows, rows, rows),
        out_specs=(rows, rows, whole, rows, rows, rows, rows, P(), whole, rows, rows),
        check_vma=False,
    )
```
